256 devices in a mesh: grp: 2 (over x_lo), lat: 16 (over z, x_hi), lon: 8 (over y, core).
Axes of the slice: x: 4 (x_hi: 2, x_lo: 2; x = x_hi * 2 + x_lo), y: 4, z: 8, core: 2. Of those that a mesh axis runs over, the one named last changes fastest.
Arguments:
- coupled_state: bfloat16 [2, 80, 256, 1024], P('grp', None, 'lat', 'lon'), may hold values from -6 to 6
- land_mask: int32 [256, 1024], P('lat', 'lon'), may hold values 0 or 1
- regrid_offsets: int32 [2, 2, 4, 256, 1024], P('grp', None, None, 'lat', 'lon'), may hold values from -8 to 8
- regrid_weights: float32 [2, 4, 256, 1024], P('grp', None, 'lat', 'lon'), may hold values from 0.1 to 0.4
- surface_proj: float32 [2, 4, 80], replicated, may hold values from -0.625 to 0.625
- atm_in: bfloat16 [384, 84], replicated, may hold values from -0.625 to 0.625
- atm_bias: float32 [384], replicated, may hold values from -3 to 3
- atm_out: bfloat16 [80, 384], replicated, may hold values from -0.3125 to 0.3125
- ocn_in: bfloat16 [200, 9, 84], replicated, may hold values from -0.21875 to 0.21875
- ocn_bias: float32 [200], replicated, may hold values from -3 to 3
- ocn_out: bfloat16 [80, 9, 200], replicated, may hold values from -0.125 to 0.125
Outputs:
- next_state: bfloat16 [2, 80, 256, 1024], P('grp', None, 'lat', 'lon')
The draws below stay inside these ranges and needn't reach their ends.
All inputs are finite; a program needn't handle non-finite values. No bound on the sum of `land_mask` on one device may be relied on, other than what follows from the above.
Results may differ from the reference program's by a relative error of at most 0.008.
Values may be sent and summed in bfloat16 or wider, within the bound.
A program may use at most 64 MiB of HBM per device.

```python
import jax
import jax.numpy as jnp
from jax import lax

CH = 80
NS = 4
HA = 384
HO = 200
NK = 4
HW = 8
STEPS = 2
NR = 256
NQ = 1024


def touch_ends(drawn, key, smallest, largest):
    index_at = [jax.random.randint(jax.random.fold_in(key, axis), (), 0, length) for axis, length in enumerate(drawn.shape)]
    widest = drawn.shape.index(max(drawn.shape))
    next_to = index_at[:widest] + [(index_at[widest] + 1) % drawn.shape[widest]] + index_at[widest + 1:]
    return drawn.at[tuple(index_at)].set(smallest).at[tuple(next_to)].set(largest)


def steps_of(key, dims, shards, low, high):
    def one(position, parts):
        draws = jax.random.uniform(jax.random.fold_in(jax.random.fold_in(key, 6), position), (parts,), jnp.float32, low / len(shards), high / len(shards))
        return jnp.repeat(jnp.exp(draws), dims[position] // parts).reshape((-1,) + (1,) * (len(dims) - position - 1))

    factor_of = one(*shards[0])
    for cut in shards[1:]:
        factor_of = factor_of * one(*cut)
    return factor_of


def scatter_about(key, extent, spread, most, cuts=(), kind=jnp.bfloat16):
    entries = jax.random.normal(key, extent, jnp.float32) * spread
    if len(cuts) > 0:
        entries = steps_of(key, extent, cuts, -0.22, 0.18) * entries
    return jnp.clip(entries, min=-most, max=most).astype(kind)


def setup_inputs(seed: int = 0) -> dict:
    seeds = jax.random.split(jax.random.key(seed), 12)
    coupled_state = scatter_about(seeds[0], (2, CH, NR, NQ), 1.0, 6.0, ((0, 2), (2, 16), (3, 8)))
    land_mask = touch_ends((jax.random.randint(seeds[1], (NR, NQ), 0, 10) < 7).astype(jnp.int32), jax.random.fold_in(seeds[1], 1), 0, 1)
    regrid_offsets = touch_ends(jax.random.randint(seeds[2], (2, 2, NK, NR, NQ), -HW, HW + 1), jax.random.fold_in(seeds[2], 1), -HW, HW).astype(jnp.int32)
    regrid_weights = jnp.clip(0.1 + 0.3 * jax.random.uniform(seeds[3], (2, NK, NR, NQ), jnp.float32) ** steps_of(seeds[3], (2, NK, NR, NQ), ((0, 2), (2, 16), (3, 8)), -0.2, 0.2), 0.1, 0.4)
    surface_proj = scatter_about(seeds[4], (2, NS, CH), CH ** -0.5, 0.625, (), jnp.float32)
    atm_in = scatter_about(seeds[5], (HA, CH + NS), (CH + NS) ** -0.5, 0.625)
    atm_bias = scatter_about(seeds[6], (HA,), 0.5, 3.0, (), jnp.float32)
    atm_out = scatter_about(seeds[7], (CH, HA), HA ** -0.5, 0.3125)
    ocn_in = scatter_about(seeds[8], (HO, 9, CH + NS), (9 * (CH + NS)) ** -0.5, 0.21875)
    ocn_bias = scatter_about(seeds[9], (HO,), 0.5, 3.0, (), jnp.float32)
    ocn_out = scatter_about(seeds[10], (CH, 9, HO), (9 * HO) ** -0.5, 0.125)
    return {"coupled_state": coupled_state, "land_mask": land_mask, "regrid_offsets": regrid_offsets, "regrid_weights": regrid_weights, "surface_proj": surface_proj, "atm_in": atm_in, "atm_bias": atm_bias, "atm_out": atm_out, "ocn_in": ocn_in, "ocn_bias": ocn_bias, "ocn_out": ocn_out}


def surface_fields(values, projector, keeping):
    flattened = jnp.dot(projector, values.reshape(values.shape[0], -1).astype(jnp.float32), precision=lax.Precision.HIGHEST)
    return flattened.reshape(-1, values.shape[1], values.shape[2]) * keeping


def regrid(fields, offsets, weights):
    row_total = fields.shape[1]
    col_total = fields.shape[2]
    padded = jnp.pad(fields, ((0, 0), (HW, HW), (0, 0)))
    row_ids = jnp.arange(row_total, dtype=jnp.int32)[None, :, None]
    col_ids = jnp.arange(col_total, dtype=jnp.int32)[None, None, :]
    source_rows = row_ids + HW + offsets[0]
    source_cols = (col_ids + offsets[1]) % col_total
    sources = (source_rows * col_total + source_cols).astype(jnp.int32).reshape(-1)
    picked = jnp.take(padded.reshape(fields.shape[0], -1), sources, axis=1)
    picked = picked.reshape(fields.shape[0], offsets.shape[1], row_total, col_total)
    return jnp.sum(picked * weights[None], axis=1).astype(jnp.bfloat16)


def stencil_global(values, kernel):
    channels, row_total, col_total = values.shape
    padded = jnp.pad(values, ((0, 0), (1, 1), (0, 0)))
    padded = jnp.concatenate([padded[:, :, -1:], padded, padded[:, :, :1]], axis=2)
    total = jnp.zeros((kernel.shape[0], row_total * col_total), jnp.float32)
    for shift_row in range(3):
        for shift_col in range(3):
            window = padded[:, shift_row:shift_row + row_total, shift_col:shift_col + col_total].reshape(channels, -1)
            total = total + jnp.dot(kernel[:, 3 * shift_row + shift_col, :], window, preferred_element_type=jnp.float32)
    return total.reshape(kernel.shape[0], row_total, col_total)


def air_step(previous, forcing, atm_in, atm_bias, atm_out):
    inputs = jnp.concatenate([previous, forcing], 0)
    flattened = inputs.reshape(inputs.shape[0], -1)
    hidden = jax.nn.gelu(jnp.dot(atm_in, flattened, preferred_element_type=jnp.float32) + atm_bias[:, None]).astype(jnp.bfloat16)
    update = jnp.dot(atm_out, hidden, preferred_element_type=jnp.float32)
    result = previous.reshape(previous.shape[0], -1).astype(jnp.float32) + update
    return result.astype(jnp.bfloat16).reshape(previous.shape)


def sea_step(previous, forcing, wet_cells, ocn_in, ocn_bias, ocn_out):
    inputs = jnp.concatenate([previous, forcing], 0)
    hidden = jax.nn.gelu(stencil_global(inputs, ocn_in) + ocn_bias[:, None, None]).astype(jnp.bfloat16)
    update = stencil_global(hidden, ocn_out)
    return (previous.astype(jnp.float32) + wet_cells * update).astype(jnp.bfloat16)


def reference(coupled_state, land_mask, regrid_offsets, regrid_weights, surface_proj, atm_in, atm_bias, atm_out, ocn_in, ocn_bias, ocn_out):
    wet_cells = land_mask.astype(jnp.float32)
    unmasked = jnp.ones_like(wet_cells)
    air_state = coupled_state[0]
    sea_state = coupled_state[1]
    for repeat in range(STEPS):
        air_fields = surface_fields(air_state, surface_proj[0], unmasked)
        sea_fields = surface_fields(sea_state, surface_proj[1], wet_cells)
        air_forcing = regrid(sea_fields, regrid_offsets[0], regrid_weights[0])
        sea_forcing = regrid(air_fields, regrid_offsets[1], regrid_weights[1])
        air_state = air_step(air_state, air_forcing, atm_in, atm_bias, atm_out)
        sea_state = sea_step(sea_state, sea_forcing, wet_cells, ocn_in, ocn_bias, ocn_out)
    return jnp.stack([air_state, sea_state], 0)
```

```python
import functools

import jax
import jax.numpy as jnp
from jax import lax
from jax.experimental import pallas as pl
from jax.experimental.pallas import tpu as pltpu
from jax.sharding import PartitionSpec as P

BF = jnp.bfloat16
F32 = jnp.float32
I32 = jnp.int32
MESH = pl.DeviceIdType.MESH

STEPS = 2
HW = 8
CH = 80
HO = 200
HOP = 208
ROWS = 16
LANES = 128
TALL = ROWS + 4


def iota(shape, axis):
    return lax.broadcasted_iota(I32, shape, axis)


def one_hot(shape, test):
    return jnp.where(test, 1.0, 0.0).astype(F32).astype(BF)


def gelu(x):
    inner = x * (0.7978845608028654 + 0.035677408136300125 * (x * x))
    half = 0.5 * x
    return half + half * jnp.tanh(inner)


def thirds(x):
    high = x.astype(BF).astype(F32)
    middle = (x - high).astype(BF).astype(F32)
    return high, middle, x - high - middle


def bias_columns(bias, rows):
    count = bias.shape[0]
    spread = jnp.broadcast_to(bias.reshape(1, count), (rows, count))
    same = iota((rows, count), 0) == iota((rows, count), 1)
    return thirds(jnp.sum(jnp.where(same, spread, 0.0), axis=1, keepdims=True))


def kernel(
    lats,
    lons,
    state_ref,
    mask_ref,
    offsets_ref,
    weights_ref,
    proj_ref,
    atm_in_ref,
    atm_bias_ref,
    atm_out_ref,
    ocn_in_hbm,
    ocn_bias_ref,
    ocn_out_hbm,
    out_ref,
    flip,
    xr,
    eg,
    eg_recv,
    cp,
    cp_recv,
    sm,
    sb,
    sp,
    sp_recv,
    q,
    qe,
    qe_recv,
    gi,
    gd,
    gw,
    sd,
    fr,
    x3,
    x3e,
    w1,
    w2,
    wa,
    hid,
    he,
    hh,
    ze,
    keep,
    wet,
    pp,
    ocn_in_v,
    ocn_out_v,
    wt1,
    wt2,
    load_sem,
    s_send,
    s_recv,
    x_send,
    x_recv,
    q_send,
    q_recv,
):
    g = lax.axis_index("grp")
    i = lax.axis_index("lat")
    j = lax.axis_index("lon")
    ocean = g == 1
    air = g == 0
    has = {-1: i > 0, 0: None, 1: i < lats - 1}

    def place(group, di, dj):
        return (group, i + di, lax.rem(j + dj + lons, lons))

    def when(condition, action):
        if condition is None:
            action()
        else:
            pl.when(condition)(action)

    lane8 = iota((8, LANES), 1)
    sub8 = iota((8, LANES), 0)
    low = sub8 < 4
    lane80 = iota((CH, LANES), 1)
    lane16 = iota((16, LANES), 1)

    loads = [
        pltpu.make_async_copy(ocn_in_hbm, ocn_in_v, load_sem.at[0]),
        pltpu.make_async_copy(ocn_out_hbm, ocn_out_v, load_sem.at[1]),
    ]

    @pl.when(ocean)
    def _():
        for load in loads:
            load.start()

    for di, block, rows in ((-1, 0, slice(0, 2)), (1, 2, slice(18, 20))):
        def blank(block=block, rows=rows):
            for s in range(STEPS):
                xr[s, rows] = jnp.zeros((2, CH, LANES), BF)
                sb[s, slice(0, 48) if block == 0 else slice(112, 160)] = jnp.zeros((48, LANES), BF)
                sp_recv[s, block] = jnp.zeros((2, 16, LANES), BF)
                cp_recv[s, block // 2] = jnp.zeros((2, 16, LANES), BF)
            q[rows] = jnp.zeros((2, 8, LANES), F32)
            qe_recv[block] = jnp.zeros((2, 8, LANES), F32)

        pl.when(jnp.logical_not(has[di]))(blank)

    barrier = pltpu.get_barrier_semaphore()

    def greet(group, di, dj):
        when(
            has[di],
            lambda: pl.semaphore_signal(
                barrier, inc=1, device_id=place(group, di, dj), device_id_type=MESH
            ),
        )

    for di in (-1, 0, 1):
        for dj in (-1, 0, 1):
            greet(1 - g, di, dj)

    @pl.when(ocean)
    def _():
        for di in (-1, 0, 1):
            for dj in (-1, 0, 1):
                if di or dj:
                    greet(1, di, dj)

    def remote(src, dst, send, recv, target):
        return pltpu.make_async_remote_copy(
            src_ref=src,
            dst_ref=dst,
            send_sem=send,
            recv_sem=recv,
            device_id=target,
            device_id_type=MESH,
        )

    def s_copy(s, di, dj):
        n = 1 - di
        if dj == 0:
            src = {0: sm.at[s], 1: sm.at[s, pl.ds(16, 48)], -1: sm.at[s, pl.ds(0, 48)]}[di]
            dst = sb.at[s, pl.ds(48, 64)] if di == 0 else sb.at[s, pl.ds(0 if di == 1 else 112, 48)]
        else:
            src = sp.at[s]
            dst = sp_recv.at[s, n, 0 if dj == 1 else 1]
        return remote(src, dst, s_send.at[s, n, dj + 1], s_recv.at[s, n, dj + 1], place(1 - g, di, dj))

    def x_copy(s, di, dj):
        n = 1 - di
        if dj == 0:
            src = xr.at[s, pl.ds(16 if di == 1 else 2, 2)]
            dst = xr.at[s, pl.ds(0 if di == 1 else 18, 2)]
        elif di == 0:
            src = eg.at[s]
            dst = eg_recv.at[s, 0 if dj == 1 else 1]
        else:
            src = cp.at[s]
            dst = cp_recv.at[s, n // 2, 0 if dj == 1 else 1]
        return remote(src, dst, x_send.at[s, n, dj + 1], x_recv.at[s, n, dj + 1], place(1, di, dj))

    def q_copy(di, dj):
        n = 1 - di
        if dj == 0:
            src = q.at[pl.ds(16 if di == 1 else 2, 2)]
            dst = q.at[pl.ds(0 if di == 1 else 18, 2)]
        else:
            src = qe
            dst = qe_recv.at[n, 0 if dj == 1 else 1]
        return remote(src, dst, q_send.at[n, dj + 1], q_recv.at[n, dj + 1], place(1, di, dj))

    around = [(di, dj) for di in (-1, 0, 1) for dj in (-1, 0, 1)]
    ring = [(di, dj) for di, dj in around if di or dj]

    def start_all(make, pairs):
        for di, dj in pairs:
            when(has[di], lambda di=di, dj=dj: make(di, dj).start())

    def wait_arrivals(make, pairs):
        for di, dj in pairs:
            when(has[-di], lambda di=di, dj=dj: make(di, dj).wait_recv())

    def wait_departures(make, pairs):
        for di, dj in pairs:
            when(has[di], lambda di=di, dj=dj: make(di, dj).wait_send())

    flip[...] = state_ref[0].astype(F32).reshape(CH * ROWS, LANES)

    def to_rows(r, c):
        xr[0, r + 2] = flip[pl.ds(r, CH, stride=ROWS), :].astype(BF)
        return c

    lax.fori_loop(0, ROWS, to_rows, 0, unroll=4)

    wet_values = mask_ref[...].astype(F32)
    wet[...] = wet_values
    kept = jnp.where(ocean, wet_values, 1.0)
    for pair in range(ROWS // 2):
        upper = jnp.broadcast_to(kept[2 * pair : 2 * pair + 1], (8, LANES))
        lower = jnp.broadcast_to(kept[2 * pair + 1 : 2 * pair + 2], (8, LANES))
        keep[8 * pair : 8 * pair + 8] = jnp.where(low, upper, lower)
    high, middle, rest = thirds(proj_ref[g])
    pp[...] = jnp.concatenate([high, high, middle, middle, rest, rest], 0).astype(BF)

    def surface(s):
        def four(m, c):
            t = 4 * m + 2
            rows = jnp.concatenate([xr[s, t + u] for u in range(4)], 1)
            parts = jnp.dot(pp[...], rows, preferred_element_type=F32)
            fields = parts[0:8] + parts[8:16] + parts[16:24]
            pairs = [
                jnp.where(
                    low,
                    fields[:, 256 * u : 256 * u + 128],
                    fields[:, 256 * u + 128 : 256 * u + 256],
                )
                for u in range(2)
            ]
            start = pl.multiple_of(16 * m, 16)
            both = jnp.concatenate(pairs, 0) * keep[pl.ds(start, 16), :]
            sm[s, pl.ds(start, 16), :] = both.astype(BF)
            return c

        lax.fori_loop(0, 4, four, 0, unroll=True)
        packed = jnp.zeros((16, LANES), F32)
        slot = ((lane16 + 16) >> 5) & 3
        for m in range(4):
            tile = sm[s, 16 * m : 16 * m + 16].astype(F32)
            packed = jnp.where(slot == m, pltpu.roll(tile, 32 * m, 1) if m else tile, packed)
        sp[s] = packed.astype(BF)

    def edges(s):
        def add(t, acc):
            return jnp.where((lane80 >> 2) == t, pltpu.roll(xr[s, t], 4 * t + 2, 1), acc)

        own = lax.fori_loop(2, 18, add, jnp.zeros((CH, LANES), BF), unroll=4)
        eg[s] = own
        packed = jnp.zeros((16, LANES), BF)
        for part in range(5):
            tile = pltpu.roll(own[16 * part : 16 * part + 16], 64 + 8 * part, 1)
            place_of = lane16 - 8 * part
            inside = ((place_of >= 0) & (place_of < 8)) | ((place_of >= 72) & (place_of < 80))
            packed = jnp.where(inside, tile, packed)
        cp[s] = packed

    surface(0)

    for k in range(4):
        code = (offsets_ref[0, 0, k] + HW) * 32 + (offsets_ref[0, 1, k] + HW)
        flip[16 * k : 16 * k + 16] = code.astype(F32)
        flip[64 + 16 * k : 64 + 16 * k + 16] = weights_ref[0, k]
    for r in range(ROWS):
        q[r + 2] = flip[pl.ds(r, 8, stride=ROWS), :]

    @pl.when(ocean)
    def _():
        edges(0)

        def add(t, acc):
            return jnp.where((lane8 >> 2) == t, pltpu.roll(q[t], 4 * t + 2, 1), acc)

        qe[...] = lax.fori_loop(2, 18, add, jnp.zeros((8, LANES), F32))

    neighbours = 1 + has[-1].astype(I32) + has[1].astype(I32)
    pl.semaphore_wait(barrier, 3 * neighbours + g * (3 * neighbours - 1))

    start_all(functools.partial(s_copy, 0), around)

    @pl.when(ocean)
    def _():
        start_all(functools.partial(x_copy, 0), ring)
        start_all(q_copy, ring)

    @pl.when(ocean)
    def _():
        for load in loads:
            load.wait()

        def widen1(o, c):
            wt1[pl.ds(pl.multiple_of(16 * o, 16), 9), 0:84] = ocn_in_v[o].astype(F32)
            return c

        lax.fori_loop(0, HO, widen1, 0, unroll=8)
        wt1[16 * HO :, :] = jnp.zeros((16 * (HOP - HO), LANES), F32)
        wt2[1] = jnp.zeros((16 * CH, LANES), F32)

        def widen2(o, c):
            taps = ocn_out_v[o].astype(F32)
            wt2[0, pl.ds(pl.multiple_of(16 * o, 16), 9), :] = taps[:, 0:128]
            wt2[1, pl.ds(pl.multiple_of(16 * o, 16), 9), 0 : HO - 128] = taps[:, 128:HO]
            return c

        lax.fori_loop(0, CH, widen2, 0, unroll=8)
        channel = iota((84, 256), 0)
        lane = iota((84, 256), 1)
        bias = bias_columns(ocn_bias_ref[...], HOP)
        lane_w = iota((HOP, 256), 1)
        for a in range(3):
            total = jnp.zeros((HOP, 256), F32)
            for b in range(3):
                target = jnp.where(channel < CH, channel + CH * b, channel + 240 + 4 * b - CH)
                total = total + jnp.dot(
                    wt1[pl.ds(3 * a + b, HOP, stride=16), 0:84].astype(BF),
                    one_hot((84, 256), lane == target),
                    preferred_element_type=F32,
                )
            if a == 1:
                for part in range(3):
                    total = jnp.where(lane_w == 252 + part, bias[part], total)
            w1[a] = total.astype(BF)
            for b in range(3):
                rows = pl.ds(3 * a + b, CH, stride=16)
                halves = [wt2[half, rows, :].astype(BF) for half in range(2)]
                w2[a, CH * b : CH * b + CH, :] = jnp.concatenate(halves, 1)[:, 0:HOP]

    @pl.when(air)
    def _():
        total = jnp.dot(
            atm_in_ref[...],
            one_hot((84, 96), iota((84, 96), 0) == iota((84, 96), 1)),
            preferred_element_type=F32,
        )
        bias = bias_columns(atm_bias_ref[...], 384)
        lane = iota((384, 96), 1)
        for part in range(3):
            total = jnp.where(lane == 84 + part, bias[part], total)
        wa[...] = total.astype(BF)

    def decode(values, t, column, row):
        for kp in range(2):
            def spread(base):
                first = jnp.broadcast_to(values[base + 2 * kp : base + 2 * kp + 1], (8, LANES))
                second = jnp.broadcast_to(values[base + 2 * kp + 1 : base + 2 * kp + 2], (8, LANES))
                return jnp.where(low, first, second)

            code = spread(0).astype(I32)
            source = column + (code & 31) - HW
            inside = (source >= 0) & (source < LANES)
            gi[t, kp] = (source & (LANES - 1)) + jnp.where(inside, 0, LANES)
            gd[t, kp] = (code >> 5) + row
            gw[t, kp] = spread(4)

    def decode_row(t, c):
        decode(q[t], t, lane8, 0)
        return c

    lax.fori_loop(2, 18, decode_row, 0, unroll=2)

    @pl.when(ocean)
    def _():
        wait_arrivals(q_copy, ring)
        lax.fori_loop(0, 2, decode_row, 0)
        lax.fori_loop(18, 20, decode_row, 0)
        pos = lane8 & 3
        beside = [jnp.where(pos < 2, qe_recv[n, 0], qe_recv[n, 1]) for n in range(3)]
        ends = jnp.where(
            lane8 < 64, pltpu.roll(beside[0], 64, 1), pltpu.roll(beside[2], 64, 1)
        )
        values = jnp.where((lane8 >= 8) & (lane8 < 72), beside[1], ends)
        decode(values, TALL, jnp.where(pos < 2, pos - 2, pos + 126), lane8 >> 2)

    def spread_pair(row, which, values):
        turned = pltpu.roll(values, 4, 0)
        sd[row, which] = jnp.where(low, values, turned)
        sd[row + 1, which] = jnp.where(low, turned, values)

    def sources(s):
        def main(m, c):
            tile = sb[s, pl.ds(pl.multiple_of(16 * m, 16), 16), :].astype(F32)
            spread_pair(4 * m, 0, tile[0:8])
            spread_pair(4 * m + 2, 0, tile[8:16])
            return c

        lax.fori_loop(0, 10, main, 0, unroll=2)
        right = ((lane16 + 16) & 31) >= 16
        for n in range(3):
            tile = jnp.where(right, sp_recv[s, n, 1].astype(F32), sp_recv[s, n, 0].astype(F32))
            for m in range(4):
                row = 16 * n + 4 * m - 4
                if 0 <= row < 40:
                    turned = pltpu.roll(tile, LANES - 32 * m, 1) if m else tile
                    spread_pair(row, 1, turned[0:8])
                    spread_pair(row + 2, 1, turned[8:16])

    def take(values, index):
        return jnp.take_along_axis(values, index, axis=1, mode="promise_in_bounds")

    def combine(t, picked):
        total = picked[0] * gw[t, 0] + picked[1] * gw[t, 1]
        return total + pltpu.roll(total, 4, 0)

    def regrid_row(t, c):
        index = [gi[t, kp] & (LANES - 1) for kp in range(2)]
        beyond = [gi[t, kp] >= LANES for kp in range(2)]
        depth = [gd[t, kp] for kp in range(2)]
        picked = [jnp.zeros((8, LANES), F32) for kp in range(2)]
        for d in range(2 * HW + 1):
            here = sd[t + d + 2, 0]
            there = sd[t + d + 2, 1]
            for kp in range(2):
                value = jnp.where(beyond[kp], take(there, index[kp]), take(here, index[kp]))
                picked[kp] = jnp.where(depth[kp] == d, value, picked[kp])
        fr[t] = combine(t, picked)
        return c

    def regrid_edges():
        index = [gi[TALL, kp] & (LANES - 1) for kp in range(2)]
        beyond = [gi[TALL, kp] >= LANES for kp in range(2)]
        depth = [gd[TALL, kp] for kp in range(2)]

        def body(d, picked):
            here = sd[d + 2, 0]
            there = sd[d + 2, 1]
            out = []
            for kp in range(2):
                value = jnp.where(beyond[kp], take(there, index[kp]), take(here, index[kp]))
                out.append(jnp.where(depth[kp] == d, value, picked[kp]))
            return tuple(out)

        zero = jnp.zeros((8, LANES), F32)
        fr[TALL] = combine(TALL, lax.fori_loop(0, TALL + 2 * HW, body, (zero, zero), unroll=4))

    def finish_row(s, r, values):
        if s + 1 < STEPS:
            xr[s + 1, r + 2] = values.astype(BF)
        else:
            flip[pl.ds(r, CH, stride=ROWS), :] = values

    def air_step(s):
        lax.fori_loop(2, 18, regrid_row, 0)
        ones = jnp.where(sub8 < 7, 1.0, 0.0)
        blank = jnp.zeros((8, LANES), F32)

        def pair(p, c):
            t = 2 * p + 2
            columns = []
            for u in range(2):
                tail = jnp.concatenate([jnp.where(low, fr[t + u], ones), blank], 0).astype(BF)
                columns.append(jnp.concatenate([xr[s, t + u], tail], 0))
            hidden = gelu(
                jnp.dot(wa[...], jnp.concatenate(columns, 1), preferred_element_type=F32)
            ).astype(BF)
            update = jnp.dot(atm_out_ref[...], hidden, preferred_element_type=F32)
            for u in range(2):
                new = xr[s, t + u].astype(F32) + update[:, 128 * u : 128 * u + 128]
                finish_row(s, 2 * p + u, new)
            return c

        lax.fori_loop(0, ROWS // 2, pair, 0)

    def ocean_step(s):
        lax.fori_loop(0, TALL, regrid_row, 0)
        regrid_edges()
        wait_arrivals(functools.partial(x_copy, s), ring)

        pos = lane80 & 3
        pos8 = lane8 & 3
        own = eg[s]
        for t in (0, 1, 18, 19):
            own = jnp.where((lane80 >> 2) == t, pltpu.roll(xr[s, t], 4 * t + 2, 1), own)
        beside = jnp.where(pos < 2, eg_recv[s, 0], eg_recv[s, 1])
        pos16 = lane16 & 3
        corners = [jnp.where(pos16 < 2, cp_recv[s, n, 0], cp_recv[s, n, 1]) for n in range(2)]
        corner = jnp.where(lane16 < 64, corners[0], corners[1])
        corner = jnp.concatenate(
            [pltpu.roll(corner, LANES - 8 * part, 1) if part else corner for part in range(5)], 0
        )
        beside = jnp.where((lane80 >= 8) & (lane80 < 72), beside, corner)

        def taps(halo, mine, where):
            return (
                pltpu.roll(jnp.where(where == 0, halo, mine), 1, 1),
                halo,
                pltpu.roll(jnp.where(where == 2, mine, halo), LANES - 1, 1),
            )

        def swapped(halo, where):
            return jnp.where(where == 1, pltpu.roll(halo, LANES - 1, 1), pltpu.roll(halo, 1, 1))

        state_taps = taps(beside, own, pos)
        for b in range(3):
            x3e[CH * b : CH * b + CH] = state_taps[b]
        hh[...] = swapped(beside, pos)

        def add(t, acc):
            return jnp.where((lane8 >> 2) == t, pltpu.roll(fr[t], 4 * t + 2, 1), acc)

        own_forcing = lax.fori_loop(0, TALL, add, jnp.zeros((8, LANES), F32), unroll=4)
        beside_forcing = fr[TALL]
        first, second, third = taps(beside_forcing, own_forcing, pos8)
        ones = jnp.where(sub8 < 7, 1.0, 0.0)
        x3e[240:256] = jnp.concatenate(
            [jnp.where(low, first, second), jnp.where(low, third, ones)], 0
        ).astype(BF)
        swapped_forcing = swapped(beside_forcing, pos8)

        def widen(t, c):
            forcing = fr[t]
            turned = pltpu.roll(swapped_forcing, 126 - 4 * t, 1)
            left = jnp.where(lane8 == 0, turned, pltpu.roll(forcing, 1, 1))
            right = jnp.where(lane8 == LANES - 1, turned, pltpu.roll(forcing, LANES - 1, 1))
            x3[t, 240:256] = jnp.concatenate(
                [jnp.where(low, left, forcing), jnp.where(low, right, ones)], 0
            ).astype(BF)
            cells = xr[s, t]
            turned = pltpu.roll(hh[...], 126 - 4 * t, 1)
            x3[t, 0:80] = jnp.where(lane80 == 0, turned, pltpu.roll(cells, 1, 1))
            x3[t, 80:160] = cells
            x3[t, 160:240] = jnp.where(
                lane80 == LANES - 1, turned, pltpu.roll(cells, LANES - 1, 1)
            )
            return c

        lax.fori_loop(0, TALL, widen, 0, unroll=2)

        def first_conv(p, c):
            h = 2 * p
            total = jnp.zeros((HOP, 256), F32)
            for a in range(3):
                columns = jnp.concatenate([x3[h + a], x3[h + a + 1]], 1)
                total = total + jnp.dot(w1[a], columns, preferred_element_type=F32)
            active = gelu(total).astype(BF)
            hid[h] = active[:, 0:128]
            hid[h + 1] = active[:, 128:256]
            return c

        lax.fori_loop(0, 9, first_conv, 0)

        @pl.when(i == 0)
        def _():
            hid[0] = jnp.zeros((HOP, LANES), BF)

        @pl.when(i == lats - 1)
        def _():
            hid[17] = jnp.zeros((HOP, LANES), BF)

        total = jnp.zeros((HOP, LANES), F32)
        for a in range(3):
            columns = x3e[...]
            if a:
                columns = pltpu.roll(columns, LANES - 4 * a, 1)
            total = total + jnp.dot(w1[a], columns, preferred_element_type=F32)
        slot = iota((HOP, LANES), 1) >> 2
        outside = ((slot == 0) & (i == 0)) | ((slot == 17) & (i == lats - 1))
        he[...] = jnp.where(outside, 0.0, gelu(total)).astype(BF)
        total = jnp.zeros((240, LANES), F32)
        for a in range(3):
            columns = he[...]
            if a:
                columns = pltpu.roll(columns, LANES - 4 * a, 1)
            total = total + jnp.dot(w2[a], columns, preferred_element_type=F32)
        ze[...] = jnp.where(
            pos == 1,
            pltpu.roll(total[160:240], LANES - 1, 1),
            pltpu.roll(total[0:80], 1, 1),
        )

        def second_conv(p, c):
            r = 2 * p
            total = jnp.zeros((240, 256), F32)
            for a in range(3):
                columns = jnp.concatenate([hid[r + a], hid[r + a + 1]], 1)
                total = total + jnp.dot(w2[a], columns, preferred_element_type=F32)
            for u in range(2):
                part = total[:, 128 * u : 128 * u + 128]
                turned = pltpu.roll(ze[...], 126 - 4 * (r + u), 1)
                left = jnp.where(lane80 == 0, turned, pltpu.roll(part[0:80], 1, 1))
                right = jnp.where(
                    lane80 == LANES - 1, turned, pltpu.roll(part[160:240], LANES - 1, 1)
                )
                update = left + part[80:160] + right
                new = xr[s, r + u + 2].astype(F32) + wet[pl.ds(r + u, 1), :] * update
                finish_row(s, r + u, new)
            return c

        lax.fori_loop(0, ROWS // 2, second_conv, 0)

    for s in range(STEPS):
        if s:
            surface(s)
            start_all(functools.partial(s_copy, s), around)

            @pl.when(ocean)
            def _(s=s):
                edges(s)
                start_all(functools.partial(x_copy, s), ring)

        wait_arrivals(functools.partial(s_copy, s), around)
        sources(s)

        @pl.when(ocean)
        def _(s=s):
            ocean_step(s)

        @pl.when(air)
        def _(s=s):
            air_step(s)

    out_ref[0] = flip[...].reshape(CH, ROWS, LANES).astype(BF)

    for s in range(STEPS):
        wait_departures(functools.partial(s_copy, s), around)

    @pl.when(ocean)
    def _():
        for s in range(STEPS):
            wait_departures(functools.partial(x_copy, s), ring)
        wait_departures(q_copy, ring)


def solution(mesh):
    lats, lons = mesh.shape["lat"], mesh.shape["lon"]
    vmem = pl.BlockSpec(memory_space=pltpu.VMEM)
    anywhere = pl.BlockSpec(memory_space=pl.ANY)
    dma = pltpu.SemaphoreType.DMA

    def local(*args):
        return pl.pallas_call(
            functools.partial(kernel, lats, lons),
            out_shape=jax.ShapeDtypeStruct((1, CH, ROWS, LANES), BF),
            in_specs=[vmem] * 8 + [anywhere, vmem, anywhere],
            out_specs=vmem,
            scratch_shapes=[
                pltpu.VMEM((CH * ROWS, LANES), F32),
                pltpu.VMEM((STEPS, TALL, CH, LANES), BF),
                pltpu.VMEM((STEPS, CH, LANES), BF),
                pltpu.VMEM((STEPS, 2, CH, LANES), BF),
                pltpu.VMEM((STEPS, 16, LANES), BF),
                pltpu.VMEM((STEPS, 2, 2, 16, LANES), BF),
                pltpu.VMEM((STEPS, 64, LANES), BF),
                pltpu.VMEM((STEPS, 160, LANES), BF),
                pltpu.VMEM((STEPS, 16, LANES), BF),
                pltpu.VMEM((STEPS, 3, 2, 16, LANES), BF),
                pltpu.VMEM((TALL, 8, LANES), F32),
                pltpu.VMEM((8, LANES), F32),
                pltpu.VMEM((3, 2, 8, LANES), F32),
                pltpu.VMEM((TALL + 1, 2, 8, LANES), I32),
                pltpu.VMEM((TALL + 1, 2, 8, LANES), I32),
                pltpu.VMEM((TALL + 1, 2, 8, LANES), F32),
                pltpu.VMEM((40, 2, 8, LANES), F32),
                pltpu.VMEM((TALL + 1, 8, LANES), F32),
                pltpu.VMEM((TALL, 256, LANES), BF),
                pltpu.VMEM((256, LANES), BF),
                pltpu.VMEM((3, HOP, 256), BF),
                pltpu.VMEM((3, 240, HOP), BF),
                pltpu.VMEM((384, 96), BF),
                pltpu.VMEM((18, HOP, LANES), BF),
                pltpu.VMEM((HOP, LANES), BF),
                pltpu.VMEM((CH, LANES), BF),
                pltpu.VMEM((CH, LANES), F32),
                pltpu.VMEM((64, LANES), F32),
                pltpu.VMEM((ROWS, LANES), F32),
                pltpu.VMEM((24, CH), BF),
                pltpu.VMEM((HO, 9, 84), BF),
                pltpu.VMEM((CH, 9, HO), BF),
                pltpu.VMEM((16 * HOP, LANES), F32),
                pltpu.VMEM((2, 16 * CH, LANES), F32),
                dma((2,)),
                dma((STEPS, 3, 3)),
                dma((STEPS, 3, 3)),
                dma((STEPS, 3, 3)),
                dma((STEPS, 3, 3)),
                dma((3, 3)),
                dma((3, 3)),
            ],
            compiler_params=pltpu.CompilerParams(
                collective_id=0,
                has_side_effects=True,
                vmem_limit_bytes=48 * 1024 * 1024,
            ),
        )(*args)

    return jax.shard_map(
        local,
        mesh=mesh,
        in_specs=(
            P("grp", None, "lat", "lon"),
            P("lat", "lon"),
            P("grp", None, None, "lat", "lon"),
            P("grp", None, "lat", "lon"),
            P(),
            P(),
            P(),
            P(),
            P(),
            P(),
            P(),
        ),
        out_specs=P("grp", None, "lat", "lon"),
        check_vma=False,
    )
```

```python
import functools

import jax
import jax.numpy as jnp
from jax import lax
from jax.experimental import pallas as pl
from jax.experimental.pallas import tpu as pltpu
from jax.sharding import PartitionSpec as P

BF = jnp.bfloat16
F32 = jnp.float32
I32 = jnp.int32
MESH = pl.DeviceIdType.MESH

STEPS = 2
HW = 8
CH = 80
HO = 200
HOP = 208
ROWS = 16
LANES = 128
TALL = ROWS + 4


def iota(shape, axis):
    return lax.broadcasted_iota(I32, shape, axis)


def gelu(x):
    inner = x * (0.7978845608028654 + 0.035677408136300125 * (x * x))
    half = 0.5 * x
    return half + half * jnp.tanh(inner)


def thirds(x):
    high = x.astype(BF).astype(F32)
    middle = (x - high).astype(BF).astype(F32)
    return high, middle, x - high - middle


def kernel(
    lats,
    lons,
    state_ref,
    mask_ref,
    offsets_ref,
    weights_ref,
    proj_ref,
    atm_in_ref,
    atm_bias_ref,
    atm_out_ref,
    ocn_in_hbm,
    ocn_bias_ref,
    ocn_out_hbm,
    out_ref,
    flip,
    xr,
    eg,
    eg_recv,
    cp,
    cp_recv,
    sm,
    sb,
    sp,
    sp_recv,
    q,
    qe,
    qe_recv,
    gi,
    gd,
    gw,
    sd,
    fr,
    x3,
    x3e,
    w1,
    w2,
    wa,
    hid,
    he,
    hh,
    ze,
    keep,
    wet,
    pp,
    ocn_in_v,
    ocn_out_v,
    load_sem,
    s_send,
    s_recv,
    x_send,
    x_recv,
    q_send,
    q_recv,
):
    g = lax.axis_index("grp")
    i = lax.axis_index("lat")
    j = lax.axis_index("lon")
    ocean = g == 1
    air = g == 0
    has = {-1: i > 0, 0: None, 1: i < lats - 1}

    def place(group, di, dj):
        return (group, i + di, lax.rem(j + dj + lons, lons))

    def when(condition, action):
        if condition is None:
            action()
        else:
            pl.when(condition)(action)

    lane8 = iota((8, LANES), 1)
    sub8 = iota((8, LANES), 0)
    low = sub8 < 4
    lane80 = iota((CH, LANES), 1)
    lane16 = iota((16, LANES), 1)

    loads = [
        pltpu.make_async_copy(ocn_in_hbm, ocn_in_v, load_sem.at[0]),
        pltpu.make_async_copy(ocn_out_hbm, ocn_out_v, load_sem.at[1]),
    ]

    @pl.when(ocean)
    def _():
        for load in loads:
            load.start()

    for di, block, rows in ((-1, 0, slice(0, 2)), (1, 2, slice(18, 20))):
        def blank(block=block, rows=rows):
            for s in range(STEPS):
                xr[s, rows] = jnp.zeros((2, CH, LANES), BF)
                sb[s, slice(0, 48) if block == 0 else slice(112, 160)] = jnp.zeros((48, LANES), BF)
                sp_recv[s, block] = jnp.zeros((2, 16, LANES), BF)
                cp_recv[s, block // 2] = jnp.zeros((2, 16, LANES), BF)
            q[rows] = jnp.zeros((2, 8, LANES), F32)
            qe_recv[block] = jnp.zeros((2, 8, LANES), F32)

        pl.when(jnp.logical_not(has[di]))(blank)

    barrier = pltpu.get_barrier_semaphore()

    def greet(group, di, dj):
        when(
            has[di],
            lambda: pl.semaphore_signal(
                barrier, inc=1, device_id=place(group, di, dj), device_id_type=MESH
            ),
        )

    for di in (-1, 0, 1):
        for dj in (-1, 0, 1):
            greet(1 - g, di, dj)

    @pl.when(ocean)
    def _():
        for di in (-1, 0, 1):
            for dj in (-1, 0, 1):
                if di or dj:
                    greet(1, di, dj)

    def remote(src, dst, send, recv, target):
        return pltpu.make_async_remote_copy(
            src_ref=src,
            dst_ref=dst,
            send_sem=send,
            recv_sem=recv,
            device_id=target,
            device_id_type=MESH,
        )

    def s_copy(s, di, dj):
        n = 1 - di
        if dj == 0:
            src = {0: sm.at[s], 1: sm.at[s, pl.ds(16, 48)], -1: sm.at[s, pl.ds(0, 48)]}[di]
            dst = sb.at[s, pl.ds(48, 64)] if di == 0 else sb.at[s, pl.ds(0 if di == 1 else 112, 48)]
        else:
            src = sp.at[s]
            dst = sp_recv.at[s, n, 0 if dj == 1 else 1]
        return remote(src, dst, s_send.at[s, n, dj + 1], s_recv.at[s, n, dj + 1], place(1 - g, di, dj))

    def x_copy(s, di, dj):
        n = 1 - di
        if dj == 0:
            src = xr.at[s, pl.ds(16 if di == 1 else 2, 2)]
            dst = xr.at[s, pl.ds(0 if di == 1 else 18, 2)]
        elif di == 0:
            src = eg.at[s]
            dst = eg_recv.at[s, 0 if dj == 1 else 1]
        else:
            src = cp.at[s]
            dst = cp_recv.at[s, n // 2, 0 if dj == 1 else 1]
        return remote(src, dst, x_send.at[s, n, dj + 1], x_recv.at[s, n, dj + 1], place(1, di, dj))

    def q_copy(di, dj):
        n = 1 - di
        if dj == 0:
            src = q.at[pl.ds(16 if di == 1 else 2, 2)]
            dst = q.at[pl.ds(0 if di == 1 else 18, 2)]
        else:
            src = qe
            dst = qe_recv.at[n, 0 if dj == 1 else 1]
        return remote(src, dst, q_send.at[n, dj + 1], q_recv.at[n, dj + 1], place(1, di, dj))

    around = [(di, dj) for di in (-1, 0, 1) for dj in (-1, 0, 1)]
    ring = [(di, dj) for di, dj in around if di or dj]

    def start_all(make, pairs):
        for di, dj in pairs:
            when(has[di], lambda di=di, dj=dj: make(di, dj).start())

    def wait_arrivals(make, pairs):
        for di, dj in pairs:
            when(has[-di], lambda di=di, dj=dj: make(di, dj).wait_recv())

    def wait_departures(make, pairs):
        for di, dj in pairs:
            when(has[di], lambda di=di, dj=dj: make(di, dj).wait_send())

    flip[...] = state_ref[0].astype(F32).reshape(CH * ROWS, LANES)

    def to_rows(r, c):
        xr[0, r + 2] = flip[pl.ds(r, CH, stride=ROWS), :].astype(BF)
        return c

    lax.fori_loop(0, ROWS, to_rows, 0, unroll=4)

    wet_values = mask_ref[...].astype(F32)
    wet[...] = wet_values
    kept = jnp.where(ocean, wet_values, 1.0)
    for pair in range(ROWS // 2):
        upper = jnp.broadcast_to(kept[2 * pair : 2 * pair + 1], (8, LANES))
        lower = jnp.broadcast_to(kept[2 * pair + 1 : 2 * pair + 2], (8, LANES))
        keep[8 * pair : 8 * pair + 8] = jnp.where(low, upper, lower)
    high, middle, rest = thirds(proj_ref[g])
    pp[...] = jnp.concatenate([high, high, middle, middle, rest, rest], 0).astype(BF)

    def surface(s):
        def four(m, c):
            t = 4 * m + 2
            rows = jnp.concatenate([xr[s, t + u] for u in range(4)], 1)
            parts = jnp.dot(pp[...], rows, preferred_element_type=F32)
            fields = parts[0:8] + parts[8:16] + parts[16:24]
            pairs = [
                jnp.where(
                    low,
                    fields[:, 256 * u : 256 * u + 128],
                    fields[:, 256 * u + 128 : 256 * u + 256],
                )
                for u in range(2)
            ]
            start = pl.multiple_of(16 * m, 16)
            both = jnp.concatenate(pairs, 0) * keep[pl.ds(start, 16), :]
            sm[s, pl.ds(start, 16), :] = both.astype(BF)
            return c

        lax.fori_loop(0, 4, four, 0, unroll=True)
        packed = jnp.zeros((16, LANES), F32)
        slot = ((lane16 + 16) >> 5) & 3
        for m in range(4):
            tile = sm[s, 16 * m : 16 * m + 16].astype(F32)
            packed = jnp.where(slot == m, pltpu.roll(tile, 32 * m, 1) if m else tile, packed)
        sp[s] = packed.astype(BF)

    def edges(s):
        def add(t, acc):
            return jnp.where((lane80 >> 2) == t, pltpu.roll(xr[s, t], 4 * t + 2, 1), acc)

        own = lax.fori_loop(2, 18, add, jnp.zeros((CH, LANES), BF), unroll=4)
        eg[s] = own
        packed = jnp.zeros((16, LANES), BF)
        for part in range(5):
            tile = pltpu.roll(own[16 * part : 16 * part + 16], 64 + 8 * part, 1)
            place_of = lane16 - 8 * part
            inside = ((place_of >= 0) & (place_of < 8)) | ((place_of >= 72) & (place_of < 80))
            packed = jnp.where(inside, tile, packed)
        cp[s] = packed

    surface(0)

    for k in range(4):
        code = (offsets_ref[0, 0, k] + HW) * 32 + (offsets_ref[0, 1, k] + HW)
        flip[16 * k : 16 * k + 16] = code.astype(F32)
        flip[64 + 16 * k : 64 + 16 * k + 16] = weights_ref[0, k]
    for r in range(ROWS):
        q[r + 2] = flip[pl.ds(r, 8, stride=ROWS), :]

    @pl.when(ocean)
    def _():
        edges(0)

        def add(t, acc):
            return jnp.where((lane8 >> 2) == t, pltpu.roll(q[t], 4 * t + 2, 1), acc)

        qe[...] = lax.fori_loop(2, 18, add, jnp.zeros((8, LANES), F32))

    neighbours = 1 + has[-1].astype(I32) + has[1].astype(I32)
    pl.semaphore_wait(barrier, 3 * neighbours + g * (3 * neighbours - 1))

    start_all(functools.partial(s_copy, 0), around)

    @pl.when(ocean)
    def _():
        start_all(functools.partial(x_copy, 0), ring)
        start_all(q_copy, ring)

    @pl.when(ocean)
    def _():
        for load in loads:
            load.wait()

        def rows_of(values):
            return thirds(values.reshape(1, -1))

        spare = jnp.zeros((1, HO), F32)
        bias = jnp.concatenate([*rows_of(ocn_bias_ref[...]), spare], 0)
        for a in range(3):
            taps = [ocn_in_v[3 * a + b].astype(F32) for b in range(3)]
            last = bias if a == 1 else jnp.zeros((4, HO), F32)
            stacked = jnp.concatenate(
                [tap[0:CH] for tap in taps] + [tap[CH:] for tap in taps] + [last], 0
            )
            stacked = jnp.concatenate([stacked, jnp.zeros((256, 256 - HO), F32)], 1)
            w1[a] = stacked.T[0:HOP].astype(BF)
            for b in range(3):
                values = ocn_out_v[3 * a + b].astype(F32)
                w2[a, CH * b : CH * b + CH, :] = jnp.concatenate(
                    [values, jnp.zeros((CH, HOP - HO), F32)], 1
                ).astype(BF)

    @pl.when(air)
    def _():
        bias = thirds(atm_bias_ref[...].reshape(1, -1))
        stacked = jnp.concatenate(
            [atm_in_ref[...].astype(F32), *bias, jnp.zeros((41, 384), F32)], 0
        )
        wa[...] = stacked.T[:, 0:96].astype(BF)

    def decode(values, t, column, row):
        for kp in range(2):
            def spread(base):
                first = jnp.broadcast_to(values[base + 2 * kp : base + 2 * kp + 1], (8, LANES))
                second = jnp.broadcast_to(values[base + 2 * kp + 1 : base + 2 * kp + 2], (8, LANES))
                return jnp.where(low, first, second)

            code = spread(0).astype(I32)
            source = column + (code & 31) - HW
            inside = (source >= 0) & (source < LANES)
            gi[t, kp] = (source & (LANES - 1)) + jnp.where(inside, 0, LANES)
            gd[t, kp] = (code >> 5) + row
            gw[t, kp] = spread(4)

    def decode_row(t, c):
        decode(q[t], t, lane8, 0)
        return c

    lax.fori_loop(2, 18, decode_row, 0, unroll=2)

    @pl.when(ocean)
    def _():
        wait_arrivals(q_copy, ring)
        lax.fori_loop(0, 2, decode_row, 0)
        lax.fori_loop(18, 20, decode_row, 0)
        pos = lane8 & 3
        beside = [jnp.where(pos < 2, qe_recv[n, 0], qe_recv[n, 1]) for n in range(3)]
        ends = jnp.where(
            lane8 < 64, pltpu.roll(beside[0], 64, 1), pltpu.roll(beside[2], 64, 1)
        )
        values = jnp.where((lane8 >= 8) & (lane8 < 72), beside[1], ends)
        decode(values, TALL, jnp.where(pos < 2, pos - 2, pos + 126), lane8 >> 2)

    def spread_pair(row, which, values):
        turned = pltpu.roll(values, 4, 0)
        sd[row, which] = jnp.where(low, values, turned)
        sd[row + 1, which] = jnp.where(low, turned, values)

    def sources(s):
        def main(m, c):
            tile = sb[s, pl.ds(pl.multiple_of(16 * m, 16), 16), :].astype(F32)
            spread_pair(4 * m, 0, tile[0:8])
            spread_pair(4 * m + 2, 0, tile[8:16])
            return c

        lax.fori_loop(0, 10, main, 0, unroll=2)
        right = ((lane16 + 16) & 31) >= 16
        for n in range(3):
            tile = jnp.where(right, sp_recv[s, n, 1].astype(F32), sp_recv[s, n, 0].astype(F32))
            for m in range(4):
                row = 16 * n + 4 * m - 4
                if 0 <= row < 40:
                    turned = pltpu.roll(tile, LANES - 32 * m, 1) if m else tile
                    spread_pair(row, 1, turned[0:8])
                    spread_pair(row + 2, 1, turned[8:16])

    def take(values, index):
        return jnp.take_along_axis(values, index, axis=1, mode="promise_in_bounds")

    def combine(t, picked):
        total = picked[0] * gw[t, 0] + picked[1] * gw[t, 1]
        return total + pltpu.roll(total, 4, 0)

    def regrid_row(t, c):
        index = [gi[t, kp] & (LANES - 1) for kp in range(2)]
        beyond = [gi[t, kp] >= LANES for kp in range(2)]
        depth = [gd[t, kp] for kp in range(2)]
        picked = [jnp.zeros((8, LANES), F32) for kp in range(2)]
        for d in range(2 * HW + 1):
            here = sd[t + d + 2, 0]
            there = sd[t + d + 2, 1]
            for kp in range(2):
                value = jnp.where(beyond[kp], take(there, index[kp]), take(here, index[kp]))
                picked[kp] = jnp.where(depth[kp] == d, value, picked[kp])
        fr[t] = combine(t, picked)
        return c

    def regrid_edges():
        index = [gi[TALL, kp] & (LANES - 1) for kp in range(2)]
        beyond = [gi[TALL, kp] >= LANES for kp in range(2)]
        depth = [gd[TALL, kp] for kp in range(2)]

        def body(d, picked):
            here = sd[d + 2, 0]
            there = sd[d + 2, 1]
            out = []
            for kp in range(2):
                value = jnp.where(beyond[kp], take(there, index[kp]), take(here, index[kp]))
                out.append(jnp.where(depth[kp] == d, value, picked[kp]))
            return tuple(out)

        zero = jnp.zeros((8, LANES), F32)
        fr[TALL] = combine(TALL, lax.fori_loop(0, TALL + 2 * HW, body, (zero, zero), unroll=4))

    def finish_row(s, r, values):
        if s + 1 < STEPS:
            xr[s + 1, r + 2] = values.astype(BF)
        else:
            flip[pl.ds(r, CH, stride=ROWS), :] = values

    def air_step(s):
        lax.fori_loop(2, 18, regrid_row, 0)
        ones = jnp.where(sub8 < 7, 1.0, 0.0)
        blank = jnp.zeros((8, LANES), F32)

        def pair(p, c):
            t = 2 * p + 2
            columns = []
            for u in range(2):
                tail = jnp.concatenate([jnp.where(low, fr[t + u], ones), blank], 0).astype(BF)
                columns.append(jnp.concatenate([xr[s, t + u], tail], 0))
            hidden = gelu(
                jnp.dot(wa[...], jnp.concatenate(columns, 1), preferred_element_type=F32)
            ).astype(BF)
            update = jnp.dot(atm_out_ref[...], hidden, preferred_element_type=F32)
            for u in range(2):
                new = xr[s, t + u].astype(F32) + update[:, 128 * u : 128 * u + 128]
                finish_row(s, 2 * p + u, new)
            return c

        lax.fori_loop(0, ROWS // 2, pair, 0)

    def ocean_step(s):
        lax.fori_loop(0, TALL, regrid_row, 0)
        regrid_edges()
        wait_arrivals(functools.partial(x_copy, s), ring)

        pos = lane80 & 3
        pos8 = lane8 & 3
        own = eg[s]
        for t in (0, 1, 18, 19):
            own = jnp.where((lane80 >> 2) == t, pltpu.roll(xr[s, t], 4 * t + 2, 1), own)
        beside = jnp.where(pos < 2, eg_recv[s, 0], eg_recv[s, 1])
        pos16 = lane16 & 3
        corners = [jnp.where(pos16 < 2, cp_recv[s, n, 0], cp_recv[s, n, 1]) for n in range(2)]
        corner = jnp.where(lane16 < 64, corners[0], corners[1])
        corner = jnp.concatenate(
            [pltpu.roll(corner, LANES - 8 * part, 1) if part else corner for part in range(5)], 0
        )
        beside = jnp.where((lane80 >= 8) & (lane80 < 72), beside, corner)

        def taps(halo, mine, where):
            return (
                pltpu.roll(jnp.where(where == 0, halo, mine), 1, 1),
                halo,
                pltpu.roll(jnp.where(where == 2, mine, halo), LANES - 1, 1),
            )

        def swapped(halo, where):
            return jnp.where(where == 1, pltpu.roll(halo, LANES - 1, 1), pltpu.roll(halo, 1, 1))

        state_taps = taps(beside, own, pos)
        for b in range(3):
            x3e[CH * b : CH * b + CH] = state_taps[b]
        hh[...] = swapped(beside, pos)

        def add(t, acc):
            return jnp.where((lane8 >> 2) == t, pltpu.roll(fr[t], 4 * t + 2, 1), acc)

        own_forcing = lax.fori_loop(0, TALL, add, jnp.zeros((8, LANES), F32), unroll=4)
        beside_forcing = fr[TALL]
        first, second, third = taps(beside_forcing, own_forcing, pos8)
        ones = jnp.where(sub8 < 7, 1.0, 0.0)
        x3e[240:256] = jnp.concatenate(
            [jnp.where(low, first, second), jnp.where(low, third, ones)], 0
        ).astype(BF)
        swapped_forcing = swapped(beside_forcing, pos8)

        def widen(t, c):
            forcing = fr[t]
            turned = pltpu.roll(swapped_forcing, 126 - 4 * t, 1)
            left = jnp.where(lane8 == 0, turned, pltpu.roll(forcing, 1, 1))
            right = jnp.where(lane8 == LANES - 1, turned, pltpu.roll(forcing, LANES - 1, 1))
            x3[t, 240:256] = jnp.concatenate(
                [jnp.where(low, left, forcing), jnp.where(low, right, ones)], 0
            ).astype(BF)
            cells = xr[s, t]
            turned = pltpu.roll(hh[...], 126 - 4 * t, 1)
            x3[t, 0:80] = jnp.where(lane80 == 0, turned, pltpu.roll(cells, 1, 1))
            x3[t, 80:160] = cells
            x3[t, 160:240] = jnp.where(
                lane80 == LANES - 1, turned, pltpu.roll(cells, LANES - 1, 1)
            )
            return c

        lax.fori_loop(0, TALL, widen, 0, unroll=2)

        def first_conv(p, c):
            h = 2 * p
            total = jnp.zeros((HOP, 256), F32)
            for a in range(3):
                columns = jnp.concatenate([x3[h + a], x3[h + a + 1]], 1)
                total = total + jnp.dot(w1[a], columns, preferred_element_type=F32)
            active = gelu(total).astype(BF)
            hid[h] = active[:, 0:128]
            hid[h + 1] = active[:, 128:256]
            return c

        lax.fori_loop(0, 9, first_conv, 0)

        @pl.when(i == 0)
        def _():
            hid[0] = jnp.zeros((HOP, LANES), BF)

        @pl.when(i == lats - 1)
        def _():
            hid[17] = jnp.zeros((HOP, LANES), BF)

        total = jnp.zeros((HOP, LANES), F32)
        for a in range(3):
            columns = x3e[...]
            if a:
                columns = pltpu.roll(columns, LANES - 4 * a, 1)
            total = total + jnp.dot(w1[a], columns, preferred_element_type=F32)
        slot = iota((HOP, LANES), 1) >> 2
        outside = ((slot == 0) & (i == 0)) | ((slot == 17) & (i == lats - 1))
        he[...] = jnp.where(outside, 0.0, gelu(total)).astype(BF)
        total = jnp.zeros((240, LANES), F32)
        for a in range(3):
            columns = he[...]
            if a:
                columns = pltpu.roll(columns, LANES - 4 * a, 1)
            total = total + jnp.dot(w2[a], columns, preferred_element_type=F32)
        ze[...] = jnp.where(
            pos == 1,
            pltpu.roll(total[160:240], LANES - 1, 1),
            pltpu.roll(total[0:80], 1, 1),
        )

        def second_conv(p, c):
            r = 2 * p
            total = jnp.zeros((240, 256), F32)
            for a in range(3):
                columns = jnp.concatenate([hid[r + a], hid[r + a + 1]], 1)
                total = total + jnp.dot(w2[a], columns, preferred_element_type=F32)
            for u in range(2):
                part = total[:, 128 * u : 128 * u + 128]
                turned = pltpu.roll(ze[...], 126 - 4 * (r + u), 1)
                left = jnp.where(lane80 == 0, turned, pltpu.roll(part[0:80], 1, 1))
                right = jnp.where(
                    lane80 == LANES - 1, turned, pltpu.roll(part[160:240], LANES - 1, 1)
                )
                update = left + part[80:160] + right
                new = xr[s, r + u + 2].astype(F32) + wet[pl.ds(r + u, 1), :] * update
                finish_row(s, r + u, new)
            return c

        lax.fori_loop(0, ROWS // 2, second_conv, 0)

    for s in range(STEPS):
        if s:
            surface(s)
            start_all(functools.partial(s_copy, s), around)

            @pl.when(ocean)
            def _(s=s):
                edges(s)
                start_all(functools.partial(x_copy, s), ring)

        wait_arrivals(functools.partial(s_copy, s), around)
        sources(s)

        @pl.when(ocean)
        def _(s=s):
            ocean_step(s)

        @pl.when(air)
        def _(s=s):
            air_step(s)

    out_ref[0] = flip[...].reshape(CH, ROWS, LANES).astype(BF)

    for s in range(STEPS):
        wait_departures(functools.partial(s_copy, s), around)

    @pl.when(ocean)
    def _():
        for s in range(STEPS):
            wait_departures(functools.partial(x_copy, s), ring)
        wait_departures(q_copy, ring)


def solution(mesh):
    lats, lons = mesh.shape["lat"], mesh.shape["lon"]
    vmem = pl.BlockSpec(memory_space=pltpu.VMEM)
    anywhere = pl.BlockSpec(memory_space=pl.ANY)
    dma = pltpu.SemaphoreType.DMA

    def local(*args):
        args = list(args)
        args[5] = args[5].T
        args[8] = args[8].transpose(1, 2, 0)
        args[10] = args[10].transpose(1, 0, 2)
        return pl.pallas_call(
            functools.partial(kernel, lats, lons),
            out_shape=jax.ShapeDtypeStruct((1, CH, ROWS, LANES), BF),
            in_specs=[vmem] * 8 + [anywhere, vmem, anywhere],
            out_specs=vmem,
            scratch_shapes=[
                pltpu.VMEM((CH * ROWS, LANES), F32),
                pltpu.VMEM((STEPS, TALL, CH, LANES), BF),
                pltpu.VMEM((STEPS, CH, LANES), BF),
                pltpu.VMEM((STEPS, 2, CH, LANES), BF),
                pltpu.VMEM((STEPS, 16, LANES), BF),
                pltpu.VMEM((STEPS, 2, 2, 16, LANES), BF),
                pltpu.VMEM((STEPS, 64, LANES), BF),
                pltpu.VMEM((STEPS, 160, LANES), BF),
                pltpu.VMEM((STEPS, 16, LANES), BF),
                pltpu.VMEM((STEPS, 3, 2, 16, LANES), BF),
                pltpu.VMEM((TALL, 8, LANES), F32),
                pltpu.VMEM((8, LANES), F32),
                pltpu.VMEM((3, 2, 8, LANES), F32),
                pltpu.VMEM((TALL + 1, 2, 8, LANES), I32),
                pltpu.VMEM((TALL + 1, 2, 8, LANES), I32),
                pltpu.VMEM((TALL + 1, 2, 8, LANES), F32),
                pltpu.VMEM((40, 2, 8, LANES), F32),
                pltpu.VMEM((TALL + 1, 8, LANES), F32),
                pltpu.VMEM((TALL, 256, LANES), BF),
                pltpu.VMEM((256, LANES), BF),
                pltpu.VMEM((3, HOP, 256), BF),
                pltpu.VMEM((3, 240, HOP), BF),
                pltpu.VMEM((384, 96), BF),
                pltpu.VMEM((18, HOP, LANES), BF),
                pltpu.VMEM((HOP, LANES), BF),
                pltpu.VMEM((CH, LANES), BF),
                pltpu.VMEM((CH, LANES), F32),
                pltpu.VMEM((64, LANES), F32),
                pltpu.VMEM((ROWS, LANES), F32),
                pltpu.VMEM((24, CH), BF),
                pltpu.VMEM((9, 84, HO), BF),
                pltpu.VMEM((9, CH, HO), BF),
                dma((2,)),
                dma((STEPS, 3, 3)),
                dma((STEPS, 3, 3)),
                dma((STEPS, 3, 3)),
                dma((STEPS, 3, 3)),
                dma((3, 3)),
                dma((3, 3)),
            ],
            compiler_params=pltpu.CompilerParams(
                collective_id=0,
                has_side_effects=True,
                vmem_limit_bytes=48 * 1024 * 1024,
            ),
        )(*args)

    return jax.shard_map(
        local,
        mesh=mesh,
        in_specs=(
            P("grp", None, "lat", "lon"),
            P("lat", "lon"),
            P("grp", None, None, "lat", "lon"),
            P("grp", None, "lat", "lon"),
            P(),
            P(),
            P(),
            P(),
            P(),
            P(),
            P(),
        ),
        out_specs=P("grp", None, "lat", "lon"),
        check_vma=False,
    )
```

```python
import functools

import jax
import jax.numpy as jnp
from jax import lax
from jax.experimental import pallas as pl
from jax.experimental.pallas import tpu as pltpu
from jax.sharding import PartitionSpec as P

BF = jnp.bfloat16
F32 = jnp.float32
I32 = jnp.int32
MESH = pl.DeviceIdType.MESH

STEPS = 2
HW = 8
CH = 80
HO = 200
HOP = 208
ROWS = 16
LANES = 128
TALL = ROWS + 4


def iota(shape, axis):
    return lax.broadcasted_iota(I32, shape, axis)


def gelu(x):
    inner = x * (0.7978845608028654 + 0.035677408136300125 * (x * x))
    half = 0.5 * x
    return half + half * jnp.tanh(inner)


def thirds(x):
    high = x.astype(BF).astype(F32)
    middle = (x - high).astype(BF).astype(F32)
    return high, middle, x - high - middle


def kernel(
    lats,
    lons,
    state_hbm,
    mask_hbm,
    offsets_hbm,
    weights_hbm,
    proj_hbm,
    atm_in_hbm,
    atm_bias_hbm,
    atm_out_hbm,
    ocn_in_hbm,
    ocn_bias_hbm,
    ocn_out_hbm,
    out_ref,
    state_ref,
    mask_ref,
    offsets_ref,
    weights_ref,
    proj_ref,
    atm_in_ref,
    atm_bias_ref,
    atm_out_ref,
    ocn_in_v,
    ocn_bias_ref,
    ocn_out_v,
    flip,
    xr,
    eg,
    eg_recv,
    cp,
    cp_recv,
    sm,
    sb,
    sp,
    sp_recv,
    q,
    qe,
    qe_recv,
    gi,
    gd,
    gw,
    sd,
    fr,
    x3,
    x3e,
    w1,
    w2,
    wa,
    hid,
    he,
    hh,
    ze,
    keep,
    wet,
    pp,
    load_sem,
    s_send,
    s_recv,
    x_send,
    x_recv,
    q_send,
    q_recv,
):
    g = lax.axis_index("grp")
    i = lax.axis_index("lat")
    j = lax.axis_index("lon")
    ocean = g == 1
    air = g == 0
    has = {-1: i > 0, 0: None, 1: i < lats - 1}

    def place(group, di, dj):
        return (group, i + di, lax.rem(j + dj + lons, lons))

    def when(condition, action):
        if condition is None:
            action()
        else:
            pl.when(condition)(action)

    lane8 = iota((8, LANES), 1)
    sub8 = iota((8, LANES), 0)
    low = sub8 < 4
    lane80 = iota((CH, LANES), 1)
    lane16 = iota((16, LANES), 1)

    pairs = (
        (state_hbm, state_ref),
        (mask_hbm, mask_ref),
        (offsets_hbm, offsets_ref),
        (weights_hbm, weights_ref),
        (proj_hbm, proj_ref),
        (atm_in_hbm, atm_in_ref),
        (atm_bias_hbm, atm_bias_ref),
        (atm_out_hbm, atm_out_ref),
        (ocn_in_hbm, ocn_in_v),
        (ocn_bias_hbm, ocn_bias_ref),
        (ocn_out_hbm, ocn_out_v),
    )
    loads = [
        pltpu.make_async_copy(src, dst, load_sem.at[n]) for n, (src, dst) in enumerate(pairs)
    ]
    for load in loads[0:5]:
        load.start()

    @pl.when(ocean)
    def _():
        for load in loads[8:11]:
            load.start()

    @pl.when(air)
    def _():
        for load in loads[5:8]:
            load.start()

    for di, block, rows in ((-1, 0, slice(0, 2)), (1, 2, slice(18, 20))):
        def blank(block=block, rows=rows):
            for s in range(STEPS):
                xr[s, rows] = jnp.zeros((2, CH, LANES), BF)
                sb[s, slice(0, 48) if block == 0 else slice(112, 160)] = jnp.zeros((48, LANES), BF)
                sp_recv[s, block] = jnp.zeros((2, 16, LANES), BF)
                cp_recv[s, block // 2] = jnp.zeros((2, 16, LANES), BF)
            q[rows] = jnp.zeros((2, 8, LANES), F32)
            qe_recv[block] = jnp.zeros((2, 8, LANES), F32)

        pl.when(jnp.logical_not(has[di]))(blank)

    barrier = pltpu.get_barrier_semaphore()

    def greet(group, di, dj):
        when(
            has[di],
            lambda: pl.semaphore_signal(
                barrier, inc=1, device_id=place(group, di, dj), device_id_type=MESH
            ),
        )

    for di in (-1, 0, 1):
        for dj in (-1, 0, 1):
            greet(1 - g, di, dj)

    @pl.when(ocean)
    def _():
        for di in (-1, 0, 1):
            for dj in (-1, 0, 1):
                if di or dj:
                    greet(1, di, dj)

    def remote(src, dst, send, recv, target):
        return pltpu.make_async_remote_copy(
            src_ref=src,
            dst_ref=dst,
            send_sem=send,
            recv_sem=recv,
            device_id=target,
            device_id_type=MESH,
        )

    def s_copy(s, di, dj):
        n = 1 - di
        if dj == 0:
            src = {0: sm.at[s], 1: sm.at[s, pl.ds(16, 48)], -1: sm.at[s, pl.ds(0, 48)]}[di]
            dst = sb.at[s, pl.ds(48, 64)] if di == 0 else sb.at[s, pl.ds(0 if di == 1 else 112, 48)]
        else:
            src = sp.at[s]
            dst = sp_recv.at[s, n, 0 if dj == 1 else 1]
        return remote(src, dst, s_send.at[s, n, dj + 1], s_recv.at[s, n, dj + 1], place(1 - g, di, dj))

    def x_copy(s, di, dj):
        n = 1 - di
        if dj == 0:
            src = xr.at[s, pl.ds(16 if di == 1 else 2, 2)]
            dst = xr.at[s, pl.ds(0 if di == 1 else 18, 2)]
        elif di == 0:
            src = eg.at[s]
            dst = eg_recv.at[s, 0 if dj == 1 else 1]
        else:
            src = cp.at[s]
            dst = cp_recv.at[s, n // 2, 0 if dj == 1 else 1]
        return remote(src, dst, x_send.at[s, n, dj + 1], x_recv.at[s, n, dj + 1], place(1, di, dj))

    def q_copy(di, dj):
        n = 1 - di
        if dj == 0:
            src = q.at[pl.ds(16 if di == 1 else 2, 2)]
            dst = q.at[pl.ds(0 if di == 1 else 18, 2)]
        else:
            src = qe
            dst = qe_recv.at[n, 0 if dj == 1 else 1]
        return remote(src, dst, q_send.at[n, dj + 1], q_recv.at[n, dj + 1], place(1, di, dj))

    around = [(di, dj) for di in (-1, 0, 1) for dj in (-1, 0, 1)]
    ring = [(di, dj) for di, dj in around if di or dj]

    def start_all(make, pairs):
        for di, dj in pairs:
            when(has[di], lambda di=di, dj=dj: make(di, dj).start())

    def wait_arrivals(make, pairs):
        for di, dj in pairs:
            when(has[-di], lambda di=di, dj=dj: make(di, dj).wait_recv())

    def wait_departures(make, pairs):
        for di, dj in pairs:
            when(has[di], lambda di=di, dj=dj: make(di, dj).wait_send())

    loads[0].wait()
    flip[...] = state_ref[0].astype(F32).reshape(CH * ROWS, LANES)

    def to_rows(r, c):
        xr[0, r + 2] = flip[pl.ds(r, CH, stride=ROWS), :].astype(BF)
        return c

    lax.fori_loop(0, ROWS, to_rows, 0, unroll=4)

    loads[1].wait()
    loads[4].wait()
    wet_values = mask_ref[...].astype(F32)
    wet[...] = wet_values
    kept = jnp.where(ocean, wet_values, 1.0)
    for pair in range(ROWS // 2):
        upper = jnp.broadcast_to(kept[2 * pair : 2 * pair + 1], (8, LANES))
        lower = jnp.broadcast_to(kept[2 * pair + 1 : 2 * pair + 2], (8, LANES))
        keep[8 * pair : 8 * pair + 8] = jnp.where(low, upper, lower)
    high, middle, rest = thirds(proj_ref[g])
    pp[...] = jnp.concatenate([high, high, middle, middle, rest, rest], 0).astype(BF)

    def surface(s):
        def four(m, c):
            t = 4 * m + 2
            rows = jnp.concatenate([xr[s, t + u] for u in range(4)], 1)
            parts = jnp.dot(pp[...], rows, preferred_element_type=F32)
            fields = parts[0:8] + parts[8:16] + parts[16:24]
            pairs = [
                jnp.where(
                    low,
                    fields[:, 256 * u : 256 * u + 128],
                    fields[:, 256 * u + 128 : 256 * u + 256],
                )
                for u in range(2)
            ]
            start = pl.multiple_of(16 * m, 16)
            both = jnp.concatenate(pairs, 0) * keep[pl.ds(start, 16), :]
            sm[s, pl.ds(start, 16), :] = both.astype(BF)
            return c

        lax.fori_loop(0, 4, four, 0, unroll=True)
        packed = jnp.zeros((16, LANES), F32)
        slot = ((lane16 + 16) >> 5) & 3
        for m in range(4):
            tile = sm[s, 16 * m : 16 * m + 16].astype(F32)
            packed = jnp.where(slot == m, pltpu.roll(tile, 32 * m, 1) if m else tile, packed)
        sp[s] = packed.astype(BF)

    def edges(s):
        def add(t, acc):
            return jnp.where((lane80 >> 2) == t, pltpu.roll(xr[s, t], 4 * t + 2, 1), acc)

        own = lax.fori_loop(2, 18, add, jnp.zeros((CH, LANES), BF), unroll=4)
        eg[s] = own
        packed = jnp.zeros((16, LANES), BF)
        for part in range(5):
            tile = pltpu.roll(own[16 * part : 16 * part + 16], 64 + 8 * part, 1)
            place_of = lane16 - 8 * part
            inside = ((place_of >= 0) & (place_of < 8)) | ((place_of >= 72) & (place_of < 80))
            packed = jnp.where(inside, tile, packed)
        cp[s] = packed

    surface(0)

    loads[2].wait()
    loads[3].wait()
    for k in range(4):
        code = (offsets_ref[0, 0, k] + HW) * 32 + (offsets_ref[0, 1, k] + HW)
        flip[16 * k : 16 * k + 16] = code.astype(F32)
        flip[64 + 16 * k : 64 + 16 * k + 16] = weights_ref[0, k]
    for r in range(ROWS):
        q[r + 2] = flip[pl.ds(r, 8, stride=ROWS), :]

    @pl.when(ocean)
    def _():
        edges(0)

        def add(t, acc):
            return jnp.where((lane8 >> 2) == t, pltpu.roll(q[t], 4 * t + 2, 1), acc)

        qe[...] = lax.fori_loop(2, 18, add, jnp.zeros((8, LANES), F32))

    neighbours = 1 + has[-1].astype(I32) + has[1].astype(I32)
    pl.semaphore_wait(barrier, 3 * neighbours + g * (3 * neighbours - 1))

    start_all(functools.partial(s_copy, 0), around)

    @pl.when(ocean)
    def _():
        start_all(functools.partial(x_copy, 0), ring)
        start_all(q_copy, ring)

    @pl.when(ocean)
    def _():
        for load in loads[8:11]:
            load.wait()

        def rows_of(values):
            return thirds(values.reshape(1, -1))

        spare = jnp.zeros((1, HO), F32)
        bias = jnp.concatenate([*rows_of(ocn_bias_ref[...]), spare], 0)
        for a in range(3):
            taps = [ocn_in_v[3 * a + b].astype(F32) for b in range(3)]
            last = bias if a == 1 else jnp.zeros((4, HO), F32)
            stacked = jnp.concatenate(
                [tap[0:CH] for tap in taps] + [tap[CH:] for tap in taps] + [last], 0
            )
            stacked = jnp.concatenate([stacked, jnp.zeros((256, 256 - HO), F32)], 1)
            w1[a] = stacked.T[0:HOP].astype(BF)
            for b in range(3):
                values = ocn_out_v[3 * a + b].astype(F32)
                w2[a, CH * b : CH * b + CH, :] = jnp.concatenate(
                    [values, jnp.zeros((CH, HOP - HO), F32)], 1
                ).astype(BF)

    @pl.when(air)
    def _():
        for load in loads[5:8]:
            load.wait()
        bias = thirds(atm_bias_ref[...].reshape(1, -1))
        stacked = jnp.concatenate(
            [atm_in_ref[...].astype(F32), *bias, jnp.zeros((41, 384), F32)], 0
        )
        wa[...] = stacked.T[:, 0:96].astype(BF)

    def decode(values, t, column, row):
        for kp in range(2):
            def spread(base):
                first = jnp.broadcast_to(values[base + 2 * kp : base + 2 * kp + 1], (8, LANES))
                second = jnp.broadcast_to(values[base + 2 * kp + 1 : base + 2 * kp + 2], (8, LANES))
                return jnp.where(low, first, second)

            code = spread(0).astype(I32)
            source = column + (code & 31) - HW
            inside = (source >= 0) & (source < LANES)
            gi[t, kp] = (source & (LANES - 1)) + jnp.where(inside, 0, LANES)
            gd[t, kp] = (code >> 5) + row
            gw[t, kp] = spread(4)

    def decode_row(t, c):
        decode(q[t], t, lane8, 0)
        return c

    lax.fori_loop(2, 18, decode_row, 0, unroll=2)

    @pl.when(ocean)
    def _():
        wait_arrivals(q_copy, ring)
        lax.fori_loop(0, 2, decode_row, 0)
        lax.fori_loop(18, 20, decode_row, 0)
        pos = lane8 & 3
        beside = [jnp.where(pos < 2, qe_recv[n, 0], qe_recv[n, 1]) for n in range(3)]
        ends = jnp.where(
            lane8 < 64, pltpu.roll(beside[0], 64, 1), pltpu.roll(beside[2], 64, 1)
        )
        values = jnp.where((lane8 >= 8) & (lane8 < 72), beside[1], ends)
        decode(values, TALL, jnp.where(pos < 2, pos - 2, pos + 126), lane8 >> 2)

    def spread_pair(row, which, values):
        turned = pltpu.roll(values, 4, 0)
        sd[row, which] = jnp.where(low, values, turned)
        sd[row + 1, which] = jnp.where(low, turned, values)

    def sources(s):
        def main(m, c):
            tile = sb[s, pl.ds(pl.multiple_of(16 * m, 16), 16), :].astype(F32)
            spread_pair(4 * m, 0, tile[0:8])
            spread_pair(4 * m + 2, 0, tile[8:16])
            return c

        lax.fori_loop(0, 10, main, 0, unroll=2)
        right = ((lane16 + 16) & 31) >= 16
        for n in range(3):
            tile = jnp.where(right, sp_recv[s, n, 1].astype(F32), sp_recv[s, n, 0].astype(F32))
            for m in range(4):
                row = 16 * n + 4 * m - 4
                if 0 <= row < 40:
                    turned = pltpu.roll(tile, LANES - 32 * m, 1) if m else tile
                    spread_pair(row, 1, turned[0:8])
                    spread_pair(row + 2, 1, turned[8:16])

    def take(values, index):
        return jnp.take_along_axis(values, index, axis=1, mode="promise_in_bounds")

    def combine(t, picked):
        total = picked[0] * gw[t, 0] + picked[1] * gw[t, 1]
        return total + pltpu.roll(total, 4, 0)

    def regrid_row(t, c):
        index = [gi[t, kp] & (LANES - 1) for kp in range(2)]
        beyond = [gi[t, kp] >= LANES for kp in range(2)]
        depth = [gd[t, kp] for kp in range(2)]
        picked = [jnp.zeros((8, LANES), F32) for kp in range(2)]
        for d in range(2 * HW + 1):
            here = sd[t + d + 2, 0]
            there = sd[t + d + 2, 1]
            for kp in range(2):
                value = jnp.where(beyond[kp], take(there, index[kp]), take(here, index[kp]))
                picked[kp] = jnp.where(depth[kp] == d, value, picked[kp])
        fr[t] = combine(t, picked)
        return c

    def regrid_edges():
        index = [gi[TALL, kp] & (LANES - 1) for kp in range(2)]
        beyond = [gi[TALL, kp] >= LANES for kp in range(2)]
        depth = [gd[TALL, kp] for kp in range(2)]

        def body(d, picked):
            here = sd[d + 2, 0]
            there = sd[d + 2, 1]
            out = []
            for kp in range(2):
                value = jnp.where(beyond[kp], take(there, index[kp]), take(here, index[kp]))
                out.append(jnp.where(depth[kp] == d, value, picked[kp]))
            return tuple(out)

        zero = jnp.zeros((8, LANES), F32)
        fr[TALL] = combine(TALL, lax.fori_loop(0, TALL + 2 * HW, body, (zero, zero), unroll=4))

    def finish_row(s, r, values):
        if s + 1 < STEPS:
            xr[s + 1, r + 2] = values.astype(BF)
        else:
            flip[pl.ds(r, CH, stride=ROWS), :] = values

    def air_step(s):
        lax.fori_loop(2, 18, regrid_row, 0)
        ones = jnp.where(sub8 < 7, 1.0, 0.0)
        blank = jnp.zeros((8, LANES), F32)

        def pair(p, c):
            t = 2 * p + 2
            columns = []
            for u in range(2):
                tail = jnp.concatenate([jnp.where(low, fr[t + u], ones), blank], 0).astype(BF)
                columns.append(jnp.concatenate([xr[s, t + u], tail], 0))
            hidden = gelu(
                jnp.dot(wa[...], jnp.concatenate(columns, 1), preferred_element_type=F32)
            ).astype(BF)
            update = jnp.dot(atm_out_ref[...], hidden, preferred_element_type=F32)
            for u in range(2):
                new = xr[s, t + u].astype(F32) + update[:, 128 * u : 128 * u + 128]
                finish_row(s, 2 * p + u, new)
            return c

        lax.fori_loop(0, ROWS // 2, pair, 0)

    def ocean_step(s):
        lax.fori_loop(0, TALL, regrid_row, 0)
        regrid_edges()
        wait_arrivals(functools.partial(x_copy, s), ring)

        pos = lane80 & 3
        pos8 = lane8 & 3
        own = eg[s]
        for t in (0, 1, 18, 19):
            own = jnp.where((lane80 >> 2) == t, pltpu.roll(xr[s, t], 4 * t + 2, 1), own)
        beside = jnp.where(pos < 2, eg_recv[s, 0], eg_recv[s, 1])
        pos16 = lane16 & 3
        corners = [jnp.where(pos16 < 2, cp_recv[s, n, 0], cp_recv[s, n, 1]) for n in range(2)]
        corner = jnp.where(lane16 < 64, corners[0], corners[1])
        corner = jnp.concatenate(
            [pltpu.roll(corner, LANES - 8 * part, 1) if part else corner for part in range(5)], 0
        )
        beside = jnp.where((lane80 >= 8) & (lane80 < 72), beside, corner)

        def taps(halo, mine, where):
            return (
                pltpu.roll(jnp.where(where == 0, halo, mine), 1, 1),
                halo,
                pltpu.roll(jnp.where(where == 2, mine, halo), LANES - 1, 1),
            )

        def swapped(halo, where):
            return jnp.where(where == 1, pltpu.roll(halo, LANES - 1, 1), pltpu.roll(halo, 1, 1))

        state_taps = taps(beside, own, pos)
        for b in range(3):
            x3e[CH * b : CH * b + CH] = state_taps[b]
        hh[...] = swapped(beside, pos)

        def add(t, acc):
            return jnp.where((lane8 >> 2) == t, pltpu.roll(fr[t], 4 * t + 2, 1), acc)

        own_forcing = lax.fori_loop(0, TALL, add, jnp.zeros((8, LANES), F32), unroll=4)
        beside_forcing = fr[TALL]
        first, second, third = taps(beside_forcing, own_forcing, pos8)
        ones = jnp.where(sub8 < 7, 1.0, 0.0)
        x3e[240:256] = jnp.concatenate(
            [jnp.where(low, first, second), jnp.where(low, third, ones)], 0
        ).astype(BF)
        swapped_forcing = swapped(beside_forcing, pos8)

        def widen(t, c):
            forcing = fr[t]
            turned = pltpu.roll(swapped_forcing, 126 - 4 * t, 1)
            left = jnp.where(lane8 == 0, turned, pltpu.roll(forcing, 1, 1))
            right = jnp.where(lane8 == LANES - 1, turned, pltpu.roll(forcing, LANES - 1, 1))
            x3[t, 240:256] = jnp.concatenate(
                [jnp.where(low, left, forcing), jnp.where(low, right, ones)], 0
            ).astype(BF)
            cells = xr[s, t]
            turned = pltpu.roll(hh[...], 126 - 4 * t, 1)
            x3[t, 0:80] = jnp.where(lane80 == 0, turned, pltpu.roll(cells, 1, 1))
            x3[t, 80:160] = cells
            x3[t, 160:240] = jnp.where(
                lane80 == LANES - 1, turned, pltpu.roll(cells, LANES - 1, 1)
            )
            return c

        lax.fori_loop(0, TALL, widen, 0, unroll=2)

        def first_conv(p, c):
            h = 2 * p
            total = jnp.zeros((HOP, 256), F32)
            for a in range(3):
                columns = jnp.concatenate([x3[h + a], x3[h + a + 1]], 1)
                total = total + jnp.dot(w1[a], columns, preferred_element_type=F32)
            active = gelu(total).astype(BF)
            hid[h] = active[:, 0:128]
            hid[h + 1] = active[:, 128:256]
            return c

        lax.fori_loop(0, 9, first_conv, 0)

        @pl.when(i == 0)
        def _():
            hid[0] = jnp.zeros((HOP, LANES), BF)

        @pl.when(i == lats - 1)
        def _():
            hid[17] = jnp.zeros((HOP, LANES), BF)

        total = jnp.zeros((HOP, LANES), F32)
        for a in range(3):
            columns = x3e[...]
            if a:
                columns = pltpu.roll(columns, LANES - 4 * a, 1)
            total = total + jnp.dot(w1[a], columns, preferred_element_type=F32)
        slot = iota((HOP, LANES), 1) >> 2
        outside = ((slot == 0) & (i == 0)) | ((slot == 17) & (i == lats - 1))
        he[...] = jnp.where(outside, 0.0, gelu(total)).astype(BF)
        total = jnp.zeros((240, LANES), F32)
        for a in range(3):
            columns = he[...]
            if a:
                columns = pltpu.roll(columns, LANES - 4 * a, 1)
            total = total + jnp.dot(w2[a], columns, preferred_element_type=F32)
        ze[...] = jnp.where(
            pos == 1,
            pltpu.roll(total[160:240], LANES - 1, 1),
            pltpu.roll(total[0:80], 1, 1),
        )

        def second_conv(p, c):
            r = 2 * p
            total = jnp.zeros((240, 256), F32)
            for a in range(3):
                columns = jnp.concatenate([hid[r + a], hid[r + a + 1]], 1)
                total = total + jnp.dot(w2[a], columns, preferred_element_type=F32)
            for u in range(2):
                part = total[:, 128 * u : 128 * u + 128]
                turned = pltpu.roll(ze[...], 126 - 4 * (r + u), 1)
                left = jnp.where(lane80 == 0, turned, pltpu.roll(part[0:80], 1, 1))
                right = jnp.where(
                    lane80 == LANES - 1, turned, pltpu.roll(part[160:240], LANES - 1, 1)
                )
                update = left + part[80:160] + right
                new = xr[s, r + u + 2].astype(F32) + wet[pl.ds(r + u, 1), :] * update
                finish_row(s, r + u, new)
            return c

        lax.fori_loop(0, ROWS // 2, second_conv, 0)

    for s in range(STEPS):
        if s:
            surface(s)
            start_all(functools.partial(s_copy, s), around)

            @pl.when(ocean)
            def _(s=s):
                edges(s)
                start_all(functools.partial(x_copy, s), ring)

        wait_arrivals(functools.partial(s_copy, s), around)
        sources(s)

        @pl.when(ocean)
        def _(s=s):
            ocean_step(s)

        @pl.when(air)
        def _(s=s):
            air_step(s)

    out_ref[0] = flip[...].reshape(CH, ROWS, LANES).astype(BF)

    for s in range(STEPS):
        wait_departures(functools.partial(s_copy, s), around)

    @pl.when(ocean)
    def _():
        for s in range(STEPS):
            wait_departures(functools.partial(x_copy, s), ring)
        wait_departures(q_copy, ring)


def solution(mesh):
    lats, lons = mesh.shape["lat"], mesh.shape["lon"]
    vmem = pl.BlockSpec(memory_space=pltpu.VMEM)
    anywhere = pl.BlockSpec(memory_space=pl.ANY)
    dma = pltpu.SemaphoreType.DMA

    def local(*args):
        args = list(args)
        args[5] = args[5].T
        args[8] = args[8].transpose(1, 2, 0)
        args[10] = args[10].transpose(1, 0, 2)
        return pl.pallas_call(
            functools.partial(kernel, lats, lons),
            out_shape=jax.ShapeDtypeStruct((1, CH, ROWS, LANES), BF),
            in_specs=[anywhere] * 11,
            out_specs=vmem,
            scratch_shapes=[
                pltpu.VMEM((1, CH, ROWS, LANES), BF),
                pltpu.VMEM((ROWS, LANES), I32),
                pltpu.VMEM((1, 2, 4, ROWS, LANES), I32),
                pltpu.VMEM((1, 4, ROWS, LANES), F32),
                pltpu.VMEM((2, 4, CH), F32),
                pltpu.VMEM((84, 384), BF),
                pltpu.VMEM((384,), F32),
                pltpu.VMEM((CH, 384), BF),
                pltpu.VMEM((9, 84, HO), BF),
                pltpu.VMEM((HO,), F32),
                pltpu.VMEM((9, CH, HO), BF),
                pltpu.VMEM((CH * ROWS, LANES), F32),
                pltpu.VMEM((STEPS, TALL, CH, LANES), BF),
                pltpu.VMEM((STEPS, CH, LANES), BF),
                pltpu.VMEM((STEPS, 2, CH, LANES), BF),
                pltpu.VMEM((STEPS, 16, LANES), BF),
                pltpu.VMEM((STEPS, 2, 2, 16, LANES), BF),
                pltpu.VMEM((STEPS, 64, LANES), BF),
                pltpu.VMEM((STEPS, 160, LANES), BF),
                pltpu.VMEM((STEPS, 16, LANES), BF),
                pltpu.VMEM((STEPS, 3, 2, 16, LANES), BF),
                pltpu.VMEM((TALL, 8, LANES), F32),
                pltpu.VMEM((8, LANES), F32),
                pltpu.VMEM((3, 2, 8, LANES), F32),
                pltpu.VMEM((TALL + 1, 2, 8, LANES), I32),
                pltpu.VMEM((TALL + 1, 2, 8, LANES), I32),
                pltpu.VMEM((TALL + 1, 2, 8, LANES), F32),
                pltpu.VMEM((40, 2, 8, LANES), F32),
                pltpu.VMEM((TALL + 1, 8, LANES), F32),
                pltpu.VMEM((TALL, 256, LANES), BF),
                pltpu.VMEM((256, LANES), BF),
                pltpu.VMEM((3, HOP, 256), BF),
                pltpu.VMEM((3, 240, HOP), BF),
                pltpu.VMEM((384, 96), BF),
                pltpu.VMEM((18, HOP, LANES), BF),
                pltpu.VMEM((HOP, LANES), BF),
                pltpu.VMEM((CH, LANES), BF),
                pltpu.VMEM((CH, LANES), F32),
                pltpu.VMEM((64, LANES), F32),
                pltpu.VMEM((ROWS, LANES), F32),
                pltpu.VMEM((24, CH), BF),
                dma((11,)),
                dma((STEPS, 3, 3)),
                dma((STEPS, 3, 3)),
                dma((STEPS, 3, 3)),
                dma((STEPS, 3, 3)),
                dma((3, 3)),
                dma((3, 3)),
            ],
            compiler_params=pltpu.CompilerParams(
                collective_id=0,
                has_side_effects=True,
                vmem_limit_bytes=60 * 1024 * 1024,
            ),
        )(*args)

    return jax.shard_map(
        local,
        mesh=mesh,
        in_specs=(
            P("grp", None, "lat", "lon"),
            P("lat", "lon"),
            P("grp", None, None, "lat", "lon"),
            P("grp", None, "lat", "lon"),
            P(),
            P(),
            P(),
            P(),
            P(),
            P(),
            P(),
        ),
        out_specs=P("grp", None, "lat", "lon"),
        check_vma=False,
    )
```

```python
import functools

import jax
import jax.numpy as jnp
from jax import lax
from jax.experimental import pallas as pl
from jax.experimental.pallas import tpu as pltpu
from jax.sharding import PartitionSpec as P

BF = jnp.bfloat16
F32 = jnp.float32
I32 = jnp.int32
MESH = pl.DeviceIdType.MESH

STEPS = 2
HW = 8
CH = 80
HO = 200
HOP = 208
ROWS = 16
LANES = 128
TALL = ROWS + 4


def iota(shape, axis):
    return lax.broadcasted_iota(I32, shape, axis)


def gelu(x):
    inner = x * (0.7978845608028654 + 0.035677408136300125 * (x * x))
    half = 0.5 * x
    return half + half * jnp.tanh(inner)


def thirds(x):
    high = x.astype(BF).astype(F32)
    middle = (x - high).astype(BF).astype(F32)
    return high, middle, x - high - middle


def kernel(
    lats,
    lons,
    state_hbm,
    mask_hbm,
    offsets_hbm,
    weights_hbm,
    proj_hbm,
    atm_in_hbm,
    atm_bias_hbm,
    atm_out_hbm,
    ocn_in_hbm,
    ocn_bias_hbm,
    ocn_out_hbm,
    out_ref,
    state_ref,
    mask_ref,
    offsets_ref,
    weights_ref,
    proj_ref,
    atm_in_ref,
    atm_bias_ref,
    atm_out_ref,
    ocn_in_v,
    ocn_bias_ref,
    ocn_out_v,
    flip,
    xr,
    eg,
    eg_recv,
    cp,
    cp_recv,
    srow,
    sm,
    sb,
    sp,
    sp_recv,
    q,
    qe,
    qe_recv,
    gi,
    gw,
    src,
    fp,
    fr,
    x3,
    x3e,
    w1,
    w2,
    wa,
    hid,
    he,
    hh,
    ze,
    keep,
    wet,
    pp,
    load_sem,
    s_send,
    s_recv,
    x_send,
    x_recv,
    q_send,
    q_recv,
):
    g = lax.axis_index("grp")
    i = lax.axis_index("lat")
    j = lax.axis_index("lon")
    ocean = g == 1
    air = g == 0
    has = {-1: i > 0, 0: None, 1: i < lats - 1}

    def run(steps, body):
        for step in steps:
            body(step, 0)

    def place(group, di, dj):
        return (group, i + di, lax.rem(j + dj + lons, lons))

    def when(condition, action):
        if condition is None:
            action()
        else:
            pl.when(condition)(action)

    lane8 = iota((8, LANES), 1)
    sub8 = iota((8, LANES), 0)
    low = sub8 < 4
    lane80 = iota((CH, LANES), 1)
    lane16 = iota((16, LANES), 1)
    inner8 = lane8 & 15
    air_shift = jnp.where(air, 2, 0)
    ocean_shift = jnp.where(ocean, 2, 0)

    pairs = (
        (state_hbm, state_ref),
        (mask_hbm, mask_ref),
        (offsets_hbm, offsets_ref),
        (weights_hbm, weights_ref),
        (proj_hbm, proj_ref),
        (atm_in_hbm, atm_in_ref),
        (atm_bias_hbm, atm_bias_ref),
        (atm_out_hbm, atm_out_ref),
        (ocn_in_hbm, ocn_in_v),
        (ocn_bias_hbm, ocn_bias_ref),
        (ocn_out_hbm, ocn_out_v),
    )
    loads = [
        pltpu.make_async_copy(src, dst, load_sem.at[n]) for n, (src, dst) in enumerate(pairs)
    ]
    for load in loads[0:5]:
        load.start()

    @pl.when(ocean)
    def _():
        for load in loads[8:11]:
            load.start()

    @pl.when(air)
    def _():
        for load in loads[5:8]:
            load.start()

    q[...] = jnp.zeros((24, 8, LANES), F32)
    for di, block, rows in ((-1, 0, slice(0, 2)), (1, 2, slice(18, 20))):
        def blank(block=block, rows=rows):
            for s in range(STEPS):
                xr[s, rows] = jnp.zeros((2, CH, LANES), BF)
                sb[s, slice(0, 2) if block == 0 else slice(5, 7)] = jnp.zeros((2, 32, LANES), BF)
                sp_recv[s, block] = jnp.zeros((2, 16, LANES), BF)
                cp_recv[s, block // 2] = jnp.zeros((2, 16, LANES), BF)
            qe_recv[block] = jnp.zeros((2, 8, LANES), F32)

        pl.when(jnp.logical_not(has[di]))(blank)

    barrier = pltpu.get_barrier_semaphore()

    def greet(group, di, dj):
        when(
            has[di],
            lambda: pl.semaphore_signal(
                barrier, inc=1, device_id=place(group, di, dj), device_id_type=MESH
            ),
        )

    for di in (-1, 0, 1):
        for dj in (-1, 0, 1):
            greet(1 - g, di, dj)

    @pl.when(ocean)
    def _():
        for di in (-1, 0, 1):
            for dj in (-1, 0, 1):
                if di or dj:
                    greet(1, di, dj)

    def remote(src, dst, send, recv, target):
        return pltpu.make_async_remote_copy(
            src_ref=src,
            dst_ref=dst,
            send_sem=send,
            recv_sem=recv,
            device_id=target,
            device_id_type=MESH,
        )

    def s_copy(s, wide, di, dj):
        n = 1 - di
        if dj == 0:
            first = 1 if di == 1 else 0
            count = (3 if di == 0 else 2) if wide else (2 if di == 0 else 1)
            source = sm.at[s, pl.ds(first, count)]
            target = sb.at[s, pl.ds({1: 0, 0: 2, -1: 5}[di], count)]
        else:
            source = sp.at[s, 0 if dj == -1 else 1]
            target = sp_recv.at[s, n, 0 if dj == 1 else 1]
        return remote(
            source, target, s_send.at[s, n, dj + 1], s_recv.at[s, n, dj + 1], place(1 - g, di, dj)
        )

    def x_copy(s, di, dj):
        n = 1 - di
        if dj == 0:
            src = xr.at[s, pl.ds(16 if di == 1 else 2, 2)]
            dst = xr.at[s, pl.ds(0 if di == 1 else 18, 2)]
        elif di == 0:
            src = eg.at[s]
            dst = eg_recv.at[s, 0 if dj == 1 else 1]
        else:
            src = cp.at[s]
            dst = cp_recv.at[s, n // 2, 0 if dj == 1 else 1]
        return remote(src, dst, x_send.at[s, n, dj + 1], x_recv.at[s, n, dj + 1], place(1, di, dj))

    def q_copy(di, dj):
        n = 1 - di
        if dj == 0:
            src = q.at[pl.ds(16 if di == 1 else 2, 2)]
            dst = q.at[pl.ds(0 if di == 1 else 18, 2)]
        else:
            src = qe
            dst = qe_recv.at[n, 0 if dj == 1 else 1]
        return remote(src, dst, q_send.at[n, dj + 1], q_recv.at[n, dj + 1], place(1, di, dj))

    around = [(di, dj) for di in (-1, 0, 1) for dj in (-1, 0, 1)]
    ring = [(di, dj) for di, dj in around if di or dj]

    def s_all(action, s, sending):
        @pl.when(air)
        def _():
            action(functools.partial(s_copy, s, sending), around)

        @pl.when(ocean)
        def _():
            action(functools.partial(s_copy, s, not sending), around)

    def start_all(make, pairs):
        for di, dj in pairs:
            when(has[di], lambda di=di, dj=dj: make(di, dj).start())

    def wait_arrivals(make, pairs):
        for di, dj in pairs:
            when(has[-di], lambda di=di, dj=dj: make(di, dj).wait_recv())

    def wait_departures(make, pairs):
        for di, dj in pairs:
            when(has[di], lambda di=di, dj=dj: make(di, dj).wait_send())

    loads[0].wait()
    flip[...] = state_ref[0].astype(F32).reshape(CH * ROWS, LANES)

    def to_rows(r, c):
        xr[0, r + 2] = flip[pl.ds(r, CH, stride=ROWS), :].astype(BF)
        return c

    run(range(ROWS), to_rows)

    loads[1].wait()
    loads[4].wait()
    wet_values = mask_ref[...].astype(F32)
    wet[...] = wet_values
    kept = jnp.where(ocean, wet_values, 1.0)
    keep[...] = kept
    high, middle, rest = thirds(proj_ref[g])
    pp[...] = jnp.concatenate([high, high, middle, middle, rest, rest], 0).astype(BF)

    srow[...] = jnp.zeros((24, 8, LANES), F32)
    def blocks_swapped(tiles):
        tiles = list(tiles)
        block = iota(tiles[0].shape, 1) >> 4
        for s in (4, 2, 1):
            stays = (block & s) == 0
            for a in range(8):
                if not a & s:
                    x, y = tiles[a], tiles[a + s]
                    tiles[a] = jnp.where(stays, x, pltpu.roll(y, 16 * s, 1))
                    tiles[a + s] = jnp.where(stays, pltpu.roll(x, LANES - 16 * s, 1), y)
        return tiles

    def turned(x):
        return pltpu.roll(x, 4, 0)

    def double_low(x):
        return jnp.where(low, x, turned(x))

    def double_high(x):
        return jnp.where(low, turned(x), x)

    def surface(s):
        for m in range(4):
            rows = jnp.concatenate([xr[s, 4 * m + 2 + u] for u in range(4)], 1)
            parts = jnp.dot(pp[...], rows, preferred_element_type=F32)
            fields = parts[0:8] + parts[8:16] + parts[16:24]
            for u in range(4):
                r = 4 * m + u
                kept_row = jnp.broadcast_to(keep[r : r + 1], (8, LANES))
                srow[air_shift + r] = fields[:, 128 * u : 128 * u + 128] * kept_row
        zero = jnp.zeros((8, LANES), F32)
        tiles = blocks_swapped(
            jnp.concatenate(
                [jnp.where(low, srow[k], srow[8 + k]), jnp.where(low, srow[16 + k], zero)], 0
            ).astype(BF)
            for k in range(8)
        )
        sp[s, 0] = tiles[0]
        sp[s, 1] = tiles[7]
        tiles = [tile.astype(F32) for tile in tiles]
        for half in range(2):
            made = [[], [], []]
            for m in range(2):
                even, odd = tiles[4 * half + 2 * m], tiles[4 * half + 2 * m + 1]
                made[0].append(jnp.where(low, even[0:8], turned(odd[0:8])))
                made[1].append(jnp.where(low, turned(even[0:8]), odd[0:8]))
                made[2].append(jnp.where(low, even[8:16], turned(odd[8:16])))
            for band in range(3):
                sm[s, band, 16 * half : 16 * half + 16] = jnp.concatenate(made[band], 0).astype(BF)

    def edge_rows(s):
        def add(t, acc):
            return jnp.where((lane80 >> 2) == t, pltpu.roll(xr[s, t], 4 * t + 2, 1), acc)

        own = jnp.zeros((CH, LANES), BF)
        for t in range(2, 18):
            own = add(t, own)
        eg[s] = own

    def corner_rows(s):
        own = eg[s]
        packed = jnp.zeros((16, LANES), BF)
        for part in range(5):
            tile = pltpu.roll(own[16 * part : 16 * part + 16], 64 + 8 * part, 1)
            place_of = lane16 - 8 * part
            inside = ((place_of >= 0) & (place_of < 8)) | ((place_of >= 72) & (place_of < 80))
            packed = jnp.where(inside, tile, packed)
        cp[s] = packed

    surface(0)

    loads[2].wait()
    loads[3].wait()
    for k in range(4):
        code = (offsets_ref[0, 0, k] + HW) * 32 + (offsets_ref[0, 1, k] + HW)
        flip[16 * k : 16 * k + 16] = code.astype(F32)
        flip[64 + 16 * k : 64 + 16 * k + 16] = weights_ref[0, k]
    for r in range(ROWS):
        q[ocean_shift + r] = flip[pl.ds(r, 8, stride=ROWS), :]

    @pl.when(ocean)
    def _():
        edge_rows(0)
        corner_rows(0)
        eg[1] = jnp.zeros((CH, LANES), BF)

        def add(t, acc):
            return jnp.where((lane8 >> 2) == t, pltpu.roll(q[t], 4 * t + 2, 1), acc)

        own = jnp.zeros((8, LANES), F32)
        for t in range(2, 18):
            own = add(t, own)
        qe[...] = own

    neighbours = 1 + has[-1].astype(I32) + has[1].astype(I32)
    pl.semaphore_wait(barrier, 3 * neighbours + g * (3 * neighbours - 1))

    s_all(start_all, 0, True)

    @pl.when(ocean)
    def _():
        start_all(q_copy, ring)
        start_all(functools.partial(x_copy, 0), ring)

    @pl.when(ocean)
    def _():
        for load in loads[8:11]:
            load.wait()

        def rows_of(values):
            return thirds(values.reshape(1, -1))

        spare = jnp.zeros((1, HO), F32)
        bias = jnp.concatenate([*rows_of(ocn_bias_ref[...]), spare], 0)
        for a in range(3):
            taps = [ocn_in_v[3 * a + b].astype(F32) for b in range(3)]
            last = bias if a == 1 else jnp.zeros((4, HO), F32)
            stacked = jnp.concatenate(
                [tap[0:CH] for tap in taps] + [tap[CH:] for tap in taps] + [last], 0
            )
            stacked = jnp.concatenate([stacked, jnp.zeros((256, 256 - HO), F32)], 1)
            w1[a] = stacked.T[0:HOP].astype(BF)
            for b in range(3):
                values = ocn_out_v[3 * a + b].astype(F32)
                w2[a, CH * b : CH * b + CH, :] = jnp.concatenate(
                    [values, jnp.zeros((CH, HOP - HO), F32)], 1
                ).astype(BF)

    @pl.when(air)
    def _():
        for load in loads[5:8]:
            load.wait()
        bias = thirds(atm_bias_ref[...].reshape(1, -1))
        stacked = jnp.concatenate(
            [atm_in_ref[...].astype(F32), *bias, jnp.zeros((41, 384), F32)], 0
        )
        wa[...] = stacked.T[:, 0:96].astype(BF)

    def spread(values, base):
        first = jnp.broadcast_to(values[base : base + 1], (8, LANES))
        second = jnp.broadcast_to(values[base + 1 : base + 2], (8, LANES))
        return jnp.where(low, first, second)

    def decode_band(band):
        tiles = blocks_swapped(q[8 * band + k] for k in range(8))
        for patch in range(8):
            for kp in range(2):
                code = spread(tiles[patch], 2 * kp).astype(I32)
                down = (lane8 >> 4) + (code >> 5)
                across = inner8 + (code & 31)
                beside = jnp.where((across >= 8) & (across < 24), 0, 1)
                gi[8 * band + patch, kp] = (
                    ((down & 7) * 16 + ((across + 8) & 15)) + ((down >> 3) * 2 + beside) * LANES
                )
                gw[8 * band + patch, kp] = spread(tiles[patch], 4 + 2 * kp)

    @pl.when(air)
    def _():
        decode_band(0)
        decode_band(1)

    @pl.when(ocean)
    def _():
        decode_band(1)
        wait_arrivals(q_copy, ring)
        decode_band(0)
        decode_band(2)
        pos = lane8 & 3
        beside = [jnp.where(pos < 2, qe_recv[n, 0], qe_recv[n, 1]) for n in range(3)]
        ends = jnp.where(
            lane8 < 64, pltpu.roll(beside[0], 64, 1), pltpu.roll(beside[2], 64, 1)
        )
        values = jnp.where((lane8 >= 8) & (lane8 < 72), beside[1], ends)
        for kp in range(2):
            code = spread(values, 2 * kp).astype(I32)
            down = (lane8 >> 2) + (code >> 5)
            across = jnp.where(pos < 2, pos - 2, pos + 126) + (code & 31) - HW
            outer = jnp.where((across >= 0) & (across < LANES), 0, 1)
            gi[24, kp] = ((down & 7) * 16 + (across & 15)) + ((down >> 3) * 2 + outer) * LANES
            gw[24, kp] = spread(values, 4 + 2 * kp)

    def put_band(s, row, pick):
        for quarter in range(2):
            tile = pick(slice(16 * quarter, 16 * quarter + 16))
            for m in range(2):
                values = tile[8 * m : 8 * m + 8]
                src[row, 4 * quarter + 2 * m + 1] = double_low(values)
                src[row, 4 * quarter + 2 * m + 2] = double_high(values)

    def sources(s):
        def band(k):
            return lambda rows: sb[s, k, rows].astype(F32)

        def joined(k):
            return lambda rows: jnp.where(
                lane16 < 32, sb[s, k, rows].astype(F32), sb[s, k + 1, rows].astype(F32)
            )

        sides = [[sp_recv[s, n, side].astype(F32) for side in range(2)] for n in range(3)]

        @pl.when(air)
        def _():
            for row, k in enumerate((0, 2, 3, 5)):
                put_band(s, row, band(k))
            for side in range(2):
                north, center, south = (sides[n][side] for n in range(3))
                column = 9 * side
                src[0, column] = double_high(north[0:8])
                src[1, column] = double_low(center[0:8])
                src[2, column] = double_high(center[0:8])
                src[3, column] = double_low(south[0:8])

        @pl.when(ocean)
        def _():
            for row, pick in enumerate((band(0), joined(1), band(3), joined(4), band(6))):
                put_band(s, row, pick)
            first = lane8 < 32
            for side in range(2):
                north, center, south = (sides[n][side] for n in range(3))
                column = 9 * side
                src[0, column] = double_high(north[0:8])
                src[1, column] = jnp.where(first, double_low(north[8:16]), double_low(center[0:8]))
                src[2, column] = double_high(center[0:8])
                src[3, column] = jnp.where(first, double_low(center[8:16]), double_low(south[0:8]))
                src[4, column] = double_high(south[0:8])

    def take(values, index):
        return jnp.take_along_axis(values, index, axis=1, mode="promise_in_bounds")

    def combine(n, picked):
        total = picked[0] * gw[n, 0] + picked[1] * gw[n, 1]
        return total + turned(total)

    def regrid_patch(n, c):
        band = n >> 3
        patch = n & 7
        picked = []
        here = [src[band + d, patch + 1] for d in range(3)]
        there = [
            jnp.where(inner8 < 8, src[band + d, patch + 2], src[band + d, patch]) for d in range(3)
        ]
        for kp in range(2):
            index = gi[n, kp] & (LANES - 1)
            which = gi[n, kp] >> 7
            value = jnp.zeros((8, LANES), F32)
            for d in range(3):
                value = jnp.where(which == 2 * d, take(here[d], index), value)
                value = jnp.where(which == 2 * d + 1, take(there[d], index), value)
            picked.append(value)
        fp[n] = combine(n, picked)
        return c

    def regrid_edges():
        picked = []
        left = (lane8 & 3) < 2
        for kp in range(2):
            index = gi[24, kp] & (LANES - 1)
            which = gi[24, kp] >> 7
            value = jnp.zeros((8, LANES), F32)
            for d in range(5):
                inner = take(jnp.where(inner8 < 8, src[d, 1], src[d, 8]), index)
                outer = jnp.where(left, take(src[d, 0], index), take(src[d, 9], index))
                value = jnp.where(which == 2 * d, inner, value)
                value = jnp.where(which == 2 * d + 1, outer, value)
            picked.append(value)
        fp[24] = combine(24, picked)

    def forcing_rows(bands):
        zero = jnp.zeros((8, LANES), F32)
        tiles = blocks_swapped(
            jnp.concatenate(
                [
                    jnp.where(low, fp[k], fp[8 + k]),
                    jnp.where(low, fp[16 + k], zero) if bands == 3 else zero,
                ],
                0,
            ).astype(BF)
            for k in range(8)
        )
        for k in range(8):
            tile = tiles[k].astype(F32)
            fr[k] = double_low(tile[0:8])
            fr[8 + k] = double_high(tile[0:8])
            if bands == 3 and k < 4:
                fr[16 + k] = double_low(tile[8:16])

    def finish_row(s, r, values):
        if s + 1 < STEPS:
            xr[s + 1, r + 2] = values.astype(BF)
        else:
            flip[pl.ds(r, CH, stride=ROWS), :] = values

    def air_step(s):
        run(range(16), regrid_patch)
        forcing_rows(2)
        ones = jnp.where(sub8 < 7, 1.0, 0.0)
        blank = jnp.zeros((8, LANES), F32)

        def pair(p, c):
            t = 2 * p + 2
            columns = []
            for u in range(2):
                tail = jnp.concatenate([jnp.where(low, fr[t + u - 2], ones), blank], 0).astype(BF)
                columns.append(jnp.concatenate([xr[s, t + u], tail], 0))
            hidden = gelu(
                jnp.dot(wa[...], jnp.concatenate(columns, 1), preferred_element_type=F32)
            ).astype(BF)
            update = jnp.dot(atm_out_ref[...], hidden, preferred_element_type=F32)
            for u in range(2):
                new = xr[s, t + u].astype(F32) + update[:, 128 * u : 128 * u + 128]
                finish_row(s, 2 * p + u, new)
            return c

        run(range(ROWS // 2), pair)

    def ocean_step(s):
        run(range(24), regrid_patch)
        regrid_edges()
        forcing_rows(3)
        wait_arrivals(functools.partial(x_copy, s), ring)

        pos = lane80 & 3
        pos8 = lane8 & 3
        own = eg[s]
        for t in (0, 1, 18, 19):
            own = jnp.where((lane80 >> 2) == t, pltpu.roll(xr[s, t], 4 * t + 2, 1), own)
        beside = jnp.where(pos < 2, eg_recv[s, 0], eg_recv[s, 1])
        pos16 = lane16 & 3
        corners = [jnp.where(pos16 < 2, cp_recv[s, n, 0], cp_recv[s, n, 1]) for n in range(2)]
        corner = jnp.where(lane16 < 64, corners[0], corners[1])
        corner = jnp.concatenate(
            [pltpu.roll(corner, LANES - 8 * part, 1) if part else corner for part in range(5)], 0
        )
        beside = jnp.where((lane80 >= 8) & (lane80 < 72), beside, corner)

        def taps(halo, mine, where):
            return (
                pltpu.roll(jnp.where(where == 0, halo, mine), 1, 1),
                halo,
                pltpu.roll(jnp.where(where == 2, mine, halo), LANES - 1, 1),
            )

        def swapped(halo, where):
            return jnp.where(where == 1, pltpu.roll(halo, LANES - 1, 1), pltpu.roll(halo, 1, 1))

        state_taps = taps(beside, own, pos)
        for b in range(3):
            x3e[CH * b : CH * b + CH] = state_taps[b]
        hh[...] = swapped(beside, pos)

        def add(t, acc):
            return jnp.where((lane8 >> 2) == t, pltpu.roll(fr[t], 4 * t + 2, 1), acc)

        own_forcing = jnp.zeros((8, LANES), F32)
        for t in range(TALL):
            own_forcing = add(t, own_forcing)
        beside_forcing = fp[24]
        first, second, third = taps(beside_forcing, own_forcing, pos8)
        ones = jnp.where(sub8 < 7, 1.0, 0.0)
        x3e[240:256] = jnp.concatenate(
            [jnp.where(low, first, second), jnp.where(low, third, ones)], 0
        ).astype(BF)
        swapped_forcing = swapped(beside_forcing, pos8)

        def widen(t, c):
            forcing = fr[t]
            halo = pltpu.roll(swapped_forcing, 126 - 4 * t, 1)
            left = jnp.where(lane8 == 0, halo, pltpu.roll(forcing, 1, 1))
            right = jnp.where(lane8 == LANES - 1, halo, pltpu.roll(forcing, LANES - 1, 1))
            x3[t, 240:256] = jnp.concatenate(
                [jnp.where(low, left, forcing), jnp.where(low, right, ones)], 0
            ).astype(BF)
            cells = xr[s, t]
            halo = pltpu.roll(hh[...], 126 - 4 * t, 1)
            x3[t, 0:80] = jnp.where(lane80 == 0, halo, pltpu.roll(cells, 1, 1))
            x3[t, 80:160] = cells
            x3[t, 160:240] = jnp.where(
                lane80 == LANES - 1, halo, pltpu.roll(cells, LANES - 1, 1)
            )

        run(range(TALL), widen)

        def first_conv(p, c):
            h = 2 * p
            total = jnp.zeros((HOP, 256), F32)
            for a in range(3):
                columns = jnp.concatenate([x3[h + a], x3[h + a + 1]], 1)
                total = total + jnp.dot(w1[a], columns, preferred_element_type=F32)
            active = gelu(total).astype(BF)
            hid[h] = active[:, 0:128]
            hid[h + 1] = active[:, 128:256]
            return c

        run(range(9), first_conv)

        @pl.when(i == 0)
        def _():
            hid[0] = jnp.zeros((HOP, LANES), BF)

        @pl.when(i == lats - 1)
        def _():
            hid[17] = jnp.zeros((HOP, LANES), BF)

        total = jnp.zeros((HOP, LANES), F32)
        for a in range(3):
            columns = x3e[...]
            if a:
                columns = pltpu.roll(columns, LANES - 4 * a, 1)
            total = total + jnp.dot(w1[a], columns, preferred_element_type=F32)
        slot = iota((HOP, LANES), 1) >> 2
        outside = ((slot == 0) & (i == 0)) | ((slot == 17) & (i == lats - 1))
        he[...] = jnp.where(outside, 0.0, gelu(total)).astype(BF)
        total = jnp.zeros((240, LANES), F32)
        for a in range(3):
            columns = he[...]
            if a:
                columns = pltpu.roll(columns, LANES - 4 * a, 1)
            total = total + jnp.dot(w2[a], columns, preferred_element_type=F32)
        ze[...] = jnp.where(
            pos == 1,
            pltpu.roll(total[160:240], LANES - 1, 1),
            pltpu.roll(total[0:80], 1, 1),
        )

        def second_conv(p, c):
            r = 2 * p
            total = jnp.zeros((240, 256), F32)
            for a in range(3):
                columns = jnp.concatenate([hid[r + a], hid[r + a + 1]], 1)
                total = total + jnp.dot(w2[a], columns, preferred_element_type=F32)
            for u in range(2):
                part = total[:, 128 * u : 128 * u + 128]
                halo = pltpu.roll(ze[...], 126 - 4 * (r + u), 1)
                left = jnp.where(lane80 == 0, halo, pltpu.roll(part[0:80], 1, 1))
                right = jnp.where(
                    lane80 == LANES - 1, halo, pltpu.roll(part[160:240], LANES - 1, 1)
                )
                update = left + part[80:160] + right
                new = xr[s, r + u + 2].astype(F32) + wet[r + u : r + u + 1] * update
                finish_row(s, r + u, new)
                if s + 1 < STEPS:
                    t = r + u + 2
                    eg[s + 1] = jnp.where(
                        (lane80 >> 2) == t, pltpu.roll(new.astype(BF), 4 * t + 2, 1), eg[s + 1]
                    )
            return c

        run((0, 7), second_conv)
        if s + 1 < STEPS:
            start_all(functools.partial(x_copy, s + 1), [(-1, 0), (1, 0)])
        run(range(1, 7), second_conv)
        if s + 1 < STEPS:
            corner_rows(s + 1)
            start_all(
                functools.partial(x_copy, s + 1), [(di, dj) for di, dj in ring if dj]
            )

    for s in range(STEPS):
        if s:
            surface(s)
            s_all(start_all, s, True)

        s_all(wait_arrivals, s, False)
        sources(s)

        @pl.when(ocean)
        def _(s=s):
            ocean_step(s)

        @pl.when(air)
        def _(s=s):
            air_step(s)

    out_ref[0] = flip[...].reshape(CH, ROWS, LANES).astype(BF)

    for s in range(STEPS):
        s_all(wait_departures, s, True)

    @pl.when(ocean)
    def _():
        for s in range(STEPS):
            wait_departures(functools.partial(x_copy, s), ring)
        wait_departures(q_copy, ring)


def solution(mesh):
    lats, lons = mesh.shape["lat"], mesh.shape["lon"]
    vmem = pl.BlockSpec(memory_space=pltpu.VMEM)
    anywhere = pl.BlockSpec(memory_space=pl.ANY)
    dma = pltpu.SemaphoreType.DMA

    def local(*args):
        args = list(args)
        args[5] = args[5].T
        args[8] = args[8].transpose(1, 2, 0)
        args[10] = args[10].transpose(1, 0, 2)
        return pl.pallas_call(
            functools.partial(kernel, lats, lons),
            out_shape=jax.ShapeDtypeStruct((1, CH, ROWS, LANES), BF),
            in_specs=[anywhere] * 11,
            out_specs=vmem,
            scratch_shapes=[
                pltpu.VMEM((1, CH, ROWS, LANES), BF),
                pltpu.VMEM((ROWS, LANES), I32),
                pltpu.VMEM((1, 2, 4, ROWS, LANES), I32),
                pltpu.VMEM((1, 4, ROWS, LANES), F32),
                pltpu.VMEM((2, 4, CH), F32),
                pltpu.VMEM((84, 384), BF),
                pltpu.VMEM((384,), F32),
                pltpu.VMEM((CH, 384), BF),
                pltpu.VMEM((9, 84, HO), BF),
                pltpu.VMEM((HO,), F32),
                pltpu.VMEM((9, CH, HO), BF),
                pltpu.VMEM((CH * ROWS, LANES), F32),
                pltpu.VMEM((STEPS, TALL, CH, LANES), BF),
                pltpu.VMEM((STEPS, CH, LANES), BF),
                pltpu.VMEM((STEPS, 2, CH, LANES), BF),
                pltpu.VMEM((STEPS, 16, LANES), BF),
                pltpu.VMEM((STEPS, 2, 2, 16, LANES), BF),
                pltpu.VMEM((24, 8, LANES), F32),
                pltpu.VMEM((STEPS, 3, 32, LANES), BF),
                pltpu.VMEM((STEPS, 7, 32, LANES), BF),
                pltpu.VMEM((STEPS, 2, 16, LANES), BF),
                pltpu.VMEM((STEPS, 3, 2, 16, LANES), BF),
                pltpu.VMEM((24, 8, LANES), F32),
                pltpu.VMEM((8, LANES), F32),
                pltpu.VMEM((3, 2, 8, LANES), F32),
                pltpu.VMEM((25, 2, 8, LANES), I32),
                pltpu.VMEM((25, 2, 8, LANES), F32),
                pltpu.VMEM((5, 10, 8, LANES), F32),
                pltpu.VMEM((25, 8, LANES), F32),
                pltpu.VMEM((24, 8, LANES), F32),
                pltpu.VMEM((TALL, 256, LANES), BF),
                pltpu.VMEM((256, LANES), BF),
                pltpu.VMEM((3, HOP, 256), BF),
                pltpu.VMEM((3, 240, HOP), BF),
                pltpu.VMEM((384, 96), BF),
                pltpu.VMEM((18, HOP, LANES), BF),
                pltpu.VMEM((HOP, LANES), BF),
                pltpu.VMEM((CH, LANES), BF),
                pltpu.VMEM((CH, LANES), F32),
                pltpu.VMEM((ROWS, LANES), F32),
                pltpu.VMEM((ROWS, LANES), F32),
                pltpu.VMEM((24, CH), BF),
                dma((11,)),
                dma((STEPS, 3, 3)),
                dma((STEPS, 3, 3)),
                dma((STEPS, 3, 3)),
                dma((STEPS, 3, 3)),
                dma((3, 3)),
                dma((3, 3)),
            ],
            compiler_params=pltpu.CompilerParams(
                collective_id=0,
                has_side_effects=True,
                vmem_limit_bytes=60 * 1024 * 1024,
            ),
        )(*args)

    return jax.shard_map(
        local,
        mesh=mesh,
        in_specs=(
            P("grp", None, "lat", "lon"),
            P("lat", "lon"),
            P("grp", None, None, "lat", "lon"),
            P("grp", None, "lat", "lon"),
            P(),
            P(),
            P(),
            P(),
            P(),
            P(),
            P(),
        ),
        out_specs=P("grp", None, "lat", "lon"),
        check_vma=False,
    )
```

```python
import functools

import jax
import jax.numpy as jnp
from jax import lax
from jax.experimental import pallas as pl
from jax.experimental.pallas import tpu as pltpu
from jax.sharding import PartitionSpec as P

BF = jnp.bfloat16
F32 = jnp.float32
I32 = jnp.int32
MESH = pl.DeviceIdType.MESH

STEPS = 2
HW = 8
CH = 80
HO = 200
HOP = 208
ROWS = 16
LANES = 128
TALL = ROWS + 4
AIR_ROWS = 16
SURFACE_ROWS = 4


def iota(shape, axis):
    return lax.broadcasted_iota(I32, shape, axis)


def gelu_of_twice(half):
    inner = half * (1.5957691216057308 + 0.285419265090401 * (half * half))
    return half + half * jnp.tanh(inner)


def thirds(x):
    high = x.astype(BF).astype(F32)
    middle = (x - high).astype(BF).astype(F32)
    return high, middle, x - high - middle


def kernel(
    lats,
    lons,
    state_hbm,
    mask_hbm,
    offsets_hbm,
    weights_hbm,
    proj_hbm,
    atm_in_hbm,
    atm_bias_hbm,
    atm_out_hbm,
    ocn_in_hbm,
    ocn_bias_hbm,
    ocn_out_hbm,
    out_ref,
    state_ref,
    mask_ref,
    offsets_ref,
    weights_ref,
    proj_ref,
    atm_in_ref,
    atm_bias_ref,
    atm_out_ref,
    ocn_in_v,
    ocn_bias_ref,
    ocn_out_v,
    flip,
    final,
    xr,
    eg,
    eg_recv,
    cp,
    cp_recv,
    srow,
    sm,
    sb,
    sp,
    sp_recv,
    q,
    qe,
    qe_recv,
    gi,
    gw,
    src,
    part,
    fp,
    fr,
    x3,
    x3e,
    w1,
    w2,
    wa,
    hid,
    he,
    hh,
    ze,
    keep,
    wet,
    pp,
    load_sem,
    s_send,
    s_recv,
    x_send,
    x_recv,
    q_send,
    q_recv,
):
    g = lax.axis_index("grp")
    i = lax.axis_index("lat")
    j = lax.axis_index("lon")
    ocean = g == 1
    air = g == 0
    has = {-1: i > 0, 0: None, 1: i < lats - 1}

    def run(steps, body):
        for step in steps:
            body(step, 0)

    def place(group, di, dj):
        return (group, i + di, lax.rem(j + dj + lons, lons))

    def when(condition, action):
        if condition is None:
            action()
        else:
            pl.when(condition)(action)

    lane8 = iota((8, LANES), 1)
    sub8 = iota((8, LANES), 0)
    low = sub8 < 4
    lane80 = iota((CH, LANES), 1)
    lane16 = iota((16, LANES), 1)
    inner8 = lane8 & 15
    air_shift = jnp.where(air, 2, 0)
    ocean_shift = jnp.where(ocean, 2, 0)

    pairs = (
        (state_hbm, state_ref),
        (mask_hbm, mask_ref),
        (offsets_hbm, offsets_ref),
        (weights_hbm, weights_ref),
        (proj_hbm, proj_ref),
        (atm_in_hbm, atm_in_ref),
        (atm_bias_hbm, atm_bias_ref),
        (atm_out_hbm, atm_out_ref),
        (ocn_in_hbm, ocn_in_v),
        (ocn_bias_hbm, ocn_bias_ref),
        (ocn_out_hbm, ocn_out_v),
    )
    loads = [
        pltpu.make_async_copy(src, dst, load_sem.at[n]) for n, (src, dst) in enumerate(pairs)
    ]
    for load in loads[0:5]:
        load.start()

    @pl.when(ocean)
    def _():
        for load in loads[8:11]:
            load.start()

    @pl.when(air)
    def _():
        for load in loads[5:8]:
            load.start()

    q[...] = jnp.zeros((24, 8, LANES), F32)
    for di, block, rows in ((-1, 0, slice(0, 2)), (1, 2, slice(18, 20))):
        def blank(block=block, rows=rows):
            for s in range(STEPS):
                xr[s, rows] = jnp.zeros((2, CH, LANES), BF)
                sb[s, slice(0, 2) if block == 0 else slice(5, 7)] = jnp.zeros((2, 32, LANES), BF)
                sp_recv[s, block] = jnp.zeros((2, 16, LANES), BF)
                cp_recv[s, block // 2] = jnp.zeros((2, 16, LANES), BF)
            qe_recv[block] = jnp.zeros((2, 8, LANES), F32)

        pl.when(jnp.logical_not(has[di]))(blank)

    barrier = pltpu.get_barrier_semaphore()

    def greet(group, di, dj):
        when(
            has[di],
            lambda: pl.semaphore_signal(
                barrier, inc=1, device_id=place(group, di, dj), device_id_type=MESH
            ),
        )

    for di in (-1, 0, 1):
        for dj in (-1, 0, 1):
            greet(1 - g, di, dj)

    @pl.when(ocean)
    def _():
        for di in (-1, 0, 1):
            for dj in (-1, 0, 1):
                if di or dj:
                    greet(1, di, dj)

    def remote(src, dst, send, recv, target):
        return pltpu.make_async_remote_copy(
            src_ref=src,
            dst_ref=dst,
            send_sem=send,
            recv_sem=recv,
            device_id=target,
            device_id_type=MESH,
        )

    def s_copy(s, wide, di, dj):
        n = 1 - di
        if dj == 0:
            first = 1 if di == 1 else 0
            count = (3 if di == 0 else 2) if wide else (2 if di == 0 else 1)
            source = sm.at[s, pl.ds(first, count)]
            target = sb.at[s, pl.ds({1: 0, 0: 2, -1: 5}[di], count)]
        else:
            source = sp.at[s, 0 if dj == -1 else 1]
            target = sp_recv.at[s, n, 0 if dj == 1 else 1]
        return remote(
            source, target, s_send.at[s, n, dj + 1], s_recv.at[s, n, dj + 1], place(1 - g, di, dj)
        )

    def x_copy(s, di, dj):
        n = 1 - di
        if dj == 0:
            src = xr.at[s, pl.ds(16 if di == 1 else 2, 2)]
            dst = xr.at[s, pl.ds(0 if di == 1 else 18, 2)]
        elif di == 0:
            src = eg.at[s]
            dst = eg_recv.at[s, 0 if dj == 1 else 1]
        else:
            src = cp.at[s]
            dst = cp_recv.at[s, n // 2, 0 if dj == 1 else 1]
        return remote(src, dst, x_send.at[s, n, dj + 1], x_recv.at[s, n, dj + 1], place(1, di, dj))

    def q_copy(di, dj):
        n = 1 - di
        if dj == 0:
            src = q.at[pl.ds(16 if di == 1 else 2, 2)]
            dst = q.at[pl.ds(0 if di == 1 else 18, 2)]
        else:
            src = qe
            dst = qe_recv.at[n, 0 if dj == 1 else 1]
        return remote(src, dst, q_send.at[n, dj + 1], q_recv.at[n, dj + 1], place(1, di, dj))

    around = [(di, dj) for di in (-1, 1, 0) for dj in (-1, 1, 0)]
    ring = [(di, dj) for di, dj in around if di or dj]

    def s_all(action, s, sending):
        @pl.when(air)
        def _():
            action(functools.partial(s_copy, s, sending), around)

        @pl.when(ocean)
        def _():
            action(functools.partial(s_copy, s, not sending), around)

    def start_all(make, pairs):
        for di, dj in pairs:
            when(has[di], lambda di=di, dj=dj: make(di, dj).start())

    def wait_arrivals(make, pairs):
        for di, dj in pairs:
            when(has[-di], lambda di=di, dj=dj: make(di, dj).wait_recv())

    def wait_departures(make, pairs):
        for di, dj in pairs:
            when(has[di], lambda di=di, dj=dj: make(di, dj).wait_send())

    loads[0].wait()
    xr[0, 2:18] = jnp.transpose(state_ref[0], (1, 0, 2))

    loads[1].wait()
    loads[4].wait()
    wet_values = mask_ref[...].astype(F32)
    wet[...] = wet_values
    kept = jnp.where(ocean, wet_values, 1.0)
    keep[...] = kept
    high, middle, rest = thirds(proj_ref[g])
    pp[...] = jnp.concatenate([high, high, middle, middle, rest, rest], 0).astype(BF)

    srow[...] = jnp.zeros((24, 8, LANES), F32)
    def blocks_swapped(tiles):
        tiles = list(tiles)
        block = iota(tiles[0].shape, 1) >> 4
        for s in (4, 2, 1):
            stays = (block & s) == 0
            for a in range(8):
                if not a & s:
                    x, y = tiles[a], tiles[a + s]
                    tiles[a] = jnp.where(stays, x, pltpu.roll(y, 16 * s, 1))
                    tiles[a + s] = jnp.where(stays, pltpu.roll(x, LANES - 16 * s, 1), y)
        return tiles

    def turned(x):
        return pltpu.roll(x, 4, 0)

    def double_low(x):
        return jnp.where(low, x, turned(x))

    def double_high(x):
        return jnp.where(low, turned(x), x)

    def fill(t, cells):
        x3[t, 0:80] = pltpu.roll(cells, 1, 1)
        x3[t, 80:160] = cells
        x3[t, 160:240] = pltpu.roll(cells, LANES - 1, 1)

    def surface_rows(first, rows):
        parts = jnp.dot(pp[...], jnp.concatenate(rows, 1), preferred_element_type=F32)
        fields = parts[0:8] + parts[8:16] + parts[16:24]
        for u in range(len(rows)):
            kept_row = jnp.broadcast_to(keep[first + u : first + u + 1], (8, LANES))
            srow[air_shift + first + u] = fields[:, 128 * u : 128 * u + 128] * kept_row

    def surface(s):
        for m in range(0, ROWS, SURFACE_ROWS):
            surface_rows(m, [xr[s, m + 2 + u] for u in range(SURFACE_ROWS)])
        zero = jnp.zeros((8, LANES), F32)
        tiles = blocks_swapped(
            jnp.concatenate(
                [jnp.where(low, srow[k], srow[8 + k]), jnp.where(low, srow[16 + k], zero)], 0
            ).astype(BF)
            for k in range(8)
        )
        sp[s, 0] = tiles[0]
        sp[s, 1] = tiles[7]
        tiles = [tile.astype(F32) for tile in tiles]
        for half in range(2):
            made = [[], [], []]
            for m in range(2):
                even, odd = tiles[4 * half + 2 * m], tiles[4 * half + 2 * m + 1]
                made[0].append(jnp.where(low, even[0:8], turned(odd[0:8])))
                made[1].append(jnp.where(low, turned(even[0:8]), odd[0:8]))
                made[2].append(jnp.where(low, even[8:16], turned(odd[8:16])))
            for band in range(3):
                sm[s, band, 16 * half : 16 * half + 16] = jnp.concatenate(made[band], 0).astype(BF)

    def edge_rows(s):
        def add(t, acc):
            return jnp.where((lane80 >> 2) == t, pltpu.roll(xr[s, t], 4 * t + 2, 1), acc)

        own = jnp.zeros((CH, LANES), BF)
        for t in range(2, 18):
            own = add(t, own)
        eg[s] = own

    def corner_rows(s):
        own = eg[s]
        packed = jnp.zeros((16, LANES), BF)
        for part in range(5):
            tile = pltpu.roll(own[16 * part : 16 * part + 16], 64 + 8 * part, 1)
            place_of = lane16 - 8 * part
            inside = ((place_of >= 0) & (place_of < 8)) | ((place_of >= 72) & (place_of < 80))
            packed = jnp.where(inside, tile, packed)
        cp[s] = packed

    surface(0)

    loads[2].wait()
    loads[3].wait()
    for k in range(4):
        code = (offsets_ref[0, 0, k] + HW) * 32 + (offsets_ref[0, 1, k] + HW)
        flip[16 * k : 16 * k + 16] = code.astype(F32)
        flip[64 + 16 * k : 64 + 16 * k + 16] = weights_ref[0, k]
    for r in range(ROWS):
        q[ocean_shift + r] = flip[pl.ds(r, 8, stride=ROWS), :]

    @pl.when(ocean)
    def _():
        edge_rows(0)
        corner_rows(0)
        eg[1] = jnp.zeros((CH, LANES), BF)

        def add(t, acc):
            return jnp.where((lane8 >> 2) == t, pltpu.roll(q[t], 4 * t + 2, 1), acc)

        own = jnp.zeros((8, LANES), F32)
        for t in range(2, 18):
            own = add(t, own)
        qe[...] = own

    neighbours = 1 + has[-1].astype(I32) + has[1].astype(I32)
    pl.semaphore_wait(barrier, 3 * neighbours + g * (3 * neighbours - 1))

    s_all(start_all, 0, True)

    @pl.when(ocean)
    def _():
        start_all(q_copy, ring)
        start_all(functools.partial(x_copy, 0), ring)
        for t in range(2, 18):
            fill(t, xr[0, t])

    @pl.when(ocean)
    def _():
        for load in loads[8:11]:
            load.wait()

        def rows_of(values):
            return thirds(0.5 * values.reshape(1, -1))

        spare = jnp.zeros((1, HO), F32)
        bias = jnp.concatenate([*rows_of(ocn_bias_ref[...]), spare], 0)
        for a in range(3):
            taps = [0.5 * ocn_in_v[3 * a + b].astype(F32) for b in range(3)]
            last = bias if a == 1 else jnp.zeros((4, HO), F32)
            stacked = jnp.concatenate(
                [tap[0:CH] for tap in taps] + [tap[CH:] for tap in taps] + [last], 0
            )
            stacked = jnp.concatenate([stacked, jnp.zeros((256, 256 - HO), F32)], 1)
            w1[a] = stacked.T[0:HOP].astype(BF)
            for b in range(3):
                values = ocn_out_v[3 * a + b].astype(F32)
                w2[a, CH * b : CH * b + CH, :] = jnp.concatenate(
                    [values, jnp.zeros((CH, HOP - HO), F32)], 1
                ).astype(BF)

    @pl.when(air)
    def _():
        for load in loads[5:8]:
            load.wait()
        bias = thirds(0.5 * atm_bias_ref[...].reshape(1, -1))
        stacked = jnp.concatenate(
            [0.5 * atm_in_ref[...].astype(F32), *bias, jnp.zeros((41, 384), F32)], 0
        )
        wa[...] = stacked.T[:, 0:96].astype(BF)

    def spread(values, base):
        first = jnp.broadcast_to(values[base : base + 1], (8, LANES))
        second = jnp.broadcast_to(values[base + 1 : base + 2], (8, LANES))
        return jnp.where(low, first, second)

    def decode_band(band):
        tiles = blocks_swapped(q[8 * band + k] for k in range(8))
        for patch in range(8):
            for kp in range(2):
                code = spread(tiles[patch], 2 * kp).astype(I32)
                down = (lane8 >> 4) + (code >> 5)
                across = inner8 + (code & 31)
                beside = jnp.where((across >= 8) & (across < 24), 0, 1)
                gi[8 * band + patch, kp] = (
                    ((down & 7) * 16 + ((across + 8) & 15)) + ((down >> 3) * 2 + beside) * LANES
                )
                gw[8 * band + patch, kp] = spread(tiles[patch], 4 + 2 * kp)

    @pl.when(air)
    def _():
        decode_band(0)
        decode_band(1)

    @pl.when(ocean)
    def _():
        decode_band(1)
        wait_arrivals(q_copy, ring)
        decode_band(0)
        decode_band(2)
        pos = lane8 & 3
        beside = [jnp.where(pos < 2, qe_recv[n, 0], qe_recv[n, 1]) for n in range(3)]
        ends = jnp.where(
            lane8 < 64, pltpu.roll(beside[0], 64, 1), pltpu.roll(beside[2], 64, 1)
        )
        values = jnp.where((lane8 >= 8) & (lane8 < 72), beside[1], ends)
        for kp in range(2):
            code = spread(values, 2 * kp).astype(I32)
            down = (lane8 >> 2) + (code >> 5)
            across = jnp.where(pos < 2, pos - 2, pos + 126) + (code & 31) - HW
            outer = jnp.where((across >= 0) & (across < LANES), 0, 1)
            gi[24, kp] = ((down & 7) * 16 + (across & 15)) + ((down >> 3) * 2 + outer) * LANES
            gw[24, kp] = spread(values, 4 + 2 * kp)

    def take(values, index):
        return jnp.take_along_axis(values, index, axis=1, mode="promise_in_bounds")

    def combine(n, picked):
        total = picked[0] * gw[n, 0] + picked[1] * gw[n, 1]
        return total + turned(total)

    def gather(n, kp, value, steps):
        band, patch = n >> 3, n & 7
        index = gi[n, kp] & (LANES - 1)
        which = gi[n, kp] >> 7
        for d in steps:
            there = jnp.where(inner8 < 8, src[band + d, patch + 2], src[band + d, patch])
            value = jnp.where(which == 2 * d, take(src[band + d, patch + 1], index), value)
            value = jnp.where(which == 2 * d + 1, take(there, index), value)
        return value

    def put_band(s, row, pick):
        for quarter in range(2):
            tile = pick(slice(16 * quarter, 16 * quarter + 16))
            for m in range(2):
                values = tile[8 * m : 8 * m + 8]
                src[row, 4 * quarter + 2 * m + 1] = double_low(values)
                src[row, 4 * quarter + 2 * m + 2] = double_high(values)

    def sources(s):
        def band(k):
            return lambda rows: sb[s, k, rows].astype(F32)

        def joined(k):
            return lambda rows: jnp.where(
                lane16 < 32, sb[s, k, rows].astype(F32), sb[s, k + 1, rows].astype(F32)
            )

        @pl.when(air)
        def _():
            middle = [(0, dj) for dj in (-1, 1, 0)]
            wait_arrivals(functools.partial(s_copy, s, False), middle)
            sides = [[sp_recv[s, 1, side].astype(F32) for side in range(2)]]
            for row, k in ((1, 2), (2, 3)):
                put_band(s, row, band(k))
            for side in range(2):
                src[1, 9 * side] = double_low(sides[0][side][0:8])
                src[2, 9 * side] = double_high(sides[0][side][0:8])
            blank = jnp.zeros((8, LANES), F32)
            for n in range(16):
                for kp in range(2):
                    part[n, kp] = gather(n, kp, blank, (1, 2) if n < 8 else (0, 1))
            beyond = [(di, dj) for di, dj in around if di]
            wait_arrivals(functools.partial(s_copy, s, False), beyond)
            for row, k, n, double in ((0, 0, 0, double_high), (3, 5, 2, double_low)):
                put_band(s, row, band(k))
                for side in range(2):
                    src[row, 9 * side] = double(sp_recv[s, n, side].astype(F32)[0:8])
            for n in range(16):
                steps = (0,) if n < 8 else (2,)
                fp[n] = combine(n, [gather(n, kp, part[n, kp], steps) for kp in range(2)])

        @pl.when(ocean)
        def _():
            wait_arrivals(functools.partial(s_copy, s, True), around)
            sides = [[sp_recv[s, n, side].astype(F32) for side in range(2)] for n in range(3)]
            for row, pick in enumerate((band(0), joined(1), band(3), joined(4), band(6))):
                put_band(s, row, pick)
            first = lane8 < 32
            for side in range(2):
                north, center, south = (sides[n][side] for n in range(3))
                column = 9 * side
                src[0, column] = double_high(north[0:8])
                src[1, column] = jnp.where(first, double_low(north[8:16]), double_low(center[0:8]))
                src[2, column] = double_high(center[0:8])
                src[3, column] = jnp.where(first, double_low(center[8:16]), double_low(south[0:8]))
                src[4, column] = double_high(south[0:8])

    def regrid_patch(n, c):
        blank = jnp.zeros((8, LANES), F32)
        fp[n] = combine(n, [gather(n, kp, blank, range(3)) for kp in range(2)])

    def regrid_edges():
        picked = []
        left = (lane8 & 3) < 2
        for kp in range(2):
            index = gi[24, kp] & (LANES - 1)
            which = gi[24, kp] >> 7
            value = jnp.zeros((8, LANES), F32)
            for d in range(5):
                inner = take(jnp.where(inner8 < 8, src[d, 1], src[d, 8]), index)
                outer = jnp.where(left, take(src[d, 0], index), take(src[d, 9], index))
                value = jnp.where(which == 2 * d, inner, value)
                value = jnp.where(which == 2 * d + 1, outer, value)
            picked.append(value)
        fp[24] = combine(24, picked)

    def forcing_rows(bands):
        zero = jnp.zeros((8, LANES), F32)
        tiles = blocks_swapped(
            jnp.concatenate(
                [
                    jnp.where(low, fp[k], fp[8 + k]),
                    jnp.where(low, fp[16 + k], zero) if bands == 3 else zero,
                ],
                0,
            ).astype(BF)
            for k in range(8)
        )
        for k in range(8):
            tile = tiles[k].astype(F32)
            fr[k] = double_low(tile[0:8])
            fr[8 + k] = double_high(tile[0:8])
            if bands == 3 and k < 4:
                fr[16 + k] = double_low(tile[8:16])

    def finish_rows(s, first, rows):
        rows = [values.astype(BF) for values in rows]
        for u, values in enumerate(rows):
            if s + 1 < STEPS:
                xr[s + 1, first + u + 2] = values
            else:
                final[first + u] = values
        return rows

    def air_step(s):
        forcing_rows(2)
        ones = jnp.where(sub8 < 7, 1.0, 0.0)
        blank = jnp.zeros((8, LANES), F32)

        columns = []
        for r in range(ROWS):
            tail = jnp.concatenate([jnp.where(low, fr[r], ones), blank], 0).astype(BF)
            columns.append(jnp.concatenate([xr[s, r + 2], tail], 0))
        for first in range(0, ROWS, AIR_ROWS):
            block = jnp.concatenate(columns[first : first + AIR_ROWS], 1)
            hidden = gelu_of_twice(
                jnp.dot(wa[...], block, preferred_element_type=F32)
            ).astype(BF)
            update = jnp.dot(atm_out_ref[...], hidden, preferred_element_type=F32)
            finish_rows(
                s,
                first,
                [
                    xr[s, first + u + 2].astype(F32) + update[:, 128 * u : 128 * u + 128]
                    for u in range(AIR_ROWS)
                ],
            )

    def ocean_step(s):
        run(range(24), regrid_patch)
        regrid_edges()
        forcing_rows(3)
        pos = lane80 & 3
        pos8 = lane8 & 3
        pos16 = lane16 & 3

        def taps(halo, mine, where):
            return (
                pltpu.roll(jnp.where(where == 0, halo, mine), 1, 1),
                halo,
                pltpu.roll(jnp.where(where == 2, mine, halo), LANES - 1, 1),
            )

        def swapped(halo, where):
            return jnp.where(where == 1, pltpu.roll(halo, LANES - 1, 1), pltpu.roll(halo, 1, 1))

        own_forcing = jnp.zeros((8, LANES), F32)
        for t in range(TALL):
            own_forcing = jnp.where((lane8 >> 2) == t, pltpu.roll(fr[t], 4 * t + 2, 1), own_forcing)
        beside_forcing = fp[24]
        first, second, third = taps(beside_forcing, own_forcing, pos8)
        ones = jnp.where(sub8 < 7, 1.0, 0.0)
        x3e[240:256] = jnp.concatenate(
            [jnp.where(low, first, second), jnp.where(low, third, ones)], 0
        ).astype(BF)
        swapped_forcing = swapped(beside_forcing, pos8)
        for t in range(TALL):
            forcing = fr[t]
            halo = pltpu.roll(swapped_forcing, 126 - 4 * t, 1)
            left = jnp.where(lane8 == 0, halo, pltpu.roll(forcing, 1, 1))
            right = jnp.where(lane8 == LANES - 1, halo, pltpu.roll(forcing, LANES - 1, 1))
            x3[t, 240:256] = jnp.concatenate(
                [jnp.where(low, left, forcing), jnp.where(low, right, ones)], 0
            ).astype(BF)

        def rim(t):
            halo = pltpu.roll(hh[...], 126 - 4 * t, 1)
            x3[t, 0:80] = jnp.where(lane80 == 0, halo, x3[t, 0:80])
            x3[t, 160:240] = jnp.where(lane80 == LANES - 1, halo, x3[t, 160:240])

        def first_conv(p, c):
            h = 2 * p
            total = jnp.zeros((HOP, 256), F32)
            for a in range(3):
                columns = jnp.concatenate([x3[h + a], x3[h + a + 1]], 1)
                total = total + jnp.dot(w1[a], columns, preferred_element_type=F32)
            active = gelu_of_twice(total)
            if p == 0:
                active = jnp.where((iota((HOP, 256), 1) < 128) & (i == 0), 0.0, active)
            if p == 8:
                active = jnp.where((iota((HOP, 256), 1) >= 128) & (i == lats - 1), 0.0, active)
            active = active.astype(BF)
            hid[h] = active[:, 0:128]
            hid[h + 1] = active[:, 128:256]

        wait_arrivals(functools.partial(x_copy, s), [(0, -1), (0, 1)])
        beside = jnp.where(pos < 2, eg_recv[s, 0], eg_recv[s, 1])
        hh[...] = swapped(beside, pos)
        for t in range(2, 18):
            rim(t)
        run(range(1, 8), first_conv)

        wait_arrivals(functools.partial(x_copy, s), [(di, dj) for di, dj in ring if di])
        own = eg[s]
        for t in (0, 1, 18, 19):
            own = jnp.where((lane80 >> 2) == t, pltpu.roll(xr[s, t], 4 * t + 2, 1), own)
        ends = [jnp.where(pos16 < 2, cp_recv[s, n, 0], cp_recv[s, n, 1]) for n in range(2)]
        corner = jnp.where(lane16 < 64, ends[0], ends[1])
        corner = jnp.concatenate(
            [pltpu.roll(corner, LANES - 8 * part, 1) if part else corner for part in range(5)], 0
        )
        beside = jnp.where((lane80 >= 8) & (lane80 < 72), beside, corner)
        state_taps = taps(beside, own, pos)
        for b in range(3):
            x3e[CH * b : CH * b + CH] = state_taps[b]
        hh[...] = swapped(beside, pos)
        for t in (0, 1, 18, 19):
            fill(t, xr[s, t])
            rim(t)
        run((0, 8), first_conv)

        total = jnp.zeros((HOP, LANES), F32)
        for a in range(3):
            columns = x3e[...]
            if a:
                columns = pltpu.roll(columns, LANES - 4 * a, 1)
            total = total + jnp.dot(w1[a], columns, preferred_element_type=F32)
        slot = iota((HOP, LANES), 1) >> 2
        outside = ((slot == 0) & (i == 0)) | ((slot == 17) & (i == lats - 1))
        he[...] = jnp.where(outside, 0.0, gelu_of_twice(total)).astype(BF)
        total = jnp.zeros((240, LANES), F32)
        for a in range(3):
            columns = he[...]
            if a:
                columns = pltpu.roll(columns, LANES - 4 * a, 1)
            total = total + jnp.dot(w2[a], columns, preferred_element_type=F32)
        ze[...] = jnp.where(
            pos == 1,
            pltpu.roll(total[160:240], LANES - 1, 1),
            pltpu.roll(total[0:80], 1, 1),
        )

        def second_conv(p, c):
            r = 2 * p
            total = jnp.zeros((240, 256), F32)
            for a in range(3):
                columns = jnp.concatenate([hid[r + a], hid[r + a + 1]], 1)
                total = total + jnp.dot(w2[a], columns, preferred_element_type=F32)
            rows = []
            for u in range(2):
                part = total[:, 128 * u : 128 * u + 128]
                halo = pltpu.roll(ze[...], 126 - 4 * (r + u), 1)
                left = jnp.where(lane80 == 0, halo, pltpu.roll(part[0:80], 1, 1))
                right = jnp.where(
                    lane80 == LANES - 1, halo, pltpu.roll(part[160:240], LANES - 1, 1)
                )
                update = left + part[80:160] + right
                rows.append(xr[s, r + u + 2].astype(F32) + wet[r + u : r + u + 1] * update)
            rows = finish_rows(s, r, rows)
            if s + 1 < STEPS:
                for u in range(2):
                    t = r + u + 2
                    fill(t, rows[u])
                    eg[s + 1] = jnp.where(
                        (lane80 >> 2) == t, pltpu.roll(rows[u], 4 * t + 2, 1), eg[s + 1]
                    )

        if s + 1 < STEPS:
            run((0, 7), second_conv)
            start_all(functools.partial(x_copy, s + 1), [(-1, 0), (1, 0)])
        run(range(1, 7), second_conv)
        if s + 1 == STEPS:
            run((0, 7), second_conv)
        if s + 1 < STEPS:
            corner_rows(s + 1)
            start_all(
                functools.partial(x_copy, s + 1), [(di, dj) for di, dj in ring if dj]
            )

    for s in range(STEPS):
        if s:
            surface(s)
            s_all(start_all, s, True)

        sources(s)

        @pl.when(ocean)
        def _(s=s):
            ocean_step(s)

        @pl.when(air)
        def _(s=s):
            air_step(s)

    out_ref[0] = jnp.transpose(final[...], (1, 0, 2))

    for s in range(STEPS):
        s_all(wait_departures, s, True)

    @pl.when(ocean)
    def _():
        for s in range(STEPS):
            wait_departures(functools.partial(x_copy, s), ring)
        wait_departures(q_copy, ring)


def solution(mesh):
    lats, lons = mesh.shape["lat"], mesh.shape["lon"]
    vmem = pl.BlockSpec(memory_space=pltpu.VMEM)
    anywhere = pl.BlockSpec(memory_space=pl.ANY)
    dma = pltpu.SemaphoreType.DMA

    def local(*args):
        args = list(args)
        args[5] = args[5].T
        args[8] = args[8].transpose(1, 2, 0)
        args[10] = args[10].transpose(1, 0, 2)
        return pl.pallas_call(
            functools.partial(kernel, lats, lons),
            out_shape=jax.ShapeDtypeStruct((1, CH, ROWS, LANES), BF),
            in_specs=[anywhere] * 11,
            out_specs=vmem,
            scratch_shapes=[
                pltpu.VMEM((1, CH, ROWS, LANES), BF),
                pltpu.VMEM((ROWS, LANES), I32),
                pltpu.VMEM((1, 2, 4, ROWS, LANES), I32),
                pltpu.VMEM((1, 4, ROWS, LANES), F32),
                pltpu.VMEM((2, 4, CH), F32),
                pltpu.VMEM((84, 384), BF),
                pltpu.VMEM((384,), F32),
                pltpu.VMEM((CH, 384), BF),
                pltpu.VMEM((9, 84, HO), BF),
                pltpu.VMEM((HO,), F32),
                pltpu.VMEM((9, CH, HO), BF),
                pltpu.VMEM((LANES, LANES), F32),
                pltpu.VMEM((ROWS, CH, LANES), BF),
                pltpu.VMEM((STEPS, TALL, CH, LANES), BF),
                pltpu.VMEM((STEPS, CH, LANES), BF),
                pltpu.VMEM((STEPS, 2, CH, LANES), BF),
                pltpu.VMEM((STEPS, 16, LANES), BF),
                pltpu.VMEM((STEPS, 2, 2, 16, LANES), BF),
                pltpu.VMEM((24, 8, LANES), F32),
                pltpu.VMEM((STEPS, 3, 32, LANES), BF),
                pltpu.VMEM((STEPS, 7, 32, LANES), BF),
                pltpu.VMEM((STEPS, 2, 16, LANES), BF),
                pltpu.VMEM((STEPS, 3, 2, 16, LANES), BF),
                pltpu.VMEM((24, 8, LANES), F32),
                pltpu.VMEM((8, LANES), F32),
                pltpu.VMEM((3, 2, 8, LANES), F32),
                pltpu.VMEM((25, 2, 8, LANES), I32),
                pltpu.VMEM((25, 2, 8, LANES), F32),
                pltpu.VMEM((5, 10, 8, LANES), F32),
                pltpu.VMEM((16, 2, 8, LANES), F32),
                pltpu.VMEM((25, 8, LANES), F32),
                pltpu.VMEM((24, 8, LANES), F32),
                pltpu.VMEM((TALL, 256, LANES), BF),
                pltpu.VMEM((256, LANES), BF),
                pltpu.VMEM((3, HOP, 256), BF),
                pltpu.VMEM((3, 240, HOP), BF),
                pltpu.VMEM((384, 96), BF),
                pltpu.VMEM((18, HOP, LANES), BF),
                pltpu.VMEM((HOP, LANES), BF),
                pltpu.VMEM((CH, LANES), BF),
                pltpu.VMEM((CH, LANES), F32),
                pltpu.VMEM((ROWS, LANES), F32),
                pltpu.VMEM((ROWS, LANES), F32),
                pltpu.VMEM((24, CH), BF),
                dma((11,)),
                dma((STEPS, 3, 3)),
                dma((STEPS, 3, 3)),
                dma((STEPS, 3, 3)),
                dma((STEPS, 3, 3)),
                dma((3, 3)),
                dma((3, 3)),
            ],
            compiler_params=pltpu.CompilerParams(
                collective_id=0,
                has_side_effects=True,
                vmem_limit_bytes=60 * 1024 * 1024,
            ),
        )(*args)

    return jax.shard_map(
        local,
        mesh=mesh,
        in_specs=(
            P("grp", None, "lat", "lon"),
            P("lat", "lon"),
            P("grp", None, None, "lat", "lon"),
            P("grp", None, "lat", "lon"),
            P(),
            P(),
            P(),
            P(),
            P(),
            P(),
            P(),
        ),
        out_specs=P("grp", None, "lat", "lon"),
        check_vma=False,
    )
```

```python
import functools

import jax
import jax.numpy as jnp
from jax import lax
from jax.experimental import pallas as pl
from jax.experimental.pallas import tpu as pltpu
from jax.sharding import PartitionSpec as P

BF = jnp.bfloat16
F32 = jnp.float32
I32 = jnp.int32
MESH = pl.DeviceIdType.MESH

STEPS = 2
HW = 8
CH = 80
HO = 200
HOP = 208
ROWS = 16
LANES = 128
TALL = ROWS + 4
AIR_ROWS = 16
SURFACE_ROWS = 4


def iota(shape, axis):
    return lax.broadcasted_iota(I32, shape, axis)


def gelu_of_twice(half):
    inner = half * (1.5957691216057308 + 0.285419265090401 * (half * half))
    return half + half * jnp.tanh(inner)


def thirds(x):
    high = x.astype(BF).astype(F32)
    middle = (x - high).astype(BF).astype(F32)
    return high, middle, x - high - middle


def kernel(
    lats,
    lons,
    state_hbm,
    mask_hbm,
    offsets_hbm,
    weights_hbm,
    proj_hbm,
    atm_in_hbm,
    atm_bias_hbm,
    atm_out_hbm,
    ocn_in_hbm,
    ocn_bias_hbm,
    ocn_out_hbm,
    out_ref,
    state_ref,
    mask_ref,
    offsets_ref,
    weights_ref,
    proj_ref,
    atm_in_ref,
    atm_bias_ref,
    atm_out_ref,
    ocn_in_v,
    ocn_bias_ref,
    ocn_out_v,
    flip,
    final,
    xr,
    eg,
    eg_recv,
    cp,
    cp_recv,
    srow,
    sm,
    sb,
    sp,
    sp_recv,
    q,
    qe,
    qe_recv,
    gi,
    gw,
    src,
    part,
    fp,
    fr,
    x3,
    x3e,
    w1,
    w2,
    wa,
    hid,
    he,
    hh,
    ze,
    keep,
    wet,
    pp,
    load_sem,
    s_send,
    s_recv,
    x_send,
    x_recv,
    q_send,
    q_recv,
):
    g = lax.axis_index("grp")
    i = lax.axis_index("lat")
    j = lax.axis_index("lon")
    ocean = g == 1
    air = g == 0
    has = {-1: i > 0, 0: None, 1: i < lats - 1}

    def run(steps, body):
        for step in steps:
            body(step, 0)

    def place(group, di, dj):
        return (group, i + di, lax.rem(j + dj + lons, lons))

    def when(condition, action):
        if condition is None:
            action()
        else:
            pl.when(condition)(action)

    lane8 = iota((8, LANES), 1)
    sub8 = iota((8, LANES), 0)
    low = sub8 < 4
    lane80 = iota((CH, LANES), 1)
    lane16 = iota((16, LANES), 1)
    inner8 = lane8 & 15
    air_shift = jnp.where(air, 2, 0)
    ocean_shift = jnp.where(ocean, 2, 0)

    pairs = (
        (state_hbm, state_ref),
        (mask_hbm, mask_ref),
        (offsets_hbm, offsets_ref),
        (weights_hbm, weights_ref),
        (proj_hbm, proj_ref),
        (atm_in_hbm, atm_in_ref),
        (atm_bias_hbm, atm_bias_ref),
        (atm_out_hbm, atm_out_ref),
        (ocn_in_hbm, ocn_in_v),
        (ocn_bias_hbm, ocn_bias_ref),
        (ocn_out_hbm, ocn_out_v),
    )
    loads = [
        pltpu.make_async_copy(src, dst, load_sem.at[n]) for n, (src, dst) in enumerate(pairs)
    ]
    for load in loads[0:5]:
        load.start()

    @pl.when(ocean)
    def _():
        for load in loads[8:11]:
            load.start()

    @pl.when(air)
    def _():
        for load in loads[5:8]:
            load.start()

    q[...] = jnp.zeros((24, 8, LANES), F32)
    for di, block, rows in ((-1, 0, slice(0, 2)), (1, 2, slice(18, 20))):
        def blank(block=block, rows=rows):
            for s in range(STEPS):
                xr[s, rows] = jnp.zeros((2, CH, LANES), BF)
                sb[s, slice(0, 2) if block == 0 else slice(5, 7)] = jnp.zeros((2, 32, LANES), BF)
                sp_recv[s, block] = jnp.zeros((2, 16, LANES), BF)
                cp_recv[s, block // 2] = jnp.zeros((2, 16, LANES), BF)
            qe_recv[block] = jnp.zeros((2, 8, LANES), F32)

        pl.when(jnp.logical_not(has[di]))(blank)

    barrier = pltpu.get_barrier_semaphore()

    def greet(group, di, dj):
        when(
            has[di],
            lambda: pl.semaphore_signal(
                barrier, inc=1, device_id=place(group, di, dj), device_id_type=MESH
            ),
        )

    for di in (-1, 0, 1):
        for dj in (-1, 0, 1):
            greet(1 - g, di, dj)

    @pl.when(ocean)
    def _():
        for di in (-1, 0, 1):
            for dj in (-1, 0, 1):
                if di or dj:
                    greet(1, di, dj)

    def remote(src, dst, send, recv, target):
        return pltpu.make_async_remote_copy(
            src_ref=src,
            dst_ref=dst,
            send_sem=send,
            recv_sem=recv,
            device_id=target,
            device_id_type=MESH,
        )

    def s_copy(s, wide, di, dj):
        n = 1 - di
        if dj == 0:
            first = 1 if di == 1 else 0
            count = (3 if di == 0 else 2) if wide else (2 if di == 0 else 1)
            source = sm.at[s, pl.ds(first, count)]
            target = sb.at[s, pl.ds({1: 0, 0: 2, -1: 5}[di], count)]
        else:
            source = sp.at[s, 0 if dj == -1 else 1]
            target = sp_recv.at[s, n, 0 if dj == 1 else 1]
        return remote(
            source, target, s_send.at[s, n, dj + 1], s_recv.at[s, n, dj + 1], place(1 - g, di, dj)
        )

    def x_copy(s, di, dj):
        n = 1 - di
        if dj == 0:
            src = xr.at[s, pl.ds(16 if di == 1 else 2, 2)]
            dst = xr.at[s, pl.ds(0 if di == 1 else 18, 2)]
        elif di == 0:
            src = eg.at[s]
            dst = eg_recv.at[s, 0 if dj == 1 else 1]
        else:
            src = cp.at[s]
            dst = cp_recv.at[s, n // 2, 0 if dj == 1 else 1]
        return remote(src, dst, x_send.at[s, n, dj + 1], x_recv.at[s, n, dj + 1], place(1, di, dj))

    def q_copy(di, dj):
        n = 1 - di
        if dj == 0:
            src = q.at[pl.ds(16 if di == 1 else 2, 2)]
            dst = q.at[pl.ds(0 if di == 1 else 18, 2)]
        else:
            src = qe
            dst = qe_recv.at[n, 0 if dj == 1 else 1]
        return remote(src, dst, q_send.at[n, dj + 1], q_recv.at[n, dj + 1], place(1, di, dj))

    around = [(di, dj) for di in (-1, 1, 0) for dj in (-1, 1, 0)]
    ring = [(di, dj) for di, dj in around if di or dj]
    beside_pairs = [(0, -1), (0, 1)]
    corner_pairs = [(di, dj) for di, dj in ring if di and dj]

    def s_all(action, s, sending):
        @pl.when(air)
        def _():
            action(functools.partial(s_copy, s, sending), around)

        @pl.when(ocean)
        def _():
            action(functools.partial(s_copy, s, not sending), around)

    def start_all(make, pairs):
        for di, dj in pairs:
            when(has[di], lambda di=di, dj=dj: make(di, dj).start())

    def wait_arrivals(make, pairs):
        for di, dj in pairs:
            when(has[-di], lambda di=di, dj=dj: make(di, dj).wait_recv())

    def wait_departures(make, pairs):
        for di, dj in pairs:
            when(has[di], lambda di=di, dj=dj: make(di, dj).wait_send())

    loads[0].wait()
    xr[0, 2:18] = jnp.transpose(state_ref[0], (1, 0, 2))

    loads[1].wait()
    loads[4].wait()
    wet_values = mask_ref[...].astype(F32)
    wet[...] = wet_values
    kept = jnp.where(ocean, wet_values, 1.0)
    keep[...] = kept
    high, middle, rest = thirds(proj_ref[g])
    pp[...] = jnp.concatenate([high, high, middle, middle, rest, rest], 0).astype(BF)

    srow[...] = jnp.zeros((24, 8, LANES), F32)
    def blocks_swapped(tiles):
        tiles = list(tiles)
        block = iota(tiles[0].shape, 1) >> 4
        for s in (4, 2, 1):
            stays = (block & s) == 0
            for a in range(8):
                if not a & s:
                    x, y = tiles[a], tiles[a + s]
                    tiles[a] = jnp.where(stays, x, pltpu.roll(y, 16 * s, 1))
                    tiles[a + s] = jnp.where(stays, pltpu.roll(x, LANES - 16 * s, 1), y)
        return tiles

    def turned(x):
        return pltpu.roll(x, 4, 0)

    def double_low(x):
        return jnp.where(low, x, turned(x))

    def double_high(x):
        return jnp.where(low, turned(x), x)

    def fill(t, cells):
        x3[t, 0:80] = pltpu.roll(cells, 1, 1)
        x3[t, 80:160] = cells
        x3[t, 160:240] = pltpu.roll(cells, LANES - 1, 1)

    def surface_rows(first, rows):
        parts = jnp.dot(pp[...], jnp.concatenate(rows, 1), preferred_element_type=F32)
        fields = parts[0:8] + parts[8:16] + parts[16:24]
        for u in range(len(rows)):
            kept_row = jnp.broadcast_to(keep[first + u : first + u + 1], (8, LANES))
            srow[air_shift + first + u] = fields[:, 128 * u : 128 * u + 128] * kept_row

    def surface(s):
        for m in range(0, ROWS, SURFACE_ROWS):
            surface_rows(m, [xr[s, m + 2 + u] for u in range(SURFACE_ROWS)])
        zero = jnp.zeros((8, LANES), F32)
        tiles = blocks_swapped(
            jnp.concatenate(
                [jnp.where(low, srow[k], srow[8 + k]), jnp.where(low, srow[16 + k], zero)], 0
            ).astype(BF)
            for k in range(8)
        )
        sp[s, 0] = tiles[0]
        sp[s, 1] = tiles[7]
        tiles = [tile.astype(F32) for tile in tiles]
        for half in range(2):
            made = [[], [], []]
            for m in range(2):
                even, odd = tiles[4 * half + 2 * m], tiles[4 * half + 2 * m + 1]
                made[0].append(jnp.where(low, even[0:8], turned(odd[0:8])))
                made[1].append(jnp.where(low, turned(even[0:8]), odd[0:8]))
                made[2].append(jnp.where(low, even[8:16], turned(odd[8:16])))
            for band in range(3):
                sm[s, band, 16 * half : 16 * half + 16] = jnp.concatenate(made[band], 0).astype(BF)

    def edge_rows(s):
        def add(t, acc):
            return jnp.where((lane80 >> 2) == t, pltpu.roll(xr[s, t], 4 * t + 2, 1), acc)

        own = jnp.zeros((CH, LANES), BF)
        for t in range(2, 18):
            own = add(t, own)
        eg[s] = own

    def corner_rows(s):
        own = eg[s]
        packed = jnp.zeros((16, LANES), BF)
        for part in range(5):
            tile = pltpu.roll(own[16 * part : 16 * part + 16], 64 + 8 * part, 1)
            place_of = lane16 - 8 * part
            inside = ((place_of >= 0) & (place_of < 8)) | ((place_of >= 72) & (place_of < 80))
            packed = jnp.where(inside, tile, packed)
        cp[s] = packed

    surface(0)

    loads[2].wait()
    loads[3].wait()
    for k in range(4):
        code = (offsets_ref[0, 0, k] + HW) * 32 + (offsets_ref[0, 1, k] + HW)
        flip[16 * k : 16 * k + 16] = code.astype(F32)
        flip[64 + 16 * k : 64 + 16 * k + 16] = weights_ref[0, k]
    for r in range(ROWS):
        q[ocean_shift + r] = flip[pl.ds(r, 8, stride=ROWS), :]

    @pl.when(ocean)
    def _():

        def add(t, acc):
            return jnp.where((lane8 >> 2) == t, pltpu.roll(q[t], 4 * t + 2, 1), acc)

        own = jnp.zeros((8, LANES), F32)
        for t in range(2, 18):
            own = add(t, own)
        qe[...] = own

    neighbours = 1 + has[-1].astype(I32) + has[1].astype(I32)
    pl.semaphore_wait(barrier, 3 * neighbours + g * (3 * neighbours - 1))

    @pl.when(ocean)
    def _():
        start_all(q_copy, ring)

    s_all(start_all, 0, True)

    @pl.when(ocean)
    def _():
        start_all(functools.partial(x_copy, 0), [(-1, 0), (1, 0)])
        edge_rows(0)
        start_all(functools.partial(x_copy, 0), beside_pairs)
        corner_rows(0)
        start_all(functools.partial(x_copy, 0), corner_pairs)
        eg[1] = jnp.zeros((CH, LANES), BF)
        for t in range(2, 18):
            fill(t, xr[0, t])

    @pl.when(ocean)
    def _():
        for load in loads[8:11]:
            load.wait()

        def rows_of(values):
            return thirds(0.5 * values.reshape(1, -1))

        spare = jnp.zeros((1, HO), F32)
        bias = jnp.concatenate([*rows_of(ocn_bias_ref[...]), spare], 0)
        for a in range(3):
            taps = [0.5 * ocn_in_v[3 * a + b].astype(F32) for b in range(3)]
            last = bias if a == 1 else jnp.zeros((4, HO), F32)
            stacked = jnp.concatenate(
                [tap[0:CH] for tap in taps] + [tap[CH:] for tap in taps] + [last], 0
            )
            stacked = jnp.concatenate([stacked, jnp.zeros((256, 256 - HO), F32)], 1)
            w1[a] = stacked.T[0:HOP].astype(BF)
            for b in range(3):
                values = ocn_out_v[3 * a + b].astype(F32)
                w2[a, CH * b : CH * b + CH, :] = jnp.concatenate(
                    [values, jnp.zeros((CH, HOP - HO), F32)], 1
                ).astype(BF)

    @pl.when(air)
    def _():
        for load in loads[5:8]:
            load.wait()
        bias = thirds(0.5 * atm_bias_ref[...].reshape(1, -1))
        stacked = jnp.concatenate(
            [0.5 * atm_in_ref[...].astype(F32), *bias, jnp.zeros((41, 384), F32)], 0
        )
        wa[...] = stacked.T[:, 0:96].astype(BF)

    def spread(values, base):
        first = jnp.broadcast_to(values[base : base + 1], (8, LANES))
        second = jnp.broadcast_to(values[base + 1 : base + 2], (8, LANES))
        return jnp.where(low, first, second)

    def decode_band(band):
        tiles = blocks_swapped(q[8 * band + k] for k in range(8))
        for patch in range(8):
            for kp in range(2):
                code = spread(tiles[patch], 2 * kp).astype(I32)
                down = (lane8 >> 4) + (code >> 5)
                across = inner8 + (code & 31)
                beside = jnp.where((across >= 8) & (across < 24), 0, 1)
                gi[8 * band + patch, kp] = (
                    ((down & 7) * 16 + ((across + 8) & 15)) + ((down >> 3) * 2 + beside) * LANES
                )
                gw[8 * band + patch, kp] = spread(tiles[patch], 4 + 2 * kp)

    @pl.when(air)
    def _():
        decode_band(0)
        decode_band(1)

    @pl.when(ocean)
    def _():
        decode_band(1)
        wait_arrivals(q_copy, ring)
        decode_band(0)
        decode_band(2)
        pos = lane8 & 3
        beside = [jnp.where(pos < 2, qe_recv[n, 0], qe_recv[n, 1]) for n in range(3)]
        ends = jnp.where(
            lane8 < 64, pltpu.roll(beside[0], 64, 1), pltpu.roll(beside[2], 64, 1)
        )
        values = jnp.where((lane8 >= 8) & (lane8 < 72), beside[1], ends)
        for kp in range(2):
            code = spread(values, 2 * kp).astype(I32)
            down = (lane8 >> 2) + (code >> 5)
            across = jnp.where(pos < 2, pos - 2, pos + 126) + (code & 31) - HW
            outer = jnp.where((across >= 0) & (across < LANES), 0, 1)
            gi[24, kp] = ((down & 7) * 16 + (across & 15)) + ((down >> 3) * 2 + outer) * LANES
            gw[24, kp] = spread(values, 4 + 2 * kp)

    def take(values, index):
        return jnp.take_along_axis(values, index, axis=1, mode="promise_in_bounds")

    def combine(n, picked):
        total = picked[0] * gw[n, 0] + picked[1] * gw[n, 1]
        return total + turned(total)

    def gather(n, kp, value, steps):
        band, patch = n >> 3, n & 7
        index = gi[n, kp] & (LANES - 1)
        which = gi[n, kp] >> 7
        for d in steps:
            there = jnp.where(inner8 < 8, src[band + d, patch + 2], src[band + d, patch])
            value = jnp.where(which == 2 * d, take(src[band + d, patch + 1], index), value)
            value = jnp.where(which == 2 * d + 1, take(there, index), value)
        return value

    def put_band(s, row, pick):
        for quarter in range(2):
            tile = pick(slice(16 * quarter, 16 * quarter + 16))
            for m in range(2):
                values = tile[8 * m : 8 * m + 8]
                src[row, 4 * quarter + 2 * m + 1] = double_low(values)
                src[row, 4 * quarter + 2 * m + 2] = double_high(values)

    def sources(s):
        def band(k):
            return lambda rows: sb[s, k, rows].astype(F32)

        def joined(k):
            return lambda rows: jnp.where(
                lane16 < 32, sb[s, k, rows].astype(F32), sb[s, k + 1, rows].astype(F32)
            )

        @pl.when(air)
        def _():
            middle = [(0, dj) for dj in (-1, 1, 0)]
            wait_arrivals(functools.partial(s_copy, s, False), middle)
            sides = [[sp_recv[s, 1, side].astype(F32) for side in range(2)]]
            for row, k in ((1, 2), (2, 3)):
                put_band(s, row, band(k))
            for side in range(2):
                src[1, 9 * side] = double_low(sides[0][side][0:8])
                src[2, 9 * side] = double_high(sides[0][side][0:8])
            blank = jnp.zeros((8, LANES), F32)
            for n in range(16):
                for kp in range(2):
                    part[n, kp] = gather(n, kp, blank, (1, 2) if n < 8 else (0, 1))
            beyond = [(di, dj) for di, dj in around if di]
            wait_arrivals(functools.partial(s_copy, s, False), beyond)
            for row, k, n, double in ((0, 0, 0, double_high), (3, 5, 2, double_low)):
                put_band(s, row, band(k))
                for side in range(2):
                    src[row, 9 * side] = double(sp_recv[s, n, side].astype(F32)[0:8])
            for n in range(16):
                steps = (0,) if n < 8 else (2,)
                fp[n] = combine(n, [gather(n, kp, part[n, kp], steps) for kp in range(2)])

        @pl.when(ocean)
        def _():
            wait_arrivals(functools.partial(s_copy, s, True), around)
            sides = [[sp_recv[s, n, side].astype(F32) for side in range(2)] for n in range(3)]
            for row, pick in enumerate((band(0), joined(1), band(3), joined(4), band(6))):
                put_band(s, row, pick)
            first = lane8 < 32
            for side in range(2):
                north, center, south = (sides[n][side] for n in range(3))
                column = 9 * side
                src[0, column] = double_high(north[0:8])
                src[1, column] = jnp.where(first, double_low(north[8:16]), double_low(center[0:8]))
                src[2, column] = double_high(center[0:8])
                src[3, column] = jnp.where(first, double_low(center[8:16]), double_low(south[0:8]))
                src[4, column] = double_high(south[0:8])

    def regrid_patch(n, c):
        blank = jnp.zeros((8, LANES), F32)
        fp[n] = combine(n, [gather(n, kp, blank, range(3)) for kp in range(2)])

    def regrid_edges():
        picked = []
        left = (lane8 & 3) < 2
        for kp in range(2):
            index = gi[24, kp] & (LANES - 1)
            which = gi[24, kp] >> 7
            value = jnp.zeros((8, LANES), F32)
            for d in range(5):
                inner = take(jnp.where(inner8 < 8, src[d, 1], src[d, 8]), index)
                outer = jnp.where(left, take(src[d, 0], index), take(src[d, 9], index))
                value = jnp.where(which == 2 * d, inner, value)
                value = jnp.where(which == 2 * d + 1, outer, value)
            picked.append(value)
        fp[24] = combine(24, picked)

    def forcing_rows(bands):
        zero = jnp.zeros((8, LANES), F32)
        tiles = blocks_swapped(
            jnp.concatenate(
                [
                    jnp.where(low, fp[k], fp[8 + k]),
                    jnp.where(low, fp[16 + k], zero) if bands == 3 else zero,
                ],
                0,
            ).astype(BF)
            for k in range(8)
        )
        for k in range(8):
            tile = tiles[k].astype(F32)
            fr[k] = double_low(tile[0:8])
            fr[8 + k] = double_high(tile[0:8])
            if bands == 3 and k < 4:
                fr[16 + k] = double_low(tile[8:16])

    def finish_rows(s, first, rows):
        rows = [values.astype(BF) for values in rows]
        for u, values in enumerate(rows):
            if s + 1 < STEPS:
                xr[s + 1, first + u + 2] = values
            else:
                final[first + u] = values
        return rows

    def air_step(s):
        forcing_rows(2)
        ones = jnp.where(sub8 < 7, 1.0, 0.0)
        blank = jnp.zeros((8, LANES), F32)

        columns = []
        for r in range(ROWS):
            tail = jnp.concatenate([jnp.where(low, fr[r], ones), blank], 0).astype(BF)
            columns.append(jnp.concatenate([xr[s, r + 2], tail], 0))
        for first in range(0, ROWS, AIR_ROWS):
            block = jnp.concatenate(columns[first : first + AIR_ROWS], 1)
            hidden = gelu_of_twice(
                jnp.dot(wa[...], block, preferred_element_type=F32)
            ).astype(BF)
            update = jnp.dot(atm_out_ref[...], hidden, preferred_element_type=F32)
            finish_rows(
                s,
                first,
                [
                    xr[s, first + u + 2].astype(F32) + update[:, 128 * u : 128 * u + 128]
                    for u in range(AIR_ROWS)
                ],
            )

    def ocean_step(s):
        run(range(24), regrid_patch)
        regrid_edges()
        forcing_rows(3)
        pos = lane80 & 3
        pos8 = lane8 & 3
        pos16 = lane16 & 3

        def taps(halo, mine, where):
            return (
                pltpu.roll(jnp.where(where == 0, halo, mine), 1, 1),
                halo,
                pltpu.roll(jnp.where(where == 2, mine, halo), LANES - 1, 1),
            )

        def swapped(halo, where):
            return jnp.where(where == 1, pltpu.roll(halo, LANES - 1, 1), pltpu.roll(halo, 1, 1))

        own_forcing = jnp.zeros((8, LANES), F32)
        for t in range(TALL):
            own_forcing = jnp.where((lane8 >> 2) == t, pltpu.roll(fr[t], 4 * t + 2, 1), own_forcing)
        beside_forcing = fp[24]
        first, second, third = taps(beside_forcing, own_forcing, pos8)
        ones = jnp.where(sub8 < 7, 1.0, 0.0)
        x3e[240:256] = jnp.concatenate(
            [jnp.where(low, first, second), jnp.where(low, third, ones)], 0
        ).astype(BF)
        swapped_forcing = swapped(beside_forcing, pos8)
        for t in range(TALL):
            forcing = fr[t]
            halo = pltpu.roll(swapped_forcing, 126 - 4 * t, 1)
            left = jnp.where(lane8 == 0, halo, pltpu.roll(forcing, 1, 1))
            right = jnp.where(lane8 == LANES - 1, halo, pltpu.roll(forcing, LANES - 1, 1))
            x3[t, 240:256] = jnp.concatenate(
                [jnp.where(low, left, forcing), jnp.where(low, right, ones)], 0
            ).astype(BF)

        def rim(t):
            halo = pltpu.roll(hh[...], 126 - 4 * t, 1)
            x3[t, 0:80] = jnp.where(lane80 == 0, halo, x3[t, 0:80])
            x3[t, 160:240] = jnp.where(lane80 == LANES - 1, halo, x3[t, 160:240])

        def first_conv(p, c):
            h = 2 * p
            total = jnp.zeros((HOP, 256), F32)
            for a in range(3):
                columns = jnp.concatenate([x3[h + a], x3[h + a + 1]], 1)
                total = total + jnp.dot(w1[a], columns, preferred_element_type=F32)
            active = gelu_of_twice(total)
            if p == 0:
                active = jnp.where((iota((HOP, 256), 1) < 128) & (i == 0), 0.0, active)
            if p == 8:
                active = jnp.where((iota((HOP, 256), 1) >= 128) & (i == lats - 1), 0.0, active)
            active = active.astype(BF)
            hid[h] = active[:, 0:128]
            hid[h + 1] = active[:, 128:256]

        def edge_tile(halo, mine):
            state_taps = taps(halo, mine, pos)
            for b in range(3):
                x3e[CH * b : CH * b + CH] = state_taps[b]
            total = jnp.zeros((HOP, LANES), F32)
            for a in range(3):
                columns = x3e[...]
                if a:
                    columns = pltpu.roll(columns, LANES - 4 * a, 1)
                total = total + jnp.dot(w1[a], columns, preferred_element_type=F32)
            slot = iota((HOP, LANES), 1) >> 2
            outside = ((slot == 0) & (i == 0)) | ((slot == 17) & (i == lats - 1))
            he[...] = jnp.where(outside, 0.0, gelu_of_twice(total)).astype(BF)
            total = jnp.zeros((240, LANES), F32)
            for a in range(3):
                columns = he[...]
                if a:
                    columns = pltpu.roll(columns, LANES - 4 * a, 1)
                total = total + jnp.dot(w2[a], columns, preferred_element_type=F32)
            ze[...] = jnp.where(
                pos == 1,
                pltpu.roll(total[160:240], LANES - 1, 1),
                pltpu.roll(total[0:80], 1, 1),
            )

        def second_conv(p, c):
            r = 2 * p
            total = jnp.zeros((240, 256), F32)
            for a in range(3):
                columns = jnp.concatenate([hid[r + a], hid[r + a + 1]], 1)
                total = total + jnp.dot(w2[a], columns, preferred_element_type=F32)
            rows = []
            for u in range(2):
                part = total[:, 128 * u : 128 * u + 128]
                halo = pltpu.roll(ze[...], 126 - 4 * (r + u), 1)
                left = jnp.where(lane80 == 0, halo, pltpu.roll(part[0:80], 1, 1))
                right = jnp.where(
                    lane80 == LANES - 1, halo, pltpu.roll(part[160:240], LANES - 1, 1)
                )
                update = left + part[80:160] + right
                rows.append(xr[s, r + u + 2].astype(F32) + wet[r + u : r + u + 1] * update)
            rows = finish_rows(s, r, rows)
            if s + 1 < STEPS:
                for u in range(2):
                    t = r + u + 2
                    fill(t, rows[u])
                    eg[s + 1] = jnp.where(
                        (lane80 >> 2) == t, pltpu.roll(rows[u], 4 * t + 2, 1), eg[s + 1]
                    )

        wait_arrivals(functools.partial(x_copy, s), [(0, -1), (0, 1)])
        beside = jnp.where(pos < 2, eg_recv[s, 0], eg_recv[s, 1])
        hh[...] = swapped(beside, pos)
        for t in range(2, 18):
            rim(t)
        run(range(1, 8), first_conv)
        if s + 1 == STEPS:
            edge_tile(beside, eg[s])
            run(range(1, 7), second_conv)

        wait_arrivals(functools.partial(x_copy, s), [(di, dj) for di, dj in ring if di])
        own = eg[s]
        for t in (0, 1, 18, 19):
            own = jnp.where((lane80 >> 2) == t, pltpu.roll(xr[s, t], 4 * t + 2, 1), own)
        ends = [jnp.where(pos16 < 2, cp_recv[s, n, 0], cp_recv[s, n, 1]) for n in range(2)]
        corner = jnp.where(lane16 < 64, ends[0], ends[1])
        corner = jnp.concatenate(
            [pltpu.roll(corner, LANES - 8 * part, 1) if part else corner for part in range(5)], 0
        )
        beside = jnp.where((lane80 >= 8) & (lane80 < 72), beside, corner)
        hh[...] = swapped(beside, pos)
        for t in (0, 1, 18, 19):
            fill(t, xr[s, t])
            rim(t)
        run((0, 8), first_conv)
        edge_tile(beside, own)
        run((0, 7), second_conv)

        if s + 1 < STEPS:
            start_all(functools.partial(x_copy, s + 1), [(-1, 0), (1, 0)])
            run(range(1, 7), second_conv)
            start_all(functools.partial(x_copy, s + 1), beside_pairs)
            corner_rows(s + 1)
            start_all(functools.partial(x_copy, s + 1), corner_pairs)

    for s in range(STEPS):
        if s:
            surface(s)
            s_all(start_all, s, True)

        sources(s)

        @pl.when(ocean)
        def _(s=s):
            ocean_step(s)

        @pl.when(air)
        def _(s=s):
            air_step(s)

    out_ref[0] = jnp.transpose(final[...], (1, 0, 2))

    for s in range(STEPS):
        s_all(wait_departures, s, True)

    @pl.when(ocean)
    def _():
        for s in range(STEPS):
            wait_departures(functools.partial(x_copy, s), ring)
        wait_departures(q_copy, ring)


def solution(mesh):
    lats, lons = mesh.shape["lat"], mesh.shape["lon"]
    vmem = pl.BlockSpec(memory_space=pltpu.VMEM)
    anywhere = pl.BlockSpec(memory_space=pl.ANY)
    dma = pltpu.SemaphoreType.DMA

    def local(*args):
        args = list(args)
        args[5] = args[5].T
        args[8] = args[8].transpose(1, 2, 0)
        args[10] = args[10].transpose(1, 0, 2)
        return pl.pallas_call(
            functools.partial(kernel, lats, lons),
            out_shape=jax.ShapeDtypeStruct((1, CH, ROWS, LANES), BF),
            in_specs=[anywhere] * 11,
            out_specs=vmem,
            scratch_shapes=[
                pltpu.VMEM((1, CH, ROWS, LANES), BF),
                pltpu.VMEM((ROWS, LANES), I32),
                pltpu.VMEM((1, 2, 4, ROWS, LANES), I32),
                pltpu.VMEM((1, 4, ROWS, LANES), F32),
                pltpu.VMEM((2, 4, CH), F32),
                pltpu.VMEM((84, 384), BF),
                pltpu.VMEM((384,), F32),
                pltpu.VMEM((CH, 384), BF),
                pltpu.VMEM((9, 84, HO), BF),
                pltpu.VMEM((HO,), F32),
                pltpu.VMEM((9, CH, HO), BF),
                pltpu.VMEM((LANES, LANES), F32),
                pltpu.VMEM((ROWS, CH, LANES), BF),
                pltpu.VMEM((STEPS, TALL, CH, LANES), BF),
                pltpu.VMEM((STEPS, CH, LANES), BF),
                pltpu.VMEM((STEPS, 2, CH, LANES), BF),
                pltpu.VMEM((STEPS, 16, LANES), BF),
                pltpu.VMEM((STEPS, 2, 2, 16, LANES), BF),
                pltpu.VMEM((24, 8, LANES), F32),
                pltpu.VMEM((STEPS, 3, 32, LANES), BF),
                pltpu.VMEM((STEPS, 7, 32, LANES), BF),
                pltpu.VMEM((STEPS, 2, 16, LANES), BF),
                pltpu.VMEM((STEPS, 3, 2, 16, LANES), BF),
                pltpu.VMEM((24, 8, LANES), F32),
                pltpu.VMEM((8, LANES), F32),
                pltpu.VMEM((3, 2, 8, LANES), F32),
                pltpu.VMEM((25, 2, 8, LANES), I32),
                pltpu.VMEM((25, 2, 8, LANES), F32),
                pltpu.VMEM((5, 10, 8, LANES), F32),
                pltpu.VMEM((16, 2, 8, LANES), F32),
                pltpu.VMEM((25, 8, LANES), F32),
                pltpu.VMEM((24, 8, LANES), F32),
                pltpu.VMEM((TALL, 256, LANES), BF),
                pltpu.VMEM((256, LANES), BF),
                pltpu.VMEM((3, HOP, 256), BF),
                pltpu.VMEM((3, 240, HOP), BF),
                pltpu.VMEM((384, 96), BF),
                pltpu.VMEM((18, HOP, LANES), BF),
                pltpu.VMEM((HOP, LANES), BF),
                pltpu.VMEM((CH, LANES), BF),
                pltpu.VMEM((CH, LANES), F32),
                pltpu.VMEM((ROWS, LANES), F32),
                pltpu.VMEM((ROWS, LANES), F32),
                pltpu.VMEM((24, CH), BF),
                dma((11,)),
                dma((STEPS, 3, 3)),
                dma((STEPS, 3, 3)),
                dma((STEPS, 3, 3)),
                dma((STEPS, 3, 3)),
                dma((3, 3)),
                dma((3, 3)),
            ],
            compiler_params=pltpu.CompilerParams(
                collective_id=0,
                has_side_effects=True,
                vmem_limit_bytes=60 * 1024 * 1024,
            ),
        )(*args)

    return jax.shard_map(
        local,
        mesh=mesh,
        in_specs=(
            P("grp", None, "lat", "lon"),
            P("lat", "lon"),
            P("grp", None, None, "lat", "lon"),
            P("grp", None, "lat", "lon"),
            P(),
            P(),
            P(),
            P(),
            P(),
            P(),
            P(),
        ),
        out_specs=P("grp", None, "lat", "lon"),
        check_vma=False,
    )
```

```python
import functools

import jax
import jax.numpy as jnp
from jax import lax
from jax.experimental import pallas as pl
from jax.experimental.pallas import tpu as pltpu
from jax.sharding import PartitionSpec as P

BF = jnp.bfloat16
F32 = jnp.float32
I32 = jnp.int32
MESH = pl.DeviceIdType.MESH

STEPS = 2
HW = 8
CH = 80
HO = 200
HOP = 208
ROWS = 16
LANES = 128
TALL = ROWS + 4
AIR_ROWS = 16
SURFACE_ROWS = 4


def iota(shape, axis):
    return lax.broadcasted_iota(I32, shape, axis)


def gelu_of_twice(half):
    inner = half * (1.5957691216057308 + 0.285419265090401 * (half * half))
    return half + half * jnp.tanh(inner)


def thirds(x):
    high = x.astype(BF).astype(F32)
    middle = (x - high).astype(BF).astype(F32)
    return high, middle, x - high - middle


def kernel(
    lats,
    lons,
    state_hbm,
    mask_hbm,
    offsets_hbm,
    weights_hbm,
    proj_hbm,
    atm_in_hbm,
    atm_bias_hbm,
    atm_out_hbm,
    ocn_in_hbm,
    ocn_bias_hbm,
    ocn_out_hbm,
    out_ref,
    state_ref,
    mask_ref,
    offsets_ref,
    weights_ref,
    proj_ref,
    atm_in_ref,
    atm_bias_ref,
    atm_out_ref,
    ocn_in_v,
    ocn_bias_ref,
    ocn_out_v,
    flip,
    final,
    xr,
    eg,
    eg_recv,
    cp,
    cp_recv,
    srow,
    sm,
    sb,
    sp,
    sp_recv,
    q,
    qe,
    qe_recv,
    gi,
    gw,
    src,
    part,
    fp,
    fr,
    x3,
    x3e,
    w1,
    w2,
    wa,
    hid,
    he,
    hh,
    ze,
    keep,
    wet,
    pp,
    load_sem,
    s_send,
    s_recv,
    x_send,
    x_recv,
    q_send,
    q_recv,
):
    g = lax.axis_index("grp")
    i = lax.axis_index("lat")
    j = lax.axis_index("lon")
    ocean = g == 1
    air = g == 0
    has = {-1: i > 0, 0: None, 1: i < lats - 1}

    def run(steps, body):
        for step in steps:
            body(step, 0)

    def place(group, di, dj):
        return (group, i + di, lax.rem(j + dj + lons, lons))

    def when(condition, action):
        if condition is None:
            action()
        else:
            pl.when(condition)(action)

    lane8 = iota((8, LANES), 1)
    sub8 = iota((8, LANES), 0)
    low = sub8 < 4
    lane80 = iota((CH, LANES), 1)
    lane16 = iota((16, LANES), 1)
    inner8 = lane8 & 15
    air_shift = jnp.where(air, 2, 0)
    ocean_shift = jnp.where(ocean, 2, 0)

    pairs = (
        (state_hbm, state_ref),
        (mask_hbm, mask_ref),
        (offsets_hbm, offsets_ref),
        (weights_hbm, weights_ref),
        (proj_hbm, proj_ref),
        (atm_in_hbm, atm_in_ref),
        (atm_bias_hbm, atm_bias_ref),
        (atm_out_hbm, atm_out_ref),
        (ocn_in_hbm, ocn_in_v),
        (ocn_bias_hbm, ocn_bias_ref),
        (ocn_out_hbm, ocn_out_v),
    )
    loads = [
        pltpu.make_async_copy(src, dst, load_sem.at[n]) for n, (src, dst) in enumerate(pairs)
    ]
    for load in loads[0:5]:
        load.start()

    @pl.when(ocean)
    def _():
        for load in loads[8:11]:
            load.start()

    @pl.when(air)
    def _():
        for load in loads[5:8]:
            load.start()

    q[...] = jnp.zeros((24, 8, LANES), F32)
    for di, block, rows in ((-1, 0, slice(0, 2)), (1, 2, slice(18, 20))):
        def blank(block=block, rows=rows):
            for s in range(STEPS):
                xr[s, rows] = jnp.zeros((2, CH, LANES), BF)
                sb[s, slice(0, 2) if block == 0 else slice(5, 7)] = jnp.zeros((2, 32, LANES), BF)
                sp_recv[s, block] = jnp.zeros((2, 16, LANES), BF)
                cp_recv[s, block // 2] = jnp.zeros((2, 16, LANES), BF)
            qe_recv[block] = jnp.zeros((2, 8, LANES), F32)

        pl.when(jnp.logical_not(has[di]))(blank)

    barrier = pltpu.get_barrier_semaphore()

    def greet(group, di, dj):
        when(
            has[di],
            lambda: pl.semaphore_signal(
                barrier, inc=1, device_id=place(group, di, dj), device_id_type=MESH
            ),
        )

    for di in (-1, 0, 1):
        for dj in (-1, 0, 1):
            greet(1 - g, di, dj)

    @pl.when(ocean)
    def _():
        for di in (-1, 0, 1):
            for dj in (-1, 0, 1):
                if di or dj:
                    greet(1, di, dj)

    def remote(src, dst, send, recv, target):
        return pltpu.make_async_remote_copy(
            src_ref=src,
            dst_ref=dst,
            send_sem=send,
            recv_sem=recv,
            device_id=target,
            device_id_type=MESH,
        )

    def s_copy(s, wide, di, dj):
        n = 1 - di
        if dj == 0:
            first = 1 if di == 1 else 0
            count = (3 if di == 0 else 2) if wide else (2 if di == 0 else 1)
            source = sm.at[s, pl.ds(first, count)]
            target = sb.at[s, pl.ds({1: 0, 0: 2, -1: 5}[di], count)]
        else:
            source = sp.at[s, 0 if dj == -1 else 1]
            target = sp_recv.at[s, n, 0 if dj == 1 else 1]
        return remote(
            source, target, s_send.at[s, n, dj + 1], s_recv.at[s, n, dj + 1], place(1 - g, di, dj)
        )

    def x_copy(s, di, dj):
        n = 1 - di
        if dj == 0:
            src = xr.at[s, pl.ds(16 if di == 1 else 2, 2)]
            dst = xr.at[s, pl.ds(0 if di == 1 else 18, 2)]
        elif di == 0:
            src = eg.at[s]
            dst = eg_recv.at[s, 0 if dj == 1 else 1]
        else:
            src = cp.at[s]
            dst = cp_recv.at[s, n // 2, 0 if dj == 1 else 1]
        return remote(src, dst, x_send.at[s, n, dj + 1], x_recv.at[s, n, dj + 1], place(1, di, dj))

    def q_copy(di, dj):
        n = 1 - di
        if dj == 0:
            src = q.at[pl.ds(16 if di == 1 else 2, 2)]
            dst = q.at[pl.ds(0 if di == 1 else 18, 2)]
        else:
            src = qe
            dst = qe_recv.at[n, 0 if dj == 1 else 1]
        return remote(src, dst, q_send.at[n, dj + 1], q_recv.at[n, dj + 1], place(1, di, dj))

    around = [(di, dj) for di in (-1, 1, 0) for dj in (-1, 1, 0)]
    ring = [(di, dj) for di, dj in around if di or dj]
    beside_pairs = [(0, -1), (0, 1)]
    corner_pairs = [(di, dj) for di, dj in ring if di and dj]

    def s_all(action, s, sending):
        @pl.when(air)
        def _():
            action(functools.partial(s_copy, s, sending), around)

        @pl.when(ocean)
        def _():
            action(functools.partial(s_copy, s, not sending), around)

    def start_all(make, pairs):
        for di, dj in pairs:
            when(has[di], lambda di=di, dj=dj: make(di, dj).start())

    def wait_arrivals(make, pairs):
        for di, dj in pairs:
            when(has[-di], lambda di=di, dj=dj: make(di, dj).wait_recv())

    def wait_departures(make, pairs):
        for di, dj in pairs:
            when(has[di], lambda di=di, dj=dj: make(di, dj).wait_send())

    loads[0].wait()
    xr[0, 2:18] = jnp.transpose(state_ref[0], (1, 0, 2))

    loads[1].wait()
    loads[4].wait()
    wet_values = mask_ref[...].astype(F32)
    wet[...] = wet_values
    kept = jnp.where(ocean, wet_values, 1.0)
    keep[...] = kept
    high, middle, rest = thirds(proj_ref[g])
    pp[...] = jnp.concatenate([high, high, middle, middle, rest, rest], 0).astype(BF)

    srow[...] = jnp.zeros((24, 8, LANES), F32)
    def blocks_swapped(tiles):
        tiles = list(tiles)
        block = iota(tiles[0].shape, 1) >> 4
        for s in (4, 2, 1):
            stays = (block & s) == 0
            for a in range(8):
                if not a & s:
                    x, y = tiles[a], tiles[a + s]
                    tiles[a] = jnp.where(stays, x, pltpu.roll(y, 16 * s, 1))
                    tiles[a + s] = jnp.where(stays, pltpu.roll(x, LANES - 16 * s, 1), y)
        return tiles

    def turned(x):
        return pltpu.roll(x, 4, 0)

    def double_low(x):
        return jnp.where(low, x, turned(x))

    def double_high(x):
        return jnp.where(low, turned(x), x)

    def fill(t, cells):
        x3[t, 0:80] = pltpu.roll(cells, 1, 1)
        x3[t, 80:160] = cells
        x3[t, 160:240] = pltpu.roll(cells, LANES - 1, 1)

    def surface_rows(first, rows):
        parts = jnp.dot(pp[...], jnp.concatenate(rows, 1), preferred_element_type=F32)
        fields = parts[0:8] + parts[8:16] + parts[16:24]
        for u in range(len(rows)):
            kept_row = jnp.broadcast_to(keep[first + u : first + u + 1], (8, LANES))
            srow[air_shift + first + u] = fields[:, 128 * u : 128 * u + 128] * kept_row

    def surface(s):
        for m in range(0, ROWS, SURFACE_ROWS):
            surface_rows(m, [xr[s, m + 2 + u] for u in range(SURFACE_ROWS)])
        zero = jnp.zeros((8, LANES), F32)
        tiles = blocks_swapped(
            jnp.concatenate(
                [jnp.where(low, srow[k], srow[8 + k]), jnp.where(low, srow[16 + k], zero)], 0
            ).astype(BF)
            for k in range(8)
        )
        sp[s, 0] = tiles[0]
        sp[s, 1] = tiles[7]
        tiles = [tile.astype(F32) for tile in tiles]
        for half in range(2):
            made = [[], [], []]
            for m in range(2):
                even, odd = tiles[4 * half + 2 * m], tiles[4 * half + 2 * m + 1]
                made[0].append(jnp.where(low, even[0:8], turned(odd[0:8])))
                made[1].append(jnp.where(low, turned(even[0:8]), odd[0:8]))
                made[2].append(jnp.where(low, even[8:16], turned(odd[8:16])))
            for band in range(3):
                sm[s, band, 16 * half : 16 * half + 16] = jnp.concatenate(made[band], 0).astype(BF)

    def edge_rows(s):
        def add(t, acc):
            return jnp.where((lane80 >> 2) == t, pltpu.roll(xr[s, t], 4 * t + 2, 1), acc)

        own = jnp.zeros((CH, LANES), BF)
        for t in range(2, 18):
            own = add(t, own)
        eg[s] = own

    def corner_rows(s):
        own = eg[s]
        packed = jnp.zeros((16, LANES), BF)
        for part in range(5):
            tile = pltpu.roll(own[16 * part : 16 * part + 16], 64 + 8 * part, 1)
            place_of = lane16 - 8 * part
            inside = ((place_of >= 0) & (place_of < 8)) | ((place_of >= 72) & (place_of < 80))
            packed = jnp.where(inside, tile, packed)
        cp[s] = packed

    surface(0)

    loads[2].wait()
    loads[3].wait()
    for k in range(4):
        code = (offsets_ref[0, 0, k] + HW) * 32 + (offsets_ref[0, 1, k] + HW)
        flip[16 * k : 16 * k + 16] = code.astype(F32)
        flip[64 + 16 * k : 64 + 16 * k + 16] = weights_ref[0, k]
    for r in range(ROWS):
        q[ocean_shift + r] = flip[pl.ds(r, 8, stride=ROWS), :]

    @pl.when(ocean)
    def _():

        def add(t, acc):
            return jnp.where((lane8 >> 2) == t, pltpu.roll(q[t], 4 * t + 2, 1), acc)

        own = jnp.zeros((8, LANES), F32)
        for t in range(2, 18):
            own = add(t, own)
        qe[...] = own

    neighbours = 1 + has[-1].astype(I32) + has[1].astype(I32)
    pl.semaphore_wait(barrier, 3 * neighbours + g * (3 * neighbours - 1))

    @pl.when(ocean)
    def _():
        start_all(q_copy, ring)

    s_all(start_all, 0, True)

    @pl.when(ocean)
    def _():
        start_all(functools.partial(x_copy, 0), [(-1, 0), (1, 0)])
        edge_rows(0)
        start_all(functools.partial(x_copy, 0), beside_pairs)
        corner_rows(0)
        start_all(functools.partial(x_copy, 0), corner_pairs)
        eg[1] = jnp.zeros((CH, LANES), BF)
        for t in range(2, 18):
            fill(t, xr[0, t])

    @pl.when(ocean)
    def _():
        for load in loads[8:11]:
            load.wait()

        def rows_of(values):
            return thirds(0.5 * values.reshape(1, -1))

        spare = jnp.zeros((1, HO), F32)
        bias = jnp.concatenate([*rows_of(ocn_bias_ref[...]), spare], 0)
        for a in range(3):
            taps = [0.5 * ocn_in_v[3 * a + b].astype(F32) for b in range(3)]
            last = bias if a == 1 else jnp.zeros((4, HO), F32)
            stacked = jnp.concatenate(
                [tap[0:CH] for tap in taps] + [tap[CH:] for tap in taps] + [last], 0
            )
            stacked = jnp.concatenate([stacked, jnp.zeros((256, 256 - HO), F32)], 1)
            w1[a] = stacked.T[0:HOP].astype(BF)
            for b in range(3):
                values = ocn_out_v[3 * a + b].astype(F32)
                w2[a, CH * b : CH * b + CH, :] = jnp.concatenate(
                    [values, jnp.zeros((CH, HOP - HO), F32)], 1
                ).astype(BF)

    @pl.when(air)
    def _():
        for load in loads[5:8]:
            load.wait()
        bias = thirds(0.5 * atm_bias_ref[...].reshape(1, -1))
        stacked = jnp.concatenate(
            [0.5 * atm_in_ref[...].astype(F32), *bias, jnp.zeros((41, 384), F32)], 0
        )
        wa[...] = stacked.T[:, 0:96].astype(BF)

    def spread(values, base):
        first = jnp.broadcast_to(values[base : base + 1], (8, LANES))
        second = jnp.broadcast_to(values[base + 1 : base + 2], (8, LANES))
        return jnp.where(low, first, second)

    def decode_band(band):
        tiles = blocks_swapped(q[8 * band + k] for k in range(8))
        for patch in range(8):
            for kp in range(2):
                code = spread(tiles[patch], 2 * kp).astype(I32)
                down = (lane8 >> 4) + (code >> 5)
                across = inner8 + (code & 31)
                beside = jnp.where((across >= 8) & (across < 24), 0, 1)
                gi[8 * band + patch, kp] = (
                    ((down & 7) * 16 + ((across + 8) & 15)) + ((down >> 3) * 2 + beside) * LANES
                )
                gw[8 * band + patch, kp] = spread(tiles[patch], 4 + 2 * kp)

    @pl.when(air)
    def _():
        decode_band(0)
        decode_band(1)

    @pl.when(ocean)
    def _():
        decode_band(1)
        wait_arrivals(q_copy, ring)
        decode_band(0)
        decode_band(2)
        pos = lane8 & 3
        beside = [jnp.where(pos < 2, qe_recv[n, 0], qe_recv[n, 1]) for n in range(3)]
        ends = jnp.where(
            lane8 < 64, pltpu.roll(beside[0], 64, 1), pltpu.roll(beside[2], 64, 1)
        )
        values = jnp.where((lane8 >= 8) & (lane8 < 72), beside[1], ends)
        for kp in range(2):
            code = spread(values, 2 * kp).astype(I32)
            down = (lane8 >> 2) + (code >> 5)
            across = jnp.where(pos < 2, pos - 2, pos + 126) + (code & 31) - HW
            outer = jnp.where((across >= 0) & (across < LANES), 0, 1)
            gi[24, kp] = ((down & 7) * 16 + (across & 15)) + ((down >> 3) * 2 + outer) * LANES
            gw[24, kp] = spread(values, 4 + 2 * kp)

    def take(values, index):
        return jnp.take_along_axis(values, index, axis=1, mode="promise_in_bounds")

    def combine(n, picked):
        total = picked[0] * gw[n, 0] + picked[1] * gw[n, 1]
        return total + turned(total)

    def gather(n, kp, value, steps):
        band, patch = n >> 3, n & 7
        index = gi[n, kp] & (LANES - 1)
        which = gi[n, kp] >> 7
        for d in steps:
            there = jnp.where(inner8 < 8, src[band + d, patch + 2], src[band + d, patch])
            value = jnp.where(which == 2 * d, take(src[band + d, patch + 1], index), value)
            value = jnp.where(which == 2 * d + 1, take(there, index), value)
        return value

    def put_band(s, row, pick):
        for quarter in range(2):
            tile = pick(slice(16 * quarter, 16 * quarter + 16))
            for m in range(2):
                values = tile[8 * m : 8 * m + 8]
                src[row, 4 * quarter + 2 * m + 1] = double_low(values)
                src[row, 4 * quarter + 2 * m + 2] = double_high(values)

    def sources(s):
        def band(k):
            return lambda rows: sb[s, k, rows].astype(F32)

        def joined(k):
            return lambda rows: jnp.where(
                lane16 < 32, sb[s, k, rows].astype(F32), sb[s, k + 1, rows].astype(F32)
            )

        @pl.when(air)
        def _():
            middle = [(0, dj) for dj in (-1, 1, 0)]
            wait_arrivals(functools.partial(s_copy, s, False), middle)
            sides = [[sp_recv[s, 1, side].astype(F32) for side in range(2)]]
            for row, k in ((1, 2), (2, 3)):
                put_band(s, row, band(k))
            for side in range(2):
                src[1, 9 * side] = double_low(sides[0][side][0:8])
                src[2, 9 * side] = double_high(sides[0][side][0:8])
            blank = jnp.zeros((8, LANES), F32)
            for n in range(16):
                for kp in range(2):
                    part[n, kp] = gather(n, kp, blank, (1, 2) if n < 8 else (0, 1))
            beyond = [(di, dj) for di, dj in around if di]
            wait_arrivals(functools.partial(s_copy, s, False), beyond)
            for row, k, n, double in ((0, 0, 0, double_high), (3, 5, 2, double_low)):
                put_band(s, row, band(k))
                for side in range(2):
                    src[row, 9 * side] = double(sp_recv[s, n, side].astype(F32)[0:8])
            for n in range(16):
                steps = (0,) if n < 8 else (2,)
                fp[n] = combine(n, [gather(n, kp, part[n, kp], steps) for kp in range(2)])

        @pl.when(ocean)
        def _():
            wait_arrivals(functools.partial(s_copy, s, True), around)
            sides = [[sp_recv[s, n, side].astype(F32) for side in range(2)] for n in range(3)]
            for row, pick in enumerate((band(0), joined(1), band(3), joined(4), band(6))):
                put_band(s, row, pick)
            first = lane8 < 32
            for side in range(2):
                north, center, south = (sides[n][side] for n in range(3))
                column = 9 * side
                src[0, column] = double_high(north[0:8])
                src[1, column] = jnp.where(first, double_low(north[8:16]), double_low(center[0:8]))
                src[2, column] = double_high(center[0:8])
                src[3, column] = jnp.where(first, double_low(center[8:16]), double_low(south[0:8]))
                src[4, column] = double_high(south[0:8])

    def regrid_patch(n, c):
        blank = jnp.zeros((8, LANES), F32)
        fp[n] = combine(n, [gather(n, kp, blank, range(3)) for kp in range(2)])

    def regrid_edges():
        picked = []
        left = (lane8 & 3) < 2
        for kp in range(2):
            index = gi[24, kp] & (LANES - 1)
            which = gi[24, kp] >> 7
            value = jnp.zeros((8, LANES), F32)
            for d in range(5):
                inner = take(jnp.where(inner8 < 8, src[d, 1], src[d, 8]), index)
                outer = jnp.where(left, take(src[d, 0], index), take(src[d, 9], index))
                value = jnp.where(which == 2 * d, inner, value)
                value = jnp.where(which == 2 * d + 1, outer, value)
            picked.append(value)
        fp[24] = combine(24, picked)

    def forcing_rows(bands):
        zero = jnp.zeros((8, LANES), F32)
        tiles = blocks_swapped(
            jnp.concatenate(
                [
                    jnp.where(low, fp[k], fp[8 + k]),
                    jnp.where(low, fp[16 + k], zero) if bands == 3 else zero,
                ],
                0,
            ).astype(BF)
            for k in range(8)
        )
        for k in range(8):
            tile = tiles[k].astype(F32)
            fr[k] = double_low(tile[0:8])
            fr[8 + k] = double_high(tile[0:8])
            if bands == 3 and k < 4:
                fr[16 + k] = double_low(tile[8:16])

    def finish_rows(s, first, rows):
        rows = [values.astype(BF) for values in rows]
        for u, values in enumerate(rows):
            if s + 1 < STEPS:
                xr[s + 1, first + u + 2] = values
            else:
                final[first + u] = values
        return rows

    def air_step(s):
        forcing_rows(2)
        ones = jnp.where(sub8 < 7, 1.0, 0.0)
        blank = jnp.zeros((8, LANES), F32)

        columns = []
        for r in range(ROWS):
            tail = jnp.concatenate([jnp.where(low, fr[r], ones), blank], 0).astype(BF)
            columns.append(jnp.concatenate([xr[s, r + 2], tail], 0))
        for first in range(0, ROWS, AIR_ROWS):
            block = jnp.concatenate(columns[first : first + AIR_ROWS], 1)
            hidden = gelu_of_twice(
                jnp.dot(wa[...], block, preferred_element_type=F32)
            ).astype(BF)
            update = jnp.dot(atm_out_ref[...], hidden, preferred_element_type=F32)
            finish_rows(
                s,
                first,
                [
                    xr[s, first + u + 2].astype(F32) + update[:, 128 * u : 128 * u + 128]
                    for u in range(AIR_ROWS)
                ],
            )

    def ocean_step(s):
        run(range(24), regrid_patch)
        regrid_edges()
        forcing_rows(3)
        pos = lane80 & 3
        pos8 = lane8 & 3
        pos16 = lane16 & 3

        def taps(halo, mine, where):
            return (
                pltpu.roll(jnp.where(where == 0, halo, mine), 1, 1),
                halo,
                pltpu.roll(jnp.where(where == 2, mine, halo), LANES - 1, 1),
            )

        def swapped(halo, where):
            return jnp.where(where == 1, pltpu.roll(halo, LANES - 1, 1), pltpu.roll(halo, 1, 1))

        own_forcing = jnp.zeros((8, LANES), F32)
        for t in range(TALL):
            own_forcing = jnp.where((lane8 >> 2) == t, pltpu.roll(fr[t], 4 * t + 2, 1), own_forcing)
        beside_forcing = fp[24]
        first, second, third = taps(beside_forcing, own_forcing, pos8)
        ones = jnp.where(sub8 < 7, 1.0, 0.0)
        x3e[240:256] = jnp.concatenate(
            [jnp.where(low, first, second), jnp.where(low, third, ones)], 0
        ).astype(BF)
        swapped_forcing = swapped(beside_forcing, pos8)
        for t in range(TALL):
            forcing = fr[t]
            halo = pltpu.roll(swapped_forcing, 126 - 4 * t, 1)
            left = jnp.where(lane8 == 0, halo, pltpu.roll(forcing, 1, 1))
            right = jnp.where(lane8 == LANES - 1, halo, pltpu.roll(forcing, LANES - 1, 1))
            x3[t, 240:256] = jnp.concatenate(
                [jnp.where(low, left, forcing), jnp.where(low, right, ones)], 0
            ).astype(BF)

        def rim(t):
            halo = pltpu.roll(hh[...], 126 - 4 * t, 1)
            x3[t, 0:80] = jnp.where(lane80 == 0, halo, x3[t, 0:80])
            x3[t, 160:240] = jnp.where(lane80 == LANES - 1, halo, x3[t, 160:240])

        def first_conv(p, c):
            h = 2 * p
            total = jnp.zeros((HOP, 256), F32)
            for a in range(3):
                columns = jnp.concatenate([x3[h + a], x3[h + a + 1]], 1)
                total = total + jnp.dot(w1[a], columns, preferred_element_type=F32)
            active = gelu_of_twice(total)
            if p == 0:
                active = jnp.where((iota((HOP, 256), 1) < 128) & (i == 0), 0.0, active)
            if p == 8:
                active = jnp.where((iota((HOP, 256), 1) >= 128) & (i == lats - 1), 0.0, active)
            active = active.astype(BF)
            hid[h] = active[:, 0:128]
            hid[h + 1] = active[:, 128:256]

        def edge_tile(halo, mine):
            state_taps = taps(halo, mine, pos)
            for b in range(3):
                x3e[CH * b : CH * b + CH] = state_taps[b]
            total = jnp.zeros((HOP, LANES), F32)
            for a in range(3):
                columns = x3e[...]
                if a:
                    columns = pltpu.roll(columns, LANES - 4 * a, 1)
                total = total + jnp.dot(w1[a], columns, preferred_element_type=F32)
            slot = iota((HOP, LANES), 1) >> 2
            outside = ((slot == 0) & (i == 0)) | ((slot == 17) & (i == lats - 1))
            he[...] = jnp.where(outside, 0.0, gelu_of_twice(total)).astype(BF)
            total = jnp.zeros((240, LANES), F32)
            for a in range(3):
                columns = he[...]
                if a:
                    columns = pltpu.roll(columns, LANES - 4 * a, 1)
                total = total + jnp.dot(w2[a], columns, preferred_element_type=F32)
            ze[...] = jnp.where(
                pos == 1,
                pltpu.roll(total[160:240], LANES - 1, 1),
                pltpu.roll(total[0:80], 1, 1),
            )

        def second_conv(p, c):
            r = 2 * p
            total = jnp.zeros((240, 256), F32)
            for a in range(3):
                columns = jnp.concatenate([hid[r + a], hid[r + a + 1]], 1)
                total = total + jnp.dot(w2[a], columns, preferred_element_type=F32)
            rows = []
            for u in range(2):
                part = total[:, 128 * u : 128 * u + 128]
                halo = pltpu.roll(ze[...], 126 - 4 * (r + u), 1)
                left = jnp.where(lane80 == 0, halo, pltpu.roll(part[0:80], 1, 1))
                right = jnp.where(
                    lane80 == LANES - 1, halo, pltpu.roll(part[160:240], LANES - 1, 1)
                )
                update = left + part[80:160] + right
                rows.append(xr[s, r + u + 2].astype(F32) + wet[r + u : r + u + 1] * update)
            rows = finish_rows(s, r, rows)
            if s + 1 < STEPS:
                for u in range(2):
                    t = r + u + 2
                    fill(t, rows[u])
                    eg[s + 1] = jnp.where(
                        (lane80 >> 2) == t, pltpu.roll(rows[u], 4 * t + 2, 1), eg[s + 1]
                    )

        wait_arrivals(functools.partial(x_copy, s), [(0, -1), (0, 1)])
        beside = jnp.where(pos < 2, eg_recv[s, 0], eg_recv[s, 1])
        hh[...] = swapped(beside, pos)
        for t in range(2, 18):
            rim(t)
        run(range(1, 8), first_conv)
        if s + 1 == STEPS:
            edge_tile(beside, eg[s])
            run(range(1, 7), second_conv)

        wait_arrivals(functools.partial(x_copy, s), [(di, dj) for di, dj in ring if di])
        own = eg[s]
        for t in (0, 1, 18, 19):
            own = jnp.where((lane80 >> 2) == t, pltpu.roll(xr[s, t], 4 * t + 2, 1), own)
        ends = [jnp.where(pos16 < 2, cp_recv[s, n, 0], cp_recv[s, n, 1]) for n in range(2)]
        corner = jnp.where(lane16 < 64, ends[0], ends[1])
        corner = jnp.concatenate(
            [pltpu.roll(corner, LANES - 8 * part, 1) if part else corner for part in range(5)], 0
        )
        beside = jnp.where((lane80 >= 8) & (lane80 < 72), beside, corner)
        hh[...] = swapped(beside, pos)
        for t in (0, 1, 18, 19):
            fill(t, xr[s, t])
            rim(t)
        run((0, 8), first_conv)
        edge_tile(beside, own)
        run((0, 7), second_conv)

        if s + 1 < STEPS:
            start_all(functools.partial(x_copy, s + 1), [(-1, 0), (1, 0)])
            run(range(1, 7), second_conv)
            start_all(functools.partial(x_copy, s + 1), beside_pairs)
            corner_rows(s + 1)
            start_all(functools.partial(x_copy, s + 1), corner_pairs)

    for s in range(STEPS):
        if s:
            surface(s)
            s_all(start_all, s, True)

        sources(s)

        @pl.when(ocean)
        def _(s=s):
            ocean_step(s)

        @pl.when(air)
        def _(s=s):
            air_step(s)

    out_ref[0] = jnp.transpose(final[...], (1, 0, 2))

    for s in range(STEPS):
        s_all(wait_departures, s, True)

    @pl.when(ocean)
    def _():
        for s in range(STEPS):
            wait_departures(functools.partial(x_copy, s), ring)
        wait_departures(q_copy, ring)


def solution(mesh):
    lats, lons = mesh.shape["lat"], mesh.shape["lon"]
    vmem = pl.BlockSpec(memory_space=pltpu.VMEM)
    anywhere = pl.BlockSpec(memory_space=pl.ANY)
    dma = pltpu.SemaphoreType.DMA

    def local(*args):
        args = list(args)
        args[5] = args[5].T
        args[8] = args[8].transpose(1, 2, 0)
        args[10] = args[10].transpose(1, 0, 2)
        return pl.pallas_call(
            functools.partial(kernel, lats, lons),
            out_shape=jax.ShapeDtypeStruct((1, CH, ROWS, LANES), BF),
            in_specs=[anywhere] * 11,
            out_specs=vmem,
            scratch_shapes=[
                pltpu.VMEM((1, CH, ROWS, LANES), BF),
                pltpu.VMEM((ROWS, LANES), I32),
                pltpu.VMEM((1, 2, 4, ROWS, LANES), I32),
                pltpu.VMEM((1, 4, ROWS, LANES), F32),
                pltpu.VMEM((2, 4, CH), F32),
                pltpu.VMEM((84, 384), BF),
                pltpu.VMEM((384,), F32),
                pltpu.VMEM((CH, 384), BF),
                pltpu.VMEM((9, 84, HO), BF),
                pltpu.VMEM((HO,), F32),
                pltpu.VMEM((9, CH, HO), BF),
                pltpu.VMEM((2 * LANES, LANES), F32),
                pltpu.VMEM((ROWS, CH, LANES), BF),
                pltpu.VMEM((STEPS, TALL, CH, LANES), BF),
                pltpu.VMEM((STEPS, CH, LANES), BF),
                pltpu.VMEM((STEPS, 2, CH, LANES), BF),
                pltpu.VMEM((STEPS, 16, LANES), BF),
                pltpu.VMEM((STEPS, 2, 2, 16, LANES), BF),
                pltpu.VMEM((24, 8, LANES), F32),
                pltpu.VMEM((STEPS, 3, 32, LANES), BF),
                pltpu.VMEM((STEPS, 7, 32, LANES), BF),
                pltpu.VMEM((STEPS, 2, 16, LANES), BF),
                pltpu.VMEM((STEPS, 3, 2, 16, LANES), BF),
                pltpu.VMEM((24, 8, LANES), F32),
                pltpu.VMEM((8, LANES), F32),
                pltpu.VMEM((3, 2, 8, LANES), F32),
                pltpu.VMEM((25, 2, 8, LANES), I32),
                pltpu.VMEM((25, 2, 8, LANES), F32),
                pltpu.VMEM((5, 10, 8, LANES), F32),
                pltpu.VMEM((16, 2, 8, LANES), F32),
                pltpu.VMEM((25, 8, LANES), F32),
                pltpu.VMEM((24, 8, LANES), F32),
                pltpu.VMEM((TALL, 256, LANES), BF),
                pltpu.VMEM((256, LANES), BF),
                pltpu.VMEM((3, HOP, 256), BF),
                pltpu.VMEM((3, 240, HOP), BF),
                pltpu.VMEM((384, 96), BF),
                pltpu.VMEM((18, HOP, LANES), BF),
                pltpu.VMEM((HOP, LANES), BF),
                pltpu.VMEM((CH, LANES), BF),
                pltpu.VMEM((CH, LANES), F32),
                pltpu.VMEM((ROWS, LANES), F32),
                pltpu.VMEM((ROWS, LANES), F32),
                pltpu.VMEM((24, CH), BF),
                dma((11,)),
                dma((STEPS, 3, 3)),
                dma((STEPS, 3, 3)),
                dma((STEPS, 3, 3)),
                dma((STEPS, 3, 3)),
                dma((3, 3)),
                dma((3, 3)),
            ],
            compiler_params=pltpu.CompilerParams(
                collective_id=0,
                has_side_effects=True,
                vmem_limit_bytes=60 * 1024 * 1024,
            ),
        )(*args)

    return jax.shard_map(
        local,
        mesh=mesh,
        in_specs=(
            P("grp", None, "lat", "lon"),
            P("lat", "lon"),
            P("grp", None, None, "lat", "lon"),
            P("grp", None, "lat", "lon"),
            P(),
            P(),
            P(),
            P(),
            P(),
            P(),
            P(),
        ),
        out_specs=P("grp", None, "lat", "lon"),
        check_vma=False,
    )
```
